128 devices in a mesh: dp: 16 (over z, y), tensor: 8 (over x, core).
Axes of the slice: x: 4, y: 4, z: 4, core: 2. Of those that a mesh axis runs over, the one named last changes fastest.
Arguments:
- acts: bfloat16 [8192, 4096], P('dp'), may hold values from -0.25 to 0.25
- up_cot: bfloat16 [8192, 7168], P('dp', 'tensor'), may hold values from -6 to 6
- up_weight: bfloat16 [4096, 7168], P(None, 'tensor'), may hold values from -0.0625 to 0.0625
- error_buf: bfloat16 [16, 4096, 7168], P('dp', None, 'tensor'), may hold values from -4 to 4
- q_init: float32 [64, 7168], P(None, 'tensor'), may hold values from -6 to 6
Outputs:
- input_grad: bfloat16 [8192, 4096], P(('dp', 'tensor'))
- new_error: bfloat16 [16, 4096, 7168], P('dp', None, 'tensor')
- p_factor: float32 [64, 4096], replicated
- q_factor: float32 [64, 7168], P(None, 'tensor')
The draws below stay inside these ranges and needn't reach their ends.
All inputs are finite; a program needn't handle non-finite values.
Results may differ from the reference program's by a relative error of at most 0.001.
Values sent between devices are 32-bit elements; how exact they have to be, the bound alone decides.
No kernel may reach another device: no remote copies, remote signals or barrier semaphores. Data moves between devices by JAX's collectives and lax.ppermute only.
A program may use at most 128 MiB of HBM per device.

```python
import jax
import jax.numpy as jnp
from jax import lax

D = 4096
RANK = 64
TOK_DEV = 512
FF = 7168
REPLICAS = 16
TOKENS = 8192
N_DP = 16


def shard_levels(key, extent, split, least, largest):
    def one(dim, blocks):
        heights = jax.random.uniform(jax.random.fold_in(jax.random.fold_in(key, 6), dim), (blocks,), jnp.float32, least / len(split), largest / len(split))
        return jnp.repeat(jnp.exp(heights), extent[dim] // blocks).reshape((-1,) + (1,) * (len(extent) - dim - 1))

    level = one(*split[0])
    for cut in split[1:]:
        level = level * one(*cut)
    return level


def gaussian(own_key, extent, spread, bound, cuts=(), kind=jnp.bfloat16):
    factor_of = shard_levels(own_key, extent, cuts, -0.22, 0.18) if cuts else 1.0
    entries = jax.random.normal(own_key, extent, jnp.float32) * spread * factor_of
    return jnp.minimum(jnp.maximum(entries, -bound), bound).astype(kind)


def setup_inputs(seed: int = 0) -> dict:
    keys = jax.random.split(jax.random.key(seed), 6)
    acts = gaussian(keys[0], (TOKENS, D), TOK_DEV ** -0.5, 0.25, ((0, 16),))
    up_cot = gaussian(keys[1], (TOKENS, FF), 1.0, 6.0, ((0, 16), (1, 8)))
    up_weight = gaussian(keys[2], (D, FF), FF ** -0.5, 0.0625, ((1, 8),))
    error_buf = gaussian(keys[3], (REPLICAS, D, FF), 0.5, 4.0, ((0, 16), (2, 8)))
    q_init = gaussian(keys[4], (RANK, FF), 1.0, 6.0, ((1, 8),), jnp.float32)
    return {"acts": acts, "up_cot": up_cot, "up_weight": up_weight, "error_buf": error_buf, "q_init": q_init}


def reference(acts, up_cot, up_weight, error_buf, q_init):
    hp = lax.Precision.HIGHEST
    input_grad = lax.dot_general(up_cot.astype(jnp.float32), up_weight.astype(jnp.float32), (((1,), (1,)), ((), ())), preferred_element_type=jnp.float32).astype(jnp.bfloat16)
    acts_r = acts.reshape(N_DP, TOK_DEV, D)
    cot_r = up_cot.reshape(N_DP, TOK_DEV, FF)

    def merge_one(items):
        xpart, cpart, epart = items
        grad = lax.dot_general(xpart.astype(jnp.float32), cpart.astype(jnp.float32), (((0,), (0,)), ((), ())), preferred_element_type=jnp.float32)
        return grad + epart.astype(jnp.float32)
    merged = lax.map(merge_one, (acts_r, cot_r, error_buf))
    left = jnp.einsum('kf,rdf->kd', q_init, merged, precision=hp)
    gram = jnp.dot(left, left.T, precision=hp)
    chol = jnp.linalg.cholesky(gram)
    basis = lax.linalg.triangular_solve(chol, left, left_side=True, lower=True)
    q_factor = jnp.einsum('kd,rdf->kf', basis, merged, precision=hp) / N_DP
    approx = jnp.einsum('kd,kf->df', basis, q_factor, precision=hp)
    new_error = (merged - approx[None]).astype(jnp.bfloat16)
    return (input_grad, new_error, basis, q_factor)
```

```python
import jax
import jax.numpy as jnp
from jax import lax
from jax.experimental import pallas as pl
from jax.experimental.pallas import tpu as pltpu
from jax.sharding import PartitionSpec as P

F32 = jnp.float32
BF16 = jnp.bfloat16
HIGHEST = lax.Precision.HIGHEST
RANK = 64
LANES = 128
VMEM = pl.BlockSpec(memory_space=pltpu.VMEM)
NT = (((1,), (1,)), ((), ()))
TN = (((0,), (0,)), ((), ()))


def params(mib):
    return pltpu.CompilerParams(vmem_limit_bytes=mib << 20)


def cost(flops, nbytes):
    return pl.CostEstimate(flops=flops, bytes_accessed=nbytes, transcendentals=0)


def split3(x):
    high = x.astype(BF16)
    rest = x - high.astype(F32)
    mid = rest.astype(BF16)
    low = (rest - mid.astype(F32)).astype(BF16)
    return jnp.concatenate([high, mid, low], axis=0)


def sum3(y):
    return (y[2 * RANK : 3 * RANK] + y[RANK : 2 * RANK]) + y[:RANK]


def dot(a, b, dims=(((1,), (0,)), ((), ()))):
    return lax.dot_general(a, b, dims, preferred_element_type=F32)


def left_kernel(half_ref, q_ref, cot_ref, acts_ref, error_ref, out_ref, q3_ref, p3_ref):
    @pl.when(pl.program_id(0) == 0)
    def _():
        q3_ref[...] = split3(q_ref[...])
        p3_ref[...] = split3(sum3(dot(q3_ref[...], cot_ref[...], NT)))

    term = dot(q3_ref[...], error_ref[...], NT) + dot(p3_ref[...], acts_ref[...])
    left = sum3(term)
    for j in range(left.shape[1] // LANES):
        for g in range(4):
            out_ref[4 * j + g] = left[16 * g : 16 * g + 16, LANES * j : LANES * (j + 1)]


def left_half(half, q, cot, acts, error, tile=512):
    tokens, d = acts.shape
    ff = cot.shape[1]
    steps = d // 2 // tile
    return pl.pallas_call(
        left_kernel,
        grid_spec=pltpu.PrefetchScalarGridSpec(
            num_scalar_prefetch=1,
            grid=(steps,),
            in_specs=[
                pl.BlockSpec((RANK, ff), lambda i, h: (0, 0)),
                pl.BlockSpec((tokens, ff), lambda i, h: (0, 0)),
                pl.BlockSpec((tokens, tile), lambda i, h: (0, h[0] * steps + i)),
                pl.BlockSpec((tile, ff), lambda i, h: (h[0] * steps + i, 0)),
            ],
            out_specs=pl.BlockSpec((tile // 32, 16, LANES), lambda i, h: (i, 0, 0)),
            scratch_shapes=[
                pltpu.VMEM((3 * RANK, ff), BF16),
                pltpu.VMEM((3 * RANK, tokens), BF16),
            ],
        ),
        out_shape=jax.ShapeDtypeStruct((d // 64, 16, LANES), F32),
        compiler_params=params(24),
        cost_estimate=cost(4 * 10**9, 6 << 20),
    )(half, q, cot, acts, error)


def spread_kernel(scale, in_ref, out_ref):
    n = in_ref.shape[0]
    total = in_ref[0]
    for i in range(1, n):
        total = total + in_ref[i]
    if scale != 1.0:
        total = total * scale
    for i in range(n):
        out_ref[i] = total


def spread(x, scale):
    return pl.pallas_call(
        lambda i, o: spread_kernel(scale, i, o),
        in_specs=[VMEM],
        out_specs=VMEM,
        out_shape=jax.ShapeDtypeStruct(x.shape, F32),
        compiler_params=params(8),
        cost_estimate=cost(10**6, 2 << 20),
    )(x)


def inverse_factor(gram):
    groups = RANK // 8
    a = [gram[8 * i : 8 * i + 8] for i in range(groups)]
    row = lax.broadcasted_iota(jnp.int32, (8, RANK), 0)
    col = lax.broadcasted_iota(jnp.int32, (8, RANK), 1)
    b = [jnp.where(row + 8 * i == col, 1.0, 0.0).astype(F32) for i in range(groups)]
    scale = []
    for k in range(groups):
        cols = [
            [jnp.broadcast_to(a[i][:, 8 * k + j : 8 * k + j + 1], (8, RANK)) if i >= k else None for i in range(groups)]
            for j in range(8)
        ]
        block_scale = jnp.zeros((8, RANK), F32)
        for j in range(8):
            pivot = jnp.broadcast_to(cols[j][k][j : j + 1], (8, RANK))
            inverse = 1.0 / pivot
            block_scale = jnp.where(row == j, lax.rsqrt(pivot), block_scale)
            row_a = jnp.broadcast_to(a[k][j : j + 1], (8, RANK))
            row_b = jnp.broadcast_to(b[k][j : j + 1], (8, RANK))
            entries = [jnp.broadcast_to(cols[m][k][j : j + 1], (8, RANK)) for m in range(j + 1, 8)]
            for i in range(k, groups):
                factor = cols[j][i] * inverse
                if i == k:
                    factor = jnp.where(row > j, factor, 0.0)
                a[i] = a[i] - factor * row_a
                b[i] = b[i] - factor * row_b
                for m in range(j + 1, 8):
                    cols[m][i] = cols[m][i] - factor * entries[m - j - 1]
        scale.append(block_scale)
    return jnp.concatenate([b[i] * scale[i] for i in range(groups)], axis=0)


def middle_kernel(half_ref, mine_ref, other_ref, error_ref, acts_ref, cot_ref, basis_ref, right_ref, left_ref):
    h = half_ref[0]
    width = left_ref.shape[2]
    for ref, place in ((mine_ref, h), (other_ref, 1 - h)):
        for j in range(width // LANES):
            for g in range(4):
                left_ref[place, 16 * g : 16 * g + 16, LANES * j : LANES * (j + 1)] = ref[4 * j + g]
    gram = jnp.zeros((RANK, RANK), F32)
    for p in range(2):
        part = left_ref[p]
        gram = gram + lax.dot_general(part, part, NT, precision=HIGHEST, preferred_element_type=F32)
    factor = inverse_factor(gram)
    term = None
    proj = None
    for p in range(2):
        part = lax.dot_general(factor, left_ref[p], (((1,), (0,)), ((), ())), precision=HIGHEST, preferred_element_type=F32)
        basis_ref[:, p * width : (p + 1) * width] = part
        part3 = split3(part)
        t = dot(part3, error_ref[p * width : (p + 1) * width])
        s = dot(part3, acts_ref[:, p * width : (p + 1) * width], NT)
        term = t if term is None else term + t
        proj = s if proj is None else proj + s
    right = sum3(term + dot(split3(sum3(proj)), cot_ref[...]))
    tiles = right.shape[1] // LANES
    for g in range(8):
        for j in range(tiles):
            v = g * tiles + j
            right_ref[v // 4, 8 * (v % 4) : 8 * (v % 4) + 8] = right[8 * g : 8 * g + 8, LANES * j : LANES * (j + 1)]
    for v in range(8 * tiles, 64):
        right_ref[v // 4, 8 * (v % 4) : 8 * (v % 4) + 8] = jnp.zeros((8, LANES), F32)


def middle(half, mine, other, error, acts, cot):
    d = error.shape[0]
    return pl.pallas_call(
        middle_kernel,
        in_specs=[pl.BlockSpec(memory_space=pltpu.SMEM)] + [VMEM] * 5,
        out_specs=[VMEM, VMEM],
        out_shape=[
            jax.ShapeDtypeStruct((RANK, d), F32),
            jax.ShapeDtypeStruct((16, 32, LANES), F32),
        ],
        scratch_shapes=[pltpu.VMEM((2, RANK, d // 2), F32)],
        compiler_params=params(32),
        cost_estimate=cost(4 * 10**9, 13 << 20),
    )(half, mine, other, error, acts, cot)


def merged_kernel(acts_ref, cot_ref, error_ref, out_ref):
    grad = lax.dot_general(acts_ref[...], cot_ref[...], TN, preferred_element_type=F32)
    out_ref[...] = grad + error_ref[...].astype(F32)


def merge(acts, cot, error, tile=512):
    tokens, d = acts.shape
    ff = cot.shape[1]
    return pl.pallas_call(
        merged_kernel,
        grid=(d // tile,),
        in_specs=[
            pl.BlockSpec((tokens, tile), lambda i: (0, i)),
            pl.BlockSpec((tokens, ff), lambda i: (0, 0)),
            pl.BlockSpec((tile, ff), lambda i: (i, 0)),
        ],
        out_specs=pl.BlockSpec((tile, ff), lambda i: (i, 0)),
        out_shape=jax.ShapeDtypeStruct((d, ff), F32),
        compiler_params=params(24),
        cost_estimate=cost(4 * 10**9, 27 << 20),
    )(acts, cot, error)


def prep_kernel(basis_ref, out_ref):
    x = basis_ref[...]
    high = x.astype(BF16)
    low = (x - high.astype(F32)).astype(BF16)
    both = jnp.concatenate([high, low], axis=0).T
    out_ref[:, : 2 * RANK] = both
    out_ref[:, 2 * RANK :] = both


def prep(basis, tile=1024):
    d = basis.shape[1]
    return pl.pallas_call(
        prep_kernel,
        grid=(d // tile,),
        in_specs=[pl.BlockSpec((RANK, tile), lambda i: (0, i))],
        out_specs=pl.BlockSpec((tile, 4 * RANK), lambda i: (i, 0)),
        out_shape=jax.ShapeDtypeStruct((d, 4 * RANK), BF16),
        compiler_params=params(16),
        cost_estimate=cost(10**7, 4 << 20),
    )(basis)


def final_kernel(chunks_ref, basis_ref, merged_ref, error_ref, q_ref, q4_ref):
    @pl.when(pl.program_id(0) == 0)
    def _():
        tiles = q_ref.shape[1] // LANES
        for g in range(8):
            for j in range(tiles):
                v = g * tiles + j
                q_ref[8 * g : 8 * g + 8, LANES * j : LANES * (j + 1)] = chunks_ref[v // 4, 8 * (v % 4) : 8 * (v % 4) + 8]
        q = q_ref[...]
        high = q.astype(BF16)
        low = (q - high.astype(F32)).astype(BF16)
        q4_ref[...] = jnp.concatenate([high, high, low, low], axis=0)

    error_ref[...] = (merged_ref[...] - dot(basis_ref[...], q4_ref[...])).astype(BF16)


def final(chunks, basis4, merged, tile=512):
    d, ff = merged.shape
    return pl.pallas_call(
        final_kernel,
        grid=(d // tile,),
        in_specs=[
            pl.BlockSpec(chunks.shape, lambda i: (0, 0, 0)),
            pl.BlockSpec((tile, 4 * RANK), lambda i: (i, 0)),
            pl.BlockSpec((tile, ff), lambda i: (i, 0)),
        ],
        out_specs=[
            pl.BlockSpec((tile, ff), lambda i: (i, 0)),
            pl.BlockSpec((RANK, ff), lambda i: (0, 0)),
        ],
        out_shape=[
            jax.ShapeDtypeStruct((d, ff), BF16),
            jax.ShapeDtypeStruct((RANK, ff), F32),
        ],
        scratch_shapes=[pltpu.VMEM((4 * RANK, ff), BF16)],
        compiler_params=params(24),
        cost_estimate=cost(2 * 10**9, 24 << 20),
    )(chunks, basis4, merged)


def body(acts, up_cot, up_weight, error_buf, q_init):
    n_dp = lax.axis_size("dp")
    n_tensor = lax.axis_size("tensor")
    both = ("dp", "tensor")
    groups = [[2 * i + c for i in range(n_dp * n_tensor // 2)] for c in range(2)]
    pairs = [(i, i ^ 1) for i in range(n_tensor)]
    error = error_buf[0]
    core = lax.rem(lax.axis_index("tensor"), 2).astype(jnp.int32).reshape(1)

    send = left_half(1 - core, q_init, up_cot, acts, error)
    received = lax.ppermute(send, "tensor", pairs)
    keep = left_half(core, q_init, up_cot, acts, error)
    chunks = lax.all_to_all(keep + received, both, 0, 0, axis_index_groups=groups)

    partial = lax.dot_general(up_cot, up_weight, NT, preferred_element_type=F32)
    input_grad = lax.psum_scatter(partial, "tensor", scatter_dimension=0, tiled=True)
    merged = merge(acts, up_cot, error)

    mine = lax.all_to_all(spread(chunks, 1.0), both, 0, 0, axis_index_groups=groups)
    other = lax.ppermute(mine, "tensor", pairs)
    basis, right = middle(core, mine, other, error, acts, up_cot)

    right = lax.all_to_all(right, "dp", 0, 0)
    basis4 = prep(basis)
    right = lax.all_to_all(spread(right, 1.0 / n_dp), "dp", 0, 0)
    new_error, q_factor = final(right, basis4, merged)
    return (input_grad.astype(BF16), new_error[None], basis, q_factor)


def solution(mesh):
    return jax.shard_map(
        body,
        mesh=mesh,
        in_specs=(
            P("dp", None),
            P("dp", "tensor"),
            P(None, "tensor"),
            P("dp", None, "tensor"),
            P(None, "tensor"),
        ),
        out_specs=(P(("dp", "tensor"), None), P("dp", None, "tensor"), P(), P(None, "tensor")),
        check_vma=False,
    )
```

```python
import jax
import jax.numpy as jnp
from jax import lax
from jax.experimental import pallas as pl
from jax.experimental.pallas import tpu as pltpu
from jax.sharding import PartitionSpec as P

F32 = jnp.float32
BF16 = jnp.bfloat16
HIGHEST = lax.Precision.HIGHEST
RANK = 64
LANES = 128
VMEM = pl.BlockSpec(memory_space=pltpu.VMEM)
HBM = pl.BlockSpec(memory_space=pltpu.HBM)
NN = (((1,), (0,)), ((), ()))
NT = (((1,), (1,)), ((), ()))
TN = (((0,), (0,)), ((), ()))


def shape(dims, dtype=F32):
    return jax.ShapeDtypeStruct(dims, dtype)


def call(kernel, args, specs, outs, out_specs, scratch, n_sems, limit=56 << 20):
    return pl.pallas_call(
        kernel,
        in_specs=specs,
        out_specs=out_specs,
        out_shape=outs,
        scratch_shapes=[pltpu.VMEM(dims, dtype) for dims, dtype in scratch] + [pltpu.SemaphoreType.DMA((n_sems,))],
        compiler_params=pltpu.CompilerParams(vmem_limit_bytes=limit),
        cost_estimate=pl.CostEstimate(flops=10**6, bytes_accessed=10**5, transcendentals=0),
    )(*args)


class Copies:
    def __init__(self, sems):
        self.sems = sems
        self.all = []

    def start(self, src, dst):
        copy = pltpu.make_async_copy(src, dst, self.sems.at[len(self.all)])
        copy.start()
        self.all.append(copy)
        return copy


def split3(x):
    high = x.astype(BF16)
    rest = x - high.astype(F32)
    mid = rest.astype(BF16)
    low = (rest - mid.astype(F32)).astype(BF16)
    return jnp.concatenate([high, mid, low], axis=0)


def sum3(y):
    return (y[2 * RANK : 3 * RANK] + y[RANK : 2 * RANK]) + y[:RANK]


def dot(a, b, dims=NN):
    return lax.dot_general(a, b, dims, preferred_element_type=F32)


def dot_highest(a, b):
    return lax.dot_general(a, b, NN, precision=HIGHEST, preferred_element_type=F32)


def my_core():
    return lax.rem(lax.axis_index("tensor"), 2)


def part_of(place, width, i, parts):
    step = width // parts
    return pl.ds(pl.multiple_of(place * width + i * step, step), step)


PARTS = 4


def left_part(q3t, p3, error, acts):
    y = dot(error, q3t)
    by_error = (y[:, 2 * RANK :] + y[:, RANK : 2 * RANK]) + y[:, :RANK]
    return by_error.T + sum3(dot(p3, acts))


def store_left(out_ref, i, left):
    tiles = left.shape[1] // LANES
    for j in range(tiles):
        for g in range(4):
            out_ref[4 * (i * tiles + j) + g] = left[16 * g : 16 * g + 16, LANES * j : LANES * (j + 1)]


def half_shapes(tokens, d, ff, parts):
    step = d // 2 // parts
    return [(parts, step, ff), (parts, tokens, step)]


def fetch_half(copies, place, error_hbm, acts_hbm, error_ref, acts_ref):
    width = error_hbm.shape[0] // 2
    parts = error_ref.shape[0]
    started = []
    for i in range(parts):
        at = part_of(place, width, i, parts)
        started.append(
            (copies.start(error_hbm.at[at, :], error_ref.at[i]), copies.start(acts_hbm.at[:, at], acts_ref.at[i]))
        )
    return started


def left_send_kernel(
    q_hbm,
    cot_hbm,
    acts_hbm,
    error_hbm,
    out_ref,
    q3t_ref,
    p3_ref,
    error_keep_ref,
    acts_keep_ref,
    q_ref,
    cot_ref,
    error_ref,
    acts_ref,
    sems,
):
    core = my_core()
    copies = Copies(sems)
    q_copy = copies.start(q_hbm, q_ref)
    cot_copy = copies.start(cot_hbm, cot_ref)
    now = fetch_half(copies, 1 - core, error_hbm, acts_hbm, error_ref, acts_ref)
    later = fetch_half(copies, core, error_hbm, acts_hbm, error_keep_ref, acts_keep_ref)
    q_copy.wait()
    q3 = split3(q_ref[...])
    q3t = q3.T
    q3t_ref[...] = q3t
    cot_copy.wait()
    p3 = split3(sum3(dot(q3, cot_ref[...], NT)))
    p3_ref[...] = p3
    for i, pair in enumerate(now):
        for copy in pair:
            copy.wait()
        store_left(out_ref, i, left_part(q3t, p3, error_ref[i], acts_ref[i]))
    for pair in later:
        for copy in pair:
            copy.wait()


def left_send(q, cot, acts, error):
    tokens, d = acts.shape
    ff = cot.shape[1]
    halves = half_shapes(tokens, d, ff, PARTS)
    return call(
        left_send_kernel,
        (q, cot, acts, error),
        [HBM] * 4,
        [shape((d // 64, 16, LANES)), shape((ff, 3 * RANK), BF16), shape((3 * RANK, tokens), BF16)]
        + [shape(s, BF16) for s in halves],
        [VMEM] * 5,
        [((RANK, ff), F32), ((tokens, ff), BF16)] + [(s, BF16) for s in halves],
        2 + 4 * PARTS,
        limit=44 << 20,
    )


def left_keep_kernel(q3t_ref, p3_ref, error_ref, acts_ref, out_ref):
    for i in range(error_ref.shape[0]):
        store_left(out_ref, i, left_part(q3t_ref[...], p3_ref[...], error_ref[i], acts_ref[i]))


def left_keep(held, dims):
    return pl.pallas_call(
        left_keep_kernel,
        in_specs=[VMEM] * 4,
        out_specs=VMEM,
        out_shape=shape(dims),
        compiler_params=pltpu.CompilerParams(vmem_limit_bytes=10 << 20),
        cost_estimate=pl.CostEstimate(flops=10**6, bytes_accessed=10**5, transcendentals=0),
    )(*held)


def spread_kernel(scale, in_ref, out_ref):
    n = in_ref.shape[0]
    total = in_ref[0]
    for i in range(1, n):
        total = total + in_ref[i]
    if scale != 1.0:
        total = total * scale
    for i in range(n):
        out_ref[i] = total


def spread(x, scale):
    return pl.pallas_call(
        lambda i, o: spread_kernel(scale, i, o),
        in_specs=[VMEM],
        out_specs=VMEM,
        out_shape=shape(x.shape),
        compiler_params=pltpu.CompilerParams(vmem_limit_bytes=8 << 20),
        cost_estimate=pl.CostEstimate(flops=10**6, bytes_accessed=10**5, transcendentals=0),
    )(x)


def inverse_factor(gram):
    groups = RANK // 8
    a = [gram[8 * i : 8 * i + 8] for i in range(groups)]
    row = lax.broadcasted_iota(jnp.int32, (8, RANK), 0)
    col = lax.broadcasted_iota(jnp.int32, (8, RANK), 1)
    b = [jnp.where(row + 8 * i == col, 1.0, 0.0).astype(F32) for i in range(groups)]
    scale = []
    for k in range(groups):
        cols = [
            [jnp.broadcast_to(a[i][:, 8 * k + j : 8 * k + j + 1], (8, RANK)) if i >= k else None for i in range(groups)]
            for j in range(8)
        ]
        block_scale = jnp.zeros((8, RANK), F32)
        for j in range(8):
            pivot = jnp.broadcast_to(cols[j][k][j : j + 1], (8, RANK))
            inverse = 1.0 / pivot
            block_scale = jnp.where(row == j, lax.rsqrt(pivot), block_scale)
            row_a = jnp.broadcast_to(a[k][j : j + 1], (8, RANK))
            row_b = jnp.broadcast_to(b[k][j : j + 1], (8, RANK))
            entries = [jnp.broadcast_to(cols[m][k][j : j + 1], (8, RANK)) for m in range(j + 1, 8)]
            for i in range(k, groups):
                factor = cols[j][i] * inverse
                if i == k:
                    factor = jnp.where(row > j, factor, 0.0)
                a[i] = a[i] - factor * row_a
                b[i] = b[i] - factor * row_b
                for m in range(j + 1, 8):
                    cols[m][i] = cols[m][i] - factor * entries[m - j - 1]
        scale.append(block_scale)
    return jnp.concatenate([b[i] * scale[i] for i in range(groups)], axis=0)


def half_of(chunks_ref):
    n = chunks_ref.shape[0] // 4
    return jnp.concatenate(
        [jnp.concatenate([chunks_ref[4 * j + g] for j in range(n)], axis=1) for g in range(4)], axis=0
    )


def half_terms(left, error_ref, acts_ref, ready=None):
    parts, step = error_ref.shape[:2]
    left3 = split3(left)
    gram = [sum3(dot(left3, left3[RANK * i : RANK * (i + 1)], NT)) for i in range(3)]
    with_error = with_acts = None
    for i in range(parts):
        part = left3[:, i * step : (i + 1) * step]
        if ready is not None:
            for copy in ready[i]:
                copy.wait()
        e = dot(part, error_ref[i])
        a = dot(part, acts_ref[i], NT)
        with_error = e if i == 0 else with_error + e
        with_acts = a if i == 0 else with_acts + a
    return (gram[2] + gram[1]) + gram[0], sum3(with_error), sum3(with_acts)


def first_kernel(
    mine_hbm,
    cot_hbm,
    acts_hbm,
    error_hbm,
    gram_ref,
    with_error_ref,
    with_acts_ref,
    cot_ref,
    error_other_ref,
    acts_other_ref,
    mine_ref,
    error_ref,
    acts_ref,
    sems,
):
    core = my_core()
    copies = Copies(sems)
    mine_copy = copies.start(mine_hbm, mine_ref)
    now = fetch_half(copies, core, error_hbm, acts_hbm, error_ref, acts_ref)
    later = fetch_half(copies, 1 - core, error_hbm, acts_hbm, error_other_ref, acts_other_ref)
    cot_copy = copies.start(cot_hbm, cot_ref)
    mine_copy.wait()
    gram, with_error, with_acts = half_terms(half_of(mine_ref), error_ref, acts_ref, now)
    gram_ref[...] = gram
    with_error_ref[...] = with_error
    with_acts_ref[...] = with_acts
    for pair in later:
        for copy in pair:
            copy.wait()
    cot_copy.wait()


def first(mine, cot, acts, error, parts=1):
    tokens, d = acts.shape
    ff = cot.shape[1]
    halves = half_shapes(tokens, d, ff, parts)
    return call(
        first_kernel,
        (mine, cot, acts, error),
        [HBM] * 4,
        [shape((RANK, RANK)), shape((RANK, ff)), shape((RANK, tokens)), shape((tokens, ff), BF16)]
        + [shape(s, BF16) for s in halves],
        [VMEM] * 6,
        [(mine.shape, F32)] + [(s, BF16) for s in halves],
        2 + 4 * parts,
        limit=44 << 20,
    )


def second_kernel(
    other_ref, gram_ref, with_error_ref, with_acts_ref, cot_ref, error_ref, acts_ref, factor_ref, right_ref
):
    gram, with_error, with_acts = half_terms(half_of(other_ref), error_ref, acts_ref)
    factor = inverse_factor(gram + gram_ref[...])
    factor_ref[...] = factor
    with_acts = with_acts + with_acts_ref[...]
    merged_term = (with_error + with_error_ref[...]) + sum3(dot(split3(with_acts), cot_ref[...]))
    right = dot_highest(factor, merged_term)
    tiles = right.shape[1] // LANES
    for g in range(8):
        for j in range(tiles):
            v = g * tiles + j
            right_ref[v // 4, 8 * (v % 4) : 8 * (v % 4) + 8] = right[8 * g : 8 * g + 8, LANES * j : LANES * (j + 1)]
    for v in range(8 * tiles, 64):
        right_ref[v // 4, 8 * (v % 4) : 8 * (v % 4) + 8] = jnp.zeros((8, LANES), F32)


def second(other, terms):
    return pl.pallas_call(
        second_kernel,
        in_specs=[VMEM] * 7,
        out_specs=[VMEM, VMEM],
        out_shape=[shape((RANK, RANK)), shape((16, 32, LANES))],
        compiler_params=pltpu.CompilerParams(vmem_limit_bytes=12 << 20),
        cost_estimate=pl.CostEstimate(flops=10**6, bytes_accessed=10**5, transcendentals=0),
    )(other, *terms)


def merged_kernel(acts_hbm, cot_hbm, error_hbm, out_hbm, cot_ref, acts_ref, error_ref, out_ref, sems):
    parts, step = error_ref.shape[:2]
    copies = Copies(sems)
    cot_copy = copies.start(cot_hbm, cot_ref)
    waits = []
    for i in range(parts):
        at = slice(i * step, (i + 1) * step)
        waits.append((copies.start(acts_hbm.at[:, at], acts_ref.at[i]), copies.start(error_hbm.at[at, :], error_ref.at[i])))
    cot_copy.wait()
    stores = []
    for i in range(parts):
        waits[i][0].wait()
        waits[i][1].wait()
        out_ref[i] = dot(acts_ref[i], cot_ref[...], TN) + error_ref[i].astype(F32)
        stores.append(copies.start(out_ref.at[i], out_hbm.at[i * step : (i + 1) * step, :]))
    for store in stores:
        store.wait()


def merge(acts, cot, error, parts=4):
    tokens, d = acts.shape
    ff = cot.shape[1]
    step = d // parts
    return call(
        merged_kernel,
        (acts, cot, error),
        [HBM] * 3,
        shape((d, ff)),
        HBM,
        [((tokens, ff), BF16), ((parts, tokens, step), BF16), ((parts, step, ff), BF16), ((parts, step, ff), F32)],
        1 + 3 * parts,
    )


def prep_kernel(factor_ref, mine_ref, other_ref, basis_ref, out_ref):
    core = my_core()
    for ref, place in ((mine_ref, core), (other_ref, 1 - core)):
        width = ref.shape[0] // 4 * LANES
        at = pl.ds(pl.multiple_of(place * width, width), width)
        x = dot_highest(factor_ref[...], half_of(ref))
        basis_ref[:, at] = x
        high = x.astype(BF16)
        low = (x - high.astype(F32)).astype(BF16)
        both = jnp.concatenate([high, low], axis=0).T
        out_ref[at, : 2 * RANK] = both
        out_ref[at, 2 * RANK :] = both


def prep(factor, mine, other):
    d = 2 * (mine.shape[0] // 4 * LANES)
    return pl.pallas_call(
        prep_kernel,
        in_specs=[VMEM] * 3,
        out_specs=[VMEM, VMEM],
        out_shape=[shape((RANK, d)), shape((d, 4 * RANK), BF16)],
        compiler_params=pltpu.CompilerParams(vmem_limit_bytes=12 << 20),
        cost_estimate=pl.CostEstimate(flops=10**6, bytes_accessed=10**5, transcendentals=0),
    )(factor, mine, other)


def final_kernel(chunks_hbm, basis_hbm, merged_hbm, error_hbm, q_ref, chunks_ref, q4_ref, basis_ref, merged_ref, out_ref, sems):
    parts, step = merged_ref.shape[:2]
    copies = Copies(sems)
    chunks_copy = copies.start(chunks_hbm, chunks_ref)
    waits = []
    for i in range(parts):
        at = slice(i * step, (i + 1) * step)
        waits.append(
            (copies.start(basis_hbm.at[at, :], basis_ref.at[i]), copies.start(merged_hbm.at[at, :], merged_ref.at[i]))
        )
    chunks_copy.wait()
    tiles = q_ref.shape[1] // LANES
    for g in range(8):
        for j in range(tiles):
            v = g * tiles + j
            q_ref[8 * g : 8 * g + 8, LANES * j : LANES * (j + 1)] = chunks_ref[v // 4, 8 * (v % 4) : 8 * (v % 4) + 8]
    q = q_ref[...]
    high = q.astype(BF16)
    low = (q - high.astype(F32)).astype(BF16)
    q4_ref[...] = jnp.concatenate([high, high, low, low], axis=0)
    stores = []
    for i in range(parts):
        waits[i][0].wait()
        waits[i][1].wait()
        out_ref[i] = (merged_ref[i] - dot(basis_ref[i], q4_ref[...])).astype(BF16)
        stores.append(copies.start(out_ref.at[i], error_hbm.at[i * step : (i + 1) * step, :]))
    for store in stores:
        store.wait()


def final(chunks, basis4, merged, parts=4):
    d, ff = merged.shape
    step = d // parts
    return call(
        final_kernel,
        (chunks, basis4, merged),
        [HBM] * 3,
        [shape((d, ff), BF16), shape((RANK, ff))],
        [HBM, VMEM],
        [
            (chunks.shape, F32),
            ((4 * RANK, ff), BF16),
            ((parts, step, 4 * RANK), BF16),
            ((parts, step, ff), F32),
            ((parts, step, ff), BF16),
        ],
        1 + 3 * parts,
    )


def partial_kernel(
    cot_hbm,
    weight_hbm,
    far_send_hbm,
    near_send_hbm,
    far_keep_hbm,
    near_keep_hbm,
    cot_ref,
    weight_ref,
    out_ref,
    sems,
):
    parts, step = weight_ref.shape[:2]
    core = my_core()
    x = lax.div(lax.axis_index("tensor"), 2)
    n = cot_ref.shape[0] // 8
    copies = Copies(sems)
    waits = []
    for side, h in enumerate((1 - core, core)):
        for k, hop in enumerate((2, 1, 3, 0)):
            at = pl.multiple_of((lax.rem(x + hop, 4) * 2 + h) * n, n)
            to = (side * 4 + k) * n
            waits.append(copies.start(cot_hbm.at[pl.ds(at, n), :], cot_ref.at[to : to + n, :]))
    weight_copies = [
        copies.start(weight_hbm.at[i * step : (i + 1) * step, :], weight_ref.at[i]) for i in range(parts)
    ]
    for copy in waits:
        copy.wait()
    stores = []
    targets = ((far_send_hbm, 0, n), (near_send_hbm, n, 4 * n), (far_keep_hbm, 4 * n, 5 * n), (near_keep_hbm, 5 * n, 8 * n))
    for i in range(parts):
        weight_copies[i].wait()
        out_ref[i] = dot(cot_ref[...], weight_ref[i], NT)
        for hbm, lo, hi in targets:
            stores.append(copies.start(out_ref.at[i, lo:hi, :], hbm.at[:, i * step : (i + 1) * step]))
    for store in stores:
        store.wait()


def partials(cot, weight, parts=4):
    tokens, ff = cot.shape
    d = weight.shape[0]
    n = tokens // 8
    step = d // parts
    return call(
        partial_kernel,
        (cot, weight),
        [HBM, HBM],
        [shape((r, d)) for r in (n, 3 * n, n, 3 * n)],
        [HBM] * 4,
        [((tokens, ff), BF16), ((parts, step, ff), BF16), ((parts, tokens, step), F32)],
        8 + 5 * parts,
    )


def ring_kernel(takes, ins, outs, bufs, sems):
    copies = Copies(sems)
    loads = []
    slot = 0
    for take in takes:
        started = []
        for which, rows, cols in take:
            started.append(copies.start(ins[which].at[rows, cols], bufs.at[slot]))
            slot += 1
        loads.append(started)
    stores = []
    slot = 0
    for started, out in zip(loads, outs):
        for copy in started:
            copy.wait()
        total = bufs[slot]
        for k in range(1, len(started)):
            total = total + bufs[slot + k]
        bufs[slot] = total
        stores.append(copies.start(bufs.at[slot], out))
        slot += len(started)
    for store in stores:
        store.wait()


def ring_sums(ins, takes, n, w):
    slots = sum(len(take) for take in takes)
    count = len(ins)

    def kernel(*refs):
        ring_kernel(takes, refs[:count], refs[count : count + len(takes)], *refs[count + len(takes) :])

    return call(
        kernel,
        ins,
        [HBM] * count,
        [shape((n, w))] * len(takes),
        [HBM] * len(takes),
        [((slots, n, w), F32)],
        slots + len(takes),
    )


def close_kernel(keep_hbm, got_hbm, low_right, high_right, low_left, high_left, out_hbm, own_ref, in_ref, out_ref, sems):
    copies = Copies(sems)
    n, d = out_ref.shape
    w = d // 2
    own = slice(2 * n, 3 * n)
    loads = [copies.start(src.at[own, :], own_ref.at[i]) for i, src in enumerate((keep_hbm, got_hbm))]
    loads += [copies.start(src, in_ref.at[i]) for i, src in enumerate((low_right, low_left, high_right, high_left))]
    for copy in loads:
        copy.wait()
    for k, cols in enumerate((slice(0, w), slice(w, d))):
        own_sum = own_ref[0, :, cols] + own_ref[1, :, cols]
        out_ref[:, cols] = (own_sum + (in_ref[2 * k] + in_ref[2 * k + 1])).astype(BF16)
    copies.start(out_ref, out_hbm).wait()


def close(keep, got, low_right, high_right, low_left, high_left):
    n, w = low_right.shape
    return call(
        close_kernel,
        (keep, got, low_right, high_right, low_left, high_left),
        [HBM] * 6,
        shape((n, 2 * w), BF16),
        HBM,
        [((2, n, 2 * w), F32), ((4, n, w), F32), ((n, 2 * w), BF16)],
        7,
    )


def body(acts, up_cot, up_weight, error_buf, q_init):
    n_dp = lax.axis_size("dp")
    n_tensor = lax.axis_size("tensor")
    both = ("dp", "tensor")
    groups = [[2 * i + c for i in range(n_dp * n_tensor // 2)] for c in range(2)]
    pairs = [(i, i ^ 1) for i in range(n_tensor)]
    right_ring = [(i, (i + 2) % n_tensor) for i in range(n_tensor)]
    left_ring = [(i, (i - 2) % n_tensor) for i in range(n_tensor)]
    error = error_buf[0]

    send, *held = left_send(q_init, up_cot, acts, error)
    received = lax.ppermute(send, "tensor", pairs)
    total = left_keep(held, send.shape) + received
    chunks = lax.all_to_all(total, both, 0, 0, axis_index_groups=groups)

    up_weight, _ = lax.optimization_barrier((up_weight, total))
    far_send, near_send, far_keep, near_keep = partials(up_cot, up_weight)
    acts_late, _ = lax.optimization_barrier((acts, far_keep))
    merged = merge(acts_late, up_cot, error)
    chunks, merged, far_send, near_send = lax.optimization_barrier((chunks, merged, far_send, near_send))

    spread_left = spread(chunks, 1.0)
    mine = lax.all_to_all(spread_left, both, 0, 0, axis_index_groups=groups)
    far_send, near_send, _ = lax.optimization_barrier((far_send, near_send, spread_left))
    far_got = lax.ppermute(far_send, "tensor", pairs)
    near_got = lax.ppermute(near_send, "tensor", pairs)
    n, w = far_keep.shape[0], far_keep.shape[1] // 2
    low, high = slice(0, w), slice(w, 2 * w)
    plus, minus = slice(0, n), slice(n, 2 * n)
    far_low, far_high = ring_sums(
        (far_keep, far_got), (((0, plus, low), (1, plus, low)), ((0, plus, high), (1, plus, high))), n, w
    )
    low_relay = lax.ppermute(far_low, "tensor", right_ring)
    high_relay = lax.ppermute(far_high, "tensor", left_ring)
    plus_high, minus_low = ring_sums(
        (near_keep, near_got), (((0, plus, high), (1, plus, high)), ((0, minus, low), (1, minus, low))), n, w
    )
    high_right = lax.ppermute(plus_high, "tensor", right_ring)
    low_left = lax.ppermute(minus_low, "tensor", left_ring)
    mine, _, _ = lax.optimization_barrier((mine, far_low, plus_high))

    other = lax.ppermute(mine, "tensor", pairs)
    factor, right = second(other, first(mine, up_cot, acts, error))

    right_parts = lax.all_to_all(right, "dp", 0, 0)
    basis, basis4 = prep(factor, mine, other)
    near_keep, low_relay, high_relay, _ = lax.optimization_barrier((near_keep, low_relay, high_relay, factor))
    plus_low, minus_high = ring_sums(
        (near_keep, near_got, low_relay, high_relay),
        (
            ((0, plus, low), (1, plus, low), (2, plus, slice(0, w))),
            ((0, minus, high), (1, minus, high), (3, plus, slice(0, w))),
        ),
        n,
        w,
    )
    low_right = lax.ppermute(plus_low, "tensor", right_ring)
    high_left = lax.ppermute(minus_high, "tensor", left_ring)
    right_parts, basis4, _ = lax.optimization_barrier((right_parts, basis4, plus_low))

    spread_right = spread(right_parts, 1.0 / n_dp)
    q_chunks = lax.all_to_all(spread_right, "dp", 0, 0)
    near_keep, low_right, high_left, high_right, low_left, _ = lax.optimization_barrier(
        (near_keep, low_right, high_left, high_right, low_left, spread_right)
    )
    input_grad = close(near_keep, near_got, low_right, high_right, low_left, high_left)
    q_chunks, input_grad = lax.optimization_barrier((q_chunks, input_grad))
    new_error, q_factor = final(q_chunks, basis4, merged)
    return (input_grad, new_error[None], basis, q_factor)


def solution(mesh):
    return jax.shard_map(
        body,
        mesh=mesh,
        in_specs=(
            P("dp", None),
            P("dp", "tensor"),
            P(None, "tensor"),
            P("dp", None, "tensor"),
            P(None, "tensor"),
        ),
        out_specs=(P(("dp", "tensor"), None), P("dp", None, "tensor"), P(), P(None, "tensor")),
        check_vma=False,
    )
```

```python
import jax
import jax.numpy as jnp
from jax import lax
from jax.experimental import pallas as pl
from jax.experimental.pallas import tpu as pltpu
from jax.sharding import PartitionSpec as P

F32 = jnp.float32
BF16 = jnp.bfloat16
HIGHEST = lax.Precision.HIGHEST
RANK = 64
LANES = 128
VMEM = pl.BlockSpec(memory_space=pltpu.VMEM)
HBM = pl.BlockSpec(memory_space=pltpu.HBM)
NN = (((1,), (0,)), ((), ()))
NT = (((1,), (1,)), ((), ()))
TN = (((0,), (0,)), ((), ()))


def shape(dims, dtype=F32):
    return jax.ShapeDtypeStruct(dims, dtype)


def call(kernel, args, specs, outs, out_specs, scratch, n_sems, limit=56 << 20):
    return pl.pallas_call(
        kernel,
        in_specs=specs,
        out_specs=out_specs,
        out_shape=outs,
        scratch_shapes=[pltpu.VMEM(dims, dtype) for dims, dtype in scratch] + [pltpu.SemaphoreType.DMA((n_sems,))],
        compiler_params=pltpu.CompilerParams(vmem_limit_bytes=limit),
        cost_estimate=pl.CostEstimate(flops=10**6, bytes_accessed=10**5, transcendentals=0),
    )(*args)


class Copies:
    def __init__(self, sems):
        self.sems = sems
        self.all = []

    def start(self, src, dst):
        copy = pltpu.make_async_copy(src, dst, self.sems.at[len(self.all)])
        copy.start()
        self.all.append(copy)
        return copy


def split3(x):
    high = x.astype(BF16)
    rest = x - high.astype(F32)
    mid = rest.astype(BF16)
    low = (rest - mid.astype(F32)).astype(BF16)
    return jnp.concatenate([high, mid, low], axis=0)


def sum3(y):
    return (y[2 * RANK : 3 * RANK] + y[RANK : 2 * RANK]) + y[:RANK]


def dot(a, b, dims=NN):
    return lax.dot_general(a, b, dims, preferred_element_type=F32)


def dot_highest(a, b):
    return lax.dot_general(a, b, NN, precision=HIGHEST, preferred_element_type=F32)


def my_core():
    return lax.rem(lax.axis_index("tensor"), 2)


def part_of(place, width, i, parts):
    step = width // parts
    return pl.ds(pl.multiple_of(place * width + i * step, step), step)


PARTS = 4


def left_part(q3t, p3, error, acts):
    y = dot(error, q3t)
    by_error = (y[:, 2 * RANK :] + y[:, RANK : 2 * RANK]) + y[:, :RANK]
    return by_error.T + sum3(dot(p3, acts))


def store_left(out_ref, i, left):
    tiles = left.shape[1] // LANES
    for j in range(tiles):
        for g in range(4):
            out_ref[4 * (i * tiles + j) + g] = left[16 * g : 16 * g + 16, LANES * j : LANES * (j + 1)]


def half_shapes(tokens, d, ff, parts):
    step = d // 2 // parts
    return [(parts, step, ff), (parts, tokens, step)]


def fetch_half(copies, place, error_hbm, acts_hbm, error_ref, acts_ref):
    width = error_hbm.shape[0] // 2
    parts = error_ref.shape[0]
    started = []
    for i in range(parts):
        at = part_of(place, width, i, parts)
        started.append(
            (copies.start(error_hbm.at[at, :], error_ref.at[i]), copies.start(acts_hbm.at[:, at], acts_ref.at[i]))
        )
    return started


def left_send_kernel(
    q_hbm,
    cot_hbm,
    acts_hbm,
    error_hbm,
    out_ref,
    q3t_ref,
    p3_ref,
    error_keep_ref,
    acts_keep_ref,
    q_ref,
    cot_ref,
    error_ref,
    acts_ref,
    sems,
):
    core = my_core()
    copies = Copies(sems)
    q_copy = copies.start(q_hbm, q_ref)
    cot_copy = copies.start(cot_hbm, cot_ref)
    now = fetch_half(copies, 1 - core, error_hbm, acts_hbm, error_ref, acts_ref)
    later = fetch_half(copies, core, error_hbm, acts_hbm, error_keep_ref, acts_keep_ref)
    q_copy.wait()
    q3 = split3(q_ref[...])
    q3t = q3.T
    q3t_ref[...] = q3t
    cot_copy.wait()
    p3 = split3(sum3(dot(q3, cot_ref[...], NT)))
    p3_ref[...] = p3
    for i, pair in enumerate(now):
        for copy in pair:
            copy.wait()
        store_left(out_ref, i, left_part(q3t, p3, error_ref[i], acts_ref[i]))
    for pair in later:
        for copy in pair:
            copy.wait()


def left_send(q, cot, acts, error):
    tokens, d = acts.shape
    ff = cot.shape[1]
    halves = half_shapes(tokens, d, ff, PARTS)
    return call(
        left_send_kernel,
        (q, cot, acts, error),
        [HBM] * 4,
        [shape((d // 64, 16, LANES)), shape((ff, 3 * RANK), BF16), shape((3 * RANK, tokens), BF16)]
        + [shape(s, BF16) for s in halves],
        [VMEM] * 5,
        [((RANK, ff), F32), ((tokens, ff), BF16)] + [(s, BF16) for s in halves],
        2 + 4 * PARTS,
        limit=44 << 20,
    )


def left_keep_kernel(q3t_ref, p3_ref, error_ref, acts_ref, out_ref):
    for i in range(error_ref.shape[0]):
        store_left(out_ref, i, left_part(q3t_ref[...], p3_ref[...], error_ref[i], acts_ref[i]))


def left_keep(held, dims):
    return pl.pallas_call(
        left_keep_kernel,
        in_specs=[VMEM] * 4,
        out_specs=VMEM,
        out_shape=shape(dims),
        compiler_params=pltpu.CompilerParams(vmem_limit_bytes=10 << 20),
        cost_estimate=pl.CostEstimate(flops=10**6, bytes_accessed=10**5, transcendentals=0),
    )(*held)


def spread_kernel(scale, in_ref, out_ref):
    n = in_ref.shape[0]
    total = in_ref[0]
    for i in range(1, n):
        total = total + in_ref[i]
    if scale != 1.0:
        total = total * scale
    for i in range(n):
        out_ref[i] = total


def spread(x, scale):
    return pl.pallas_call(
        lambda i, o: spread_kernel(scale, i, o),
        in_specs=[VMEM],
        out_specs=VMEM,
        out_shape=shape(x.shape),
        compiler_params=pltpu.CompilerParams(vmem_limit_bytes=8 << 20),
        cost_estimate=pl.CostEstimate(flops=10**6, bytes_accessed=10**5, transcendentals=0),
    )(x)


def inverse_factor(gram):
    groups = RANK // 8
    a = [gram[8 * i : 8 * i + 8] for i in range(groups)]
    row = lax.broadcasted_iota(jnp.int32, (8, RANK), 0)
    col = lax.broadcasted_iota(jnp.int32, (8, RANK), 1)
    b = [jnp.where(row + 8 * i == col, 1.0, 0.0).astype(F32) for i in range(groups)]
    scale = []
    for k in range(groups):
        cols = [
            [jnp.broadcast_to(a[i][:, 8 * k + j : 8 * k + j + 1], (8, RANK)) if i >= k else None for i in range(groups)]
            for j in range(8)
        ]
        block_scale = jnp.zeros((8, RANK), F32)
        for j in range(8):
            pivot = jnp.broadcast_to(cols[j][k][j : j + 1], (8, RANK))
            inverse = 1.0 / pivot
            block_scale = jnp.where(row == j, lax.rsqrt(pivot), block_scale)
            row_a = jnp.broadcast_to(a[k][j : j + 1], (8, RANK))
            row_b = jnp.broadcast_to(b[k][j : j + 1], (8, RANK))
            entries = [jnp.broadcast_to(cols[m][k][j : j + 1], (8, RANK)) for m in range(j + 1, 8)]
            for i in range(k, groups):
                factor = cols[j][i] * inverse
                if i == k:
                    factor = jnp.where(row > j, factor, 0.0)
                a[i] = a[i] - factor * row_a
                b[i] = b[i] - factor * row_b
                for m in range(j + 1, 8):
                    cols[m][i] = cols[m][i] - factor * entries[m - j - 1]
        scale.append(block_scale)
    return jnp.concatenate([b[i] * scale[i] for i in range(groups)], axis=0)


def half_of(chunks_ref):
    n = chunks_ref.shape[0] // 4
    return jnp.concatenate(
        [jnp.concatenate([chunks_ref[4 * j + g] for j in range(n)], axis=1) for g in range(4)], axis=0
    )


def half_terms(left, error_ref, acts_ref, ready=None):
    parts, step = error_ref.shape[:2]
    left3 = split3(left)
    gram = [sum3(dot(left3, left3[RANK * i : RANK * (i + 1)], NT)) for i in range(3)]
    with_error = with_acts = None
    for i in range(parts):
        part = left3[:, i * step : (i + 1) * step]
        if ready is not None:
            for copy in ready[i]:
                copy.wait()
        e = dot(part, error_ref[i])
        a = dot(part, acts_ref[i], NT)
        with_error = e if i == 0 else with_error + e
        with_acts = a if i == 0 else with_acts + a
    return (gram[2] + gram[1]) + gram[0], sum3(with_error), sum3(with_acts)


def first_kernel(
    mine_hbm,
    cot_hbm,
    acts_hbm,
    error_hbm,
    gram_ref,
    with_error_ref,
    with_acts_ref,
    cot_ref,
    error_other_ref,
    acts_other_ref,
    mine_ref,
    error_ref,
    acts_ref,
    sems,
):
    core = my_core()
    copies = Copies(sems)
    mine_copy = copies.start(mine_hbm, mine_ref)
    now = fetch_half(copies, core, error_hbm, acts_hbm, error_ref, acts_ref)
    later = fetch_half(copies, 1 - core, error_hbm, acts_hbm, error_other_ref, acts_other_ref)
    cot_copy = copies.start(cot_hbm, cot_ref)
    mine_copy.wait()
    gram, with_error, with_acts = half_terms(half_of(mine_ref), error_ref, acts_ref, now)
    gram_ref[...] = gram
    with_error_ref[...] = with_error
    with_acts_ref[...] = with_acts
    for pair in later:
        for copy in pair:
            copy.wait()
    cot_copy.wait()


def first(mine, cot, acts, error, parts=1):
    tokens, d = acts.shape
    ff = cot.shape[1]
    halves = half_shapes(tokens, d, ff, parts)
    return call(
        first_kernel,
        (mine, cot, acts, error),
        [HBM] * 4,
        [shape((RANK, RANK)), shape((RANK, ff)), shape((RANK, tokens)), shape((tokens, ff), BF16)]
        + [shape(s, BF16) for s in halves],
        [VMEM] * 6,
        [(mine.shape, F32)] + [(s, BF16) for s in halves],
        2 + 4 * parts,
        limit=44 << 20,
    )


def second_kernel(
    other_ref, gram_ref, with_error_ref, with_acts_ref, cot_ref, error_ref, acts_ref, factor_ref, right_ref
):
    gram, with_error, with_acts = half_terms(half_of(other_ref), error_ref, acts_ref)
    factor = inverse_factor(gram + gram_ref[...])
    factor_ref[...] = factor
    with_acts = with_acts + with_acts_ref[...]
    merged_term = (with_error + with_error_ref[...]) + sum3(dot(split3(with_acts), cot_ref[...]))
    right = dot_highest(factor, merged_term)
    tiles = right.shape[1] // LANES
    for g in range(8):
        for j in range(tiles):
            v = g * tiles + j
            right_ref[v // 4, 8 * (v % 4) : 8 * (v % 4) + 8] = right[8 * g : 8 * g + 8, LANES * j : LANES * (j + 1)]
    for v in range(8 * tiles, 64):
        right_ref[v // 4, 8 * (v % 4) : 8 * (v % 4) + 8] = jnp.zeros((8, LANES), F32)


def second(other, terms):
    return pl.pallas_call(
        second_kernel,
        in_specs=[VMEM] * 7,
        out_specs=[VMEM, VMEM],
        out_shape=[shape((RANK, RANK)), shape((16, 32, LANES))],
        compiler_params=pltpu.CompilerParams(vmem_limit_bytes=12 << 20),
        cost_estimate=pl.CostEstimate(flops=10**6, bytes_accessed=10**5, transcendentals=0),
    )(other, *terms)


def prep_kernel(factor_ref, mine_ref, other_ref, basis_ref, out_ref):
    core = my_core()
    for ref, place in ((mine_ref, core), (other_ref, 1 - core)):
        width = ref.shape[0] // 4 * LANES
        at = pl.ds(pl.multiple_of(place * width, width), width)
        x = dot_highest(factor_ref[...], half_of(ref))
        basis_ref[:, at] = x
        high = x.astype(BF16)
        low = (x - high.astype(F32)).astype(BF16)
        both = jnp.concatenate([high, low], axis=0).T
        out_ref[at, : 2 * RANK] = both
        out_ref[at, 2 * RANK :] = both


def prep(factor, mine, other):
    d = 2 * (mine.shape[0] // 4 * LANES)
    return pl.pallas_call(
        prep_kernel,
        in_specs=[VMEM] * 3,
        out_specs=[VMEM, VMEM],
        out_shape=[shape((RANK, d)), shape((d, 4 * RANK), BF16)],
        compiler_params=pltpu.CompilerParams(vmem_limit_bytes=12 << 20),
        cost_estimate=pl.CostEstimate(flops=10**6, bytes_accessed=10**5, transcendentals=0),
    )(factor, mine, other)


def final_kernel(
    chunks_hbm,
    basis_hbm,
    cot_hbm,
    acts_hbm,
    error_hbm,
    out_hbm,
    q_ref,
    chunks_ref,
    q4_ref,
    basis_ref,
    cot_ref,
    acts_ref,
    error_ref,
    out_ref,
    sems,
):
    parts, step = error_ref.shape[:2]
    copies = Copies(sems)
    chunks_copy = copies.start(chunks_hbm, chunks_ref)
    cot_copy = copies.start(cot_hbm, cot_ref)
    waits = []
    for i in range(parts):
        at = slice(i * step, (i + 1) * step)
        waits.append(
            (
                copies.start(acts_hbm.at[:, at], acts_ref.at[i]),
                copies.start(basis_hbm.at[at, :], basis_ref.at[i]),
                copies.start(error_hbm.at[at, :], error_ref.at[i]),
            )
        )
    chunks_copy.wait()
    tiles = q_ref.shape[1] // LANES
    for g in range(8):
        for j in range(tiles):
            v = g * tiles + j
            q_ref[8 * g : 8 * g + 8, LANES * j : LANES * (j + 1)] = chunks_ref[v // 4, 8 * (v % 4) : 8 * (v % 4) + 8]
    q = -q_ref[...]
    high = q.astype(BF16)
    low = (q - high.astype(F32)).astype(BF16)
    q4_ref[...] = jnp.concatenate([high, high, low, low], axis=0)
    cot_copy.wait()
    stores = []
    for i in range(parts):
        for copy in waits[i]:
            copy.wait()
        merged = dot(acts_ref[i], cot_ref[...], TN) + error_ref[i].astype(F32)
        out_ref[i] = (merged + dot(basis_ref[i], q4_ref[...])).astype(BF16)
        stores.append(copies.start(out_ref.at[i], out_hbm.at[i * step : (i + 1) * step, :]))
    for store in stores:
        store.wait()


def final(chunks, basis4, cot, acts, error, parts=8):
    tokens, d = acts.shape
    ff = cot.shape[1]
    step = d // parts
    return call(
        final_kernel,
        (chunks, basis4, cot, acts, error),
        [HBM] * 5,
        [shape((d, ff), BF16), shape((RANK, ff))],
        [HBM, VMEM],
        [
            (chunks.shape, F32),
            ((4 * RANK, ff), BF16),
            ((parts, step, 4 * RANK), BF16),
            ((tokens, ff), BF16),
            ((parts, tokens, step), BF16),
            ((parts, step, ff), BF16),
            ((parts, step, ff), BF16),
        ],
        2 + 4 * parts,
    )


def partial_kernel(
    cot_hbm,
    weight_hbm,
    far_send_hbm,
    near_send_hbm,
    far_keep_hbm,
    near_keep_hbm,
    cot_ref,
    weight_ref,
    out_ref,
    sems,
):
    parts, step = weight_ref.shape[:2]
    core = my_core()
    x = lax.div(lax.axis_index("tensor"), 2)
    n = cot_ref.shape[0] // 8
    copies = Copies(sems)
    waits = []
    for side, h in enumerate((1 - core, core)):
        for k, hop in enumerate((2, 1, 3, 0)):
            at = pl.multiple_of((lax.rem(x + hop, 4) * 2 + h) * n, n)
            to = (side * 4 + k) * n
            waits.append(copies.start(cot_hbm.at[pl.ds(at, n), :], cot_ref.at[to : to + n, :]))
    weight_copies = [
        copies.start(weight_hbm.at[i * step : (i + 1) * step, :], weight_ref.at[i]) for i in range(parts)
    ]
    for copy in waits:
        copy.wait()
    stores = []
    targets = ((far_send_hbm, 0, n), (near_send_hbm, n, 4 * n), (far_keep_hbm, 4 * n, 5 * n), (near_keep_hbm, 5 * n, 8 * n))
    for i in range(parts):
        weight_copies[i].wait()
        out_ref[i] = dot(cot_ref[...], weight_ref[i], NT)
        for hbm, lo, hi in targets:
            stores.append(copies.start(out_ref.at[i, lo:hi, :], hbm.at[:, i * step : (i + 1) * step]))
    for store in stores:
        store.wait()


def partials(cot, weight, parts=4):
    tokens, ff = cot.shape
    d = weight.shape[0]
    n = tokens // 8
    step = d // parts
    return call(
        partial_kernel,
        (cot, weight),
        [HBM, HBM],
        [shape((r, d)) for r in (n, 3 * n, n, 3 * n)],
        [HBM] * 4,
        [((tokens, ff), BF16), ((parts, step, ff), BF16), ((parts, tokens, step), F32)],
        8 + 5 * parts,
    )


def ring_kernel(takes, ins, outs, bufs, sems):
    copies = Copies(sems)
    loads = []
    slot = 0
    for take in takes:
        started = []
        for which, rows, cols in take:
            started.append(copies.start(ins[which].at[rows, cols], bufs.at[slot]))
            slot += 1
        loads.append(started)
    stores = []
    slot = 0
    for started, out in zip(loads, outs):
        for copy in started:
            copy.wait()
        total = bufs[slot]
        for k in range(1, len(started)):
            total = total + bufs[slot + k]
        bufs[slot] = total
        stores.append(copies.start(bufs.at[slot], out))
        slot += len(started)
    for store in stores:
        store.wait()


def ring_sums(ins, takes, n, w):
    slots = sum(len(take) for take in takes)
    count = len(ins)

    def kernel(*refs):
        ring_kernel(takes, refs[:count], refs[count : count + len(takes)], *refs[count + len(takes) :])

    return call(
        kernel,
        ins,
        [HBM] * count,
        [shape((n, w))] * len(takes),
        [HBM] * len(takes),
        [((slots, n, w), F32)],
        slots + len(takes),
    )


def near_kernel(keep_hbm, got_hbm, low_hbm, high_hbm, plus_hbm, minus_hbm, keep_ref, got_ref, relay_ref, sems):
    copies = Copies(sems)
    n, d = plus_hbm.shape
    w = d // 2
    loads = [copies.start(low_hbm, relay_ref.at[0]), copies.start(high_hbm, relay_ref.at[1])]
    loads += [copies.start(src.at[: 2 * n, :], dst) for src, dst in ((keep_hbm, keep_ref), (got_hbm, got_ref))]
    for copy in loads:
        copy.wait()
    keep_ref[:n, w:] += got_ref[:n, w:]
    keep_ref[:n, :w] = (keep_ref[:n, :w] + got_ref[:n, :w]) + relay_ref[0]
    plus = copies.start(keep_ref.at[:n, :], plus_hbm)
    keep_ref[n:, :w] += got_ref[n:, :w]
    keep_ref[n:, w:] = (keep_ref[n:, w:] + got_ref[n:, w:]) + relay_ref[1]
    minus = copies.start(keep_ref.at[n:, :], minus_hbm)
    plus.wait()
    minus.wait()


def near_sums(keep, got, low, high):
    n, d = low.shape[0], keep.shape[1]
    return call(
        near_kernel,
        (keep, got, low, high),
        [HBM] * 4,
        [shape((n, d))] * 2,
        [HBM] * 2,
        [((2 * n, d), F32), ((2 * n, d), F32), ((2, n, d // 2), F32)],
        6,
    )


def close_kernel(keep_hbm, got_hbm, right_hbm, left_hbm, out_hbm, in_ref, out_ref, sems):
    copies = Copies(sems)
    n = out_ref.shape[0]
    own = slice(2 * n, 3 * n)
    loads = [
        copies.start(src, in_ref.at[i])
        for i, src in enumerate((keep_hbm.at[own, :], got_hbm.at[own, :], right_hbm, left_hbm))
    ]
    for copy in loads:
        copy.wait()
    out_ref[...] = ((in_ref[0] + in_ref[1]) + (in_ref[2] + in_ref[3])).astype(BF16)
    copies.start(out_ref, out_hbm).wait()


def close(keep, got, right, left):
    n, d = right.shape
    return call(
        close_kernel,
        (keep, got, right, left),
        [HBM] * 4,
        shape((n, d), BF16),
        HBM,
        [((4, n, d), F32), ((n, d), BF16)],
        5,
    )


def body(acts, up_cot, up_weight, error_buf, q_init):
    n_dp = lax.axis_size("dp")
    n_tensor = lax.axis_size("tensor")
    both = ("dp", "tensor")
    groups = [[2 * i + c for i in range(n_dp * n_tensor // 2)] for c in range(2)]
    pairs = [(i, i ^ 1) for i in range(n_tensor)]
    right_ring = [(i, (i + 2) % n_tensor) for i in range(n_tensor)]
    left_ring = [(i, (i - 2) % n_tensor) for i in range(n_tensor)]
    error = error_buf[0]

    send, *held = left_send(q_init, up_cot, acts, error)
    received = lax.ppermute(send, "tensor", pairs)
    total = left_keep(held, send.shape) + received
    chunks = lax.all_to_all(total, both, 0, 0, axis_index_groups=groups)

    up_weight, _ = lax.optimization_barrier((up_weight, total))
    far_send, near_send, far_keep, near_keep = partials(up_cot, up_weight)
    chunks, far_send, near_send = lax.optimization_barrier((chunks, far_send, near_send))

    spread_left = spread(chunks, 1.0)
    mine = lax.all_to_all(spread_left, both, 0, 0, axis_index_groups=groups)
    far_send, near_send, _ = lax.optimization_barrier((far_send, near_send, spread_left))
    far_got = lax.ppermute(far_send, "tensor", pairs)
    near_got = lax.ppermute(near_send, "tensor", pairs)
    n, w = far_keep.shape[0], far_keep.shape[1] // 2
    low, high = slice(0, w), slice(w, 2 * w)
    far_low, far_high = ring_sums(
        (far_keep, far_got), (((0, slice(0, n), low), (1, slice(0, n), low)), ((0, slice(0, n), high), (1, slice(0, n), high))), n, w
    )
    low_relay = lax.ppermute(far_low, "tensor", right_ring)
    high_relay = lax.ppermute(far_high, "tensor", left_ring)
    mine, _ = lax.optimization_barrier((mine, far_low))

    other = lax.ppermute(mine, "tensor", pairs)
    terms = first(mine, up_cot, acts, error)
    gram, low_relay, high_relay = lax.optimization_barrier((terms[0], low_relay, high_relay))
    factor, right = second(other, [gram, *terms[1:]])

    near_keep, _ = lax.optimization_barrier((near_keep, factor))
    plus, minus = near_sums(near_keep, near_got, low_relay, high_relay)
    from_left = lax.ppermute(plus, "tensor", right_ring)
    from_right = lax.ppermute(minus, "tensor", left_ring)
    right_parts = lax.all_to_all(right, "dp", 0, 0)
    basis, basis4 = prep(factor, mine, other)
    right_parts, basis4, _ = lax.optimization_barrier((right_parts, basis4, plus))

    spread_right = spread(right_parts, 1.0 / n_dp)
    q_chunks = lax.all_to_all(spread_right, "dp", 0, 0)
    near_keep, from_left, from_right, _ = lax.optimization_barrier((near_keep, from_left, from_right, spread_right))
    input_grad = close(near_keep, near_got, from_left, from_right)
    q_chunks, input_grad = lax.optimization_barrier((q_chunks, input_grad))
    new_error, q_factor = final(q_chunks, basis4, up_cot, acts, error)
    return (input_grad, new_error[None], basis, q_factor)


def solution(mesh):
    return jax.shard_map(
        body,
        mesh=mesh,
        in_specs=(
            P("dp", None),
            P("dp", "tensor"),
            P(None, "tensor"),
            P("dp", None, "tensor"),
            P(None, "tensor"),
        ),
        out_specs=(P(("dp", "tensor"), None), P("dp", None, "tensor"), P(), P(None, "tensor")),
        check_vma=False,
    )
```

```python
import jax
import jax.numpy as jnp
from jax import lax
from jax.experimental import pallas as pl
from jax.experimental.pallas import tpu as pltpu
from jax.sharding import PartitionSpec as P

F32 = jnp.float32
BF16 = jnp.bfloat16
HIGHEST = lax.Precision.HIGHEST
RANK = 64
LANES = 128
VMEM = pl.BlockSpec(memory_space=pltpu.VMEM)
HBM = pl.BlockSpec(memory_space=pltpu.HBM)
NN = (((1,), (0,)), ((), ()))
NT = (((1,), (1,)), ((), ()))
TN = (((0,), (0,)), ((), ()))


def shape(dims, dtype=F32):
    return jax.ShapeDtypeStruct(dims, dtype)


def call(kernel, args, specs, outs, out_specs, scratch, n_sems, limit=56 << 20):
    return pl.pallas_call(
        kernel,
        in_specs=specs,
        out_specs=out_specs,
        out_shape=outs,
        scratch_shapes=[pltpu.VMEM(dims, dtype) for dims, dtype in scratch] + [pltpu.SemaphoreType.DMA((n_sems,))],
        compiler_params=pltpu.CompilerParams(vmem_limit_bytes=limit),
        cost_estimate=pl.CostEstimate(flops=10**6, bytes_accessed=10**5, transcendentals=0),
    )(*args)


class Copies:
    def __init__(self, sems):
        self.sems = sems
        self.all = []

    def start(self, src, dst):
        copy = pltpu.make_async_copy(src, dst, self.sems.at[len(self.all)])
        copy.start()
        self.all.append(copy)
        return copy


def split3(x):
    high = x.astype(BF16)
    rest = x - high.astype(F32)
    mid = rest.astype(BF16)
    low = (rest - mid.astype(F32)).astype(BF16)
    return jnp.concatenate([high, mid, low], axis=0)


def sum3(y):
    return (y[2 * RANK : 3 * RANK] + y[RANK : 2 * RANK]) + y[:RANK]


def dot(a, b, dims=NN):
    return lax.dot_general(a, b, dims, preferred_element_type=F32)


def dot_highest(a, b):
    return lax.dot_general(a, b, NN, precision=HIGHEST, preferred_element_type=F32)


def my_core():
    return lax.rem(lax.axis_index("tensor"), 2)


def part_of(place, width, i, parts):
    step = width // parts
    return pl.ds(pl.multiple_of(place * width + i * step, step), step)


PARTS = 4


def left_part(q3t, p3, error, acts):
    y = dot(error, q3t)
    by_error = (y[:, 2 * RANK :] + y[:, RANK : 2 * RANK]) + y[:, :RANK]
    return by_error.T + sum3(dot(p3, acts))


def store_left(out_ref, i, left):
    tiles = left.shape[1] // LANES
    for j in range(tiles):
        for g in range(4):
            out_ref[4 * (i * tiles + j) + g] = left[16 * g : 16 * g + 16, LANES * j : LANES * (j + 1)]


def half_shapes(tokens, d, ff, parts):
    step = d // 2 // parts
    return [(parts, step, ff), (parts, tokens, step)]


def fetch_half(copies, place, error_hbm, acts_hbm, error_ref, acts_ref):
    width = error_hbm.shape[0] // 2
    parts = error_ref.shape[0]
    started = []
    for i in range(parts):
        at = part_of(place, width, i, parts)
        started.append(
            (copies.start(error_hbm.at[at, :], error_ref.at[i]), copies.start(acts_hbm.at[:, at], acts_ref.at[i]))
        )
    return started


def left_send_kernel(
    q_hbm,
    cot_hbm,
    acts_hbm,
    error_hbm,
    out_ref,
    q3t_ref,
    p3_ref,
    error_keep_ref,
    acts_keep_ref,
    q_ref,
    cot_ref,
    error_ref,
    acts_ref,
    sems,
):
    core = my_core()
    copies = Copies(sems)
    q_copy = copies.start(q_hbm, q_ref)
    cot_copy = copies.start(cot_hbm, cot_ref)
    now = fetch_half(copies, 1 - core, error_hbm, acts_hbm, error_ref, acts_ref)
    later = fetch_half(copies, core, error_hbm, acts_hbm, error_keep_ref, acts_keep_ref)
    q_copy.wait()
    q3 = split3(q_ref[...])
    q3t = q3.T
    q3t_ref[...] = q3t
    cot_copy.wait()
    p3 = split3(sum3(dot(q3, cot_ref[...], NT)))
    p3_ref[...] = p3
    for i, pair in enumerate(now):
        for copy in pair:
            copy.wait()
        store_left(out_ref, i, left_part(q3t, p3, error_ref[i], acts_ref[i]))
    for pair in later:
        for copy in pair:
            copy.wait()


def left_send(q, cot, acts, error):
    tokens, d = acts.shape
    ff = cot.shape[1]
    halves = half_shapes(tokens, d, ff, PARTS)
    return call(
        left_send_kernel,
        (q, cot, acts, error),
        [HBM] * 4,
        [shape((d // 64, 16, LANES)), shape((ff, 3 * RANK), BF16), shape((3 * RANK, tokens), BF16)]
        + [shape(s, BF16) for s in halves],
        [VMEM] * 5,
        [((RANK, ff), F32), ((tokens, ff), BF16)] + [(s, BF16) for s in halves],
        2 + 4 * PARTS,
        limit=44 << 20,
    )


def left_keep_kernel(q3t_ref, p3_ref, error_ref, acts_ref, out_ref):
    for i in range(error_ref.shape[0]):
        store_left(out_ref, i, left_part(q3t_ref[...], p3_ref[...], error_ref[i], acts_ref[i]))


def left_keep(held, dims):
    return pl.pallas_call(
        left_keep_kernel,
        in_specs=[VMEM] * 4,
        out_specs=VMEM,
        out_shape=shape(dims),
        compiler_params=pltpu.CompilerParams(vmem_limit_bytes=10 << 20),
        cost_estimate=pl.CostEstimate(flops=10**6, bytes_accessed=10**5, transcendentals=0),
    )(*held)


def spread_kernel(scale, in_ref, out_ref):
    n = in_ref.shape[0]
    total = in_ref[0]
    for i in range(1, n):
        total = total + in_ref[i]
    if scale != 1.0:
        total = total * scale
    for i in range(n):
        out_ref[i] = total


def spread(x, scale):
    return pl.pallas_call(
        lambda i, o: spread_kernel(scale, i, o),
        in_specs=[VMEM],
        out_specs=VMEM,
        out_shape=shape(x.shape),
        compiler_params=pltpu.CompilerParams(vmem_limit_bytes=8 << 20),
        cost_estimate=pl.CostEstimate(flops=10**6, bytes_accessed=10**5, transcendentals=0),
    )(x)


def inverse_factor(gram):
    groups = RANK // 8
    a = [gram[8 * i : 8 * i + 8] for i in range(groups)]
    row = lax.broadcasted_iota(jnp.int32, (8, RANK), 0)
    col = lax.broadcasted_iota(jnp.int32, (8, RANK), 1)
    b = [jnp.where(row + 8 * i == col, 1.0, 0.0).astype(F32) for i in range(groups)]
    scale = []
    for k in range(groups):
        cols = [
            [jnp.broadcast_to(a[i][:, 8 * k + j : 8 * k + j + 1], (8, RANK)) if i >= k else None for i in range(groups)]
            for j in range(8)
        ]
        block_scale = jnp.zeros((8, RANK), F32)
        for j in range(8):
            pivot = jnp.broadcast_to(cols[j][k][j : j + 1], (8, RANK))
            inverse = 1.0 / pivot
            block_scale = jnp.where(row == j, lax.rsqrt(pivot), block_scale)
            row_a = jnp.broadcast_to(a[k][j : j + 1], (8, RANK))
            row_b = jnp.broadcast_to(b[k][j : j + 1], (8, RANK))
            entries = [jnp.broadcast_to(cols[m][k][j : j + 1], (8, RANK)) for m in range(j + 1, 8)]
            for i in range(k, groups):
                factor = cols[j][i] * inverse
                if i == k:
                    factor = jnp.where(row > j, factor, 0.0)
                a[i] = a[i] - factor * row_a
                b[i] = b[i] - factor * row_b
                for m in range(j + 1, 8):
                    cols[m][i] = cols[m][i] - factor * entries[m - j - 1]
        scale.append(block_scale)
    return jnp.concatenate([b[i] * scale[i] for i in range(groups)], axis=0)


def half_of(*refs):
    chunks = [ref.at[i] for ref in refs for i in range(ref.shape[0])]
    return jnp.concatenate(
        [jnp.concatenate([chunk[...] for chunk in chunks[g::4]], axis=1) for g in range(4)], axis=0
    )


def half_terms(left, error_ref, acts_ref, ready=None):
    parts, step = error_ref.shape[:2]
    left3 = split3(left)
    gram = [sum3(dot(left3, left3[RANK * i : RANK * (i + 1)], NT)) for i in range(3)]
    with_error = with_acts = None
    for i in range(parts):
        part = left3[:, i * step : (i + 1) * step]
        if ready is not None:
            for copy in ready[i]:
                copy.wait()
        e = dot(part, error_ref[i])
        a = dot(part, acts_ref[i], NT)
        with_error = e if i == 0 else with_error + e
        with_acts = a if i == 0 else with_acts + a
    return (gram[2] + gram[1]) + gram[0], sum3(with_error), sum3(with_acts)


def first_kernel(
    mine_hbm,
    cot_hbm,
    acts_hbm,
    error_hbm,
    gram_ref,
    with_error_ref,
    with_acts_ref,
    cot_ref,
    error_other_ref,
    acts_other_ref,
    mine_ref,
    error_ref,
    acts_ref,
    sems,
):
    core = my_core()
    copies = Copies(sems)
    mine_copy = copies.start(mine_hbm, mine_ref)
    now = fetch_half(copies, core, error_hbm, acts_hbm, error_ref, acts_ref)
    later = fetch_half(copies, 1 - core, error_hbm, acts_hbm, error_other_ref, acts_other_ref)
    cot_copy = copies.start(cot_hbm, cot_ref)
    mine_copy.wait()
    gram, with_error, with_acts = half_terms(half_of(mine_ref), error_ref, acts_ref, now)
    gram_ref[...] = gram
    with_error_ref[...] = with_error
    with_acts_ref[...] = with_acts
    for pair in later:
        for copy in pair:
            copy.wait()
    cot_copy.wait()


def first(mine, cot, acts, error, parts=1):
    tokens, d = acts.shape
    ff = cot.shape[1]
    halves = half_shapes(tokens, d, ff, parts)
    return call(
        first_kernel,
        (mine, cot, acts, error),
        [HBM] * 4,
        [shape((RANK, RANK)), shape((RANK, ff)), shape((RANK, tokens)), shape((tokens, ff), BF16)]
        + [shape(s, BF16) for s in halves],
        [VMEM] * 6,
        [(mine.shape, F32)] + [(s, BF16) for s in halves],
        2 + 4 * parts,
        limit=44 << 20,
    )


def second_kernel(
    other_ref, gram_ref, with_error_ref, with_acts_ref, cot_ref, error_ref, acts_ref, factor_ref, right_ref
):
    gram, with_error, with_acts = half_terms(half_of(other_ref), error_ref, acts_ref)
    factor = inverse_factor(gram + gram_ref[...])
    factor_ref[...] = factor
    with_acts = with_acts + with_acts_ref[...]
    merged_term = (with_error + with_error_ref[...]) + sum3(dot(split3(with_acts), cot_ref[...]))
    right = dot_highest(factor, merged_term)
    tiles = right.shape[1] // LANES
    for g in range(8):
        for j in range(tiles):
            v = g * tiles + j
            right_ref[v // 4, 8 * (v % 4) : 8 * (v % 4) + 8] = right[8 * g : 8 * g + 8, LANES * j : LANES * (j + 1)]
    for v in range(8 * tiles, 64):
        right_ref[v // 4, 8 * (v % 4) : 8 * (v % 4) + 8] = jnp.zeros((8, LANES), F32)


def second(other, terms):
    return pl.pallas_call(
        second_kernel,
        in_specs=[VMEM] * 7,
        out_specs=[VMEM, VMEM],
        out_shape=[shape((RANK, RANK)), shape((16, 32, LANES))],
        compiler_params=pltpu.CompilerParams(vmem_limit_bytes=12 << 20),
        cost_estimate=pl.CostEstimate(flops=10**6, bytes_accessed=10**5, transcendentals=0),
    )(other, *terms)


def prep_kernel(factor_ref, mine_ref, other_ref, basis_ref, out_ref):
    core = my_core()
    width = mine_ref.shape[0] // 4 * LANES
    for ref, place in ((mine_ref, core), (other_ref, 1 - core)):
        at = pl.ds(pl.multiple_of(place * width, width), width)
        x = dot_highest(factor_ref[...], half_of(ref))
        basis_ref[:, at] = x
        high = x.astype(BF16)
        low = (x - high.astype(F32)).astype(BF16)
        both = jnp.concatenate([high, low], axis=0).T
        out_ref[at, : 2 * RANK] = both
        out_ref[at, 2 * RANK :] = both


def prep(factor, mine, other):
    d = 2 * (mine.shape[0] // 4 * LANES)
    return pl.pallas_call(
        prep_kernel,
        in_specs=[VMEM] * 3,
        out_specs=[VMEM, VMEM],
        out_shape=[shape((RANK, d)), shape((d, 4 * RANK), BF16)],
        compiler_params=pltpu.CompilerParams(vmem_limit_bytes=12 << 20),
        cost_estimate=pl.CostEstimate(flops=10**6, bytes_accessed=10**5, transcendentals=0),
    )(factor, mine, other)


def final_kernel(
    chunks_ref,
    basis_hbm,
    cot_hbm,
    acts_hbm,
    error_hbm,
    out_hbm,
    q_ref,
    q4_ref,
    basis_ref,
    cot_ref,
    acts_ref,
    error_ref,
    out_ref,
    sems,
):
    parts, step = error_ref.shape[:2]
    copies = Copies(sems)
    cot_copy = copies.start(cot_hbm, cot_ref)
    waits = []
    for i in range(parts):
        at = slice(i * step, (i + 1) * step)
        waits.append(
            (
                copies.start(acts_hbm.at[:, at], acts_ref.at[i]),
                copies.start(basis_hbm.at[at, :], basis_ref.at[i]),
                copies.start(error_hbm.at[at, :], error_ref.at[i]),
            )
        )
    tiles = q_ref.shape[1] // LANES
    for g in range(8):
        for j in range(tiles):
            v = g * tiles + j
            q_ref[8 * g : 8 * g + 8, LANES * j : LANES * (j + 1)] = chunks_ref[v // 4, 8 * (v % 4) : 8 * (v % 4) + 8]
    q = -q_ref[...]
    high = q.astype(BF16)
    low = (q - high.astype(F32)).astype(BF16)
    q4_ref[...] = jnp.concatenate([high, high, low, low], axis=0)
    cot_copy.wait()
    stores = []
    for i in range(parts):
        for copy in waits[i]:
            copy.wait()
        merged = dot(acts_ref[i], cot_ref[...], TN) + error_ref[i].astype(F32)
        out_ref[i] = (merged + dot(basis_ref[i], q4_ref[...])).astype(BF16)
        stores.append(copies.start(out_ref.at[i], out_hbm.at[i * step : (i + 1) * step, :]))
    for store in stores:
        store.wait()


def final(chunks, basis4, cot, acts, error, parts=8):
    tokens, d = acts.shape
    ff = cot.shape[1]
    step = d // parts
    return call(
        final_kernel,
        (chunks, basis4, cot, acts, error),
        [VMEM] + [HBM] * 4,
        [shape((d, ff), BF16), shape((RANK, ff))],
        [HBM, VMEM],
        [
            ((4 * RANK, ff), BF16),
            ((parts, step, 4 * RANK), BF16),
            ((tokens, ff), BF16),
            ((parts, tokens, step), BF16),
            ((parts, step, ff), BF16),
            ((parts, step, ff), BF16),
        ],
        1 + 4 * parts,
    )


def partial_kernel(
    cot_hbm,
    weight_hbm,
    far_send_hbm,
    near_send_hbm,
    far_keep_hbm,
    near_keep_hbm,
    cot_ref,
    weight_ref,
    out_ref,
    sems,
):
    parts, step = weight_ref.shape[:2]
    core = my_core()
    x = lax.div(lax.axis_index("tensor"), 2)
    n = cot_ref.shape[0] // 8
    copies = Copies(sems)
    waits = []
    for side, h in enumerate((1 - core, core)):
        for k, hop in enumerate((2, 1, 3, 0)):
            at = pl.multiple_of((lax.rem(x + hop, 4) * 2 + h) * n, n)
            to = (side * 4 + k) * n
            waits.append(copies.start(cot_hbm.at[pl.ds(at, n), :], cot_ref.at[to : to + n, :]))
    weight_copies = [
        copies.start(weight_hbm.at[i * step : (i + 1) * step, :], weight_ref.at[i]) for i in range(parts)
    ]
    for copy in waits:
        copy.wait()
    stores = []
    targets = ((far_send_hbm, 0, n), (near_send_hbm, n, 4 * n), (far_keep_hbm, 4 * n, 5 * n), (near_keep_hbm, 5 * n, 8 * n))
    for i in range(parts):
        weight_copies[i].wait()
        out_ref[i] = dot(cot_ref[...], weight_ref[i], NT)
        for hbm, lo, hi in targets:
            stores.append(copies.start(out_ref.at[i, lo:hi, :], hbm.at[:, i * step : (i + 1) * step]))
    for store in stores:
        store.wait()


def partials(cot, weight, parts=4):
    tokens, ff = cot.shape
    d = weight.shape[0]
    n = tokens // 8
    step = d // parts
    return call(
        partial_kernel,
        (cot, weight),
        [HBM, HBM],
        [shape((r, d)) for r in (n, 3 * n, n, 3 * n)],
        [HBM] * 4,
        [((tokens, ff), BF16), ((parts, step, ff), BF16), ((parts, tokens, step), F32)],
        8 + 5 * parts,
    )


def core_kernel(
    far_keep_hbm,
    far_got_hbm,
    near_keep_hbm,
    near_got_hbm,
    far_low_hbm,
    far_high_hbm,
    plus_hbm,
    minus_hbm,
    keep_ref,
    got_ref,
    sems,
):
    copies = Copies(sems)
    n, d = plus_hbm.shape
    wide = far_low_hbm.shape[1]
    rows = [slice(i * n, (i + 1) * n) for i in range(3)]
    loads = [(copies.start(far_keep_hbm, keep_ref.at[rows[0], :]), copies.start(far_got_hbm, got_ref.at[rows[0], :]))]
    for i in range(2):
        loads.append(
            (
                copies.start(near_keep_hbm.at[rows[i], :], keep_ref.at[rows[i + 1], :]),
                copies.start(near_got_hbm.at[rows[i], :], got_ref.at[rows[i + 1], :]),
            )
        )
    stores = []
    for pair, at, outs in zip(loads, rows, ((far_low_hbm, far_high_hbm), (plus_hbm,), (minus_hbm,))):
        for copy in pair:
            copy.wait()
        keep_ref[at, :] += got_ref[at, :]
        if len(outs) == 2:
            stores += [copies.start(keep_ref.at[at, :wide], outs[0]), copies.start(keep_ref.at[at, d - wide :], outs[1])]
        else:
            stores.append(copies.start(keep_ref.at[at, :], outs[0]))
    for store in stores:
        store.wait()


def core_sums(far_keep, far_got, near_keep, near_got):
    n, d = far_keep.shape
    return call(
        core_kernel,
        (far_keep, far_got, near_keep, near_got),
        [HBM] * 4,
        [shape((n, d // 2 + LANES))] * 2 + [shape((n, d))] * 2,
        [HBM] * 4,
        [((3 * n, d), F32)] * 2,
        10,
    )


def relay_kernel(plus_hbm, minus_hbm, low_hbm, high_hbm, plus_out, minus_out, half_ref, relay_ref, sems):
    copies = Copies(sems)
    d = plus_hbm.shape[1]
    w = d // 2
    wide = low_hbm.shape[1]
    parts = (
        (plus_hbm, plus_out, low_hbm, slice(0, w), slice(0, w)),
        (minus_hbm, minus_out, high_hbm, slice(w, d), slice(wide - w, wide)),
    )
    loads = [
        (copies.start(src.at[:, at], half_ref.at[i]), copies.start(relay, relay_ref.at[i]))
        for i, (src, _, relay, at, _) in enumerate(parts)
    ]
    stores = []
    for i, (_, out, _, at, far) in enumerate(parts):
        for copy in loads[i]:
            copy.wait()
        half_ref[i] += relay_ref[i, :, far]
        stores.append(copies.start(half_ref.at[i], out.at[:, at]))
    for store in stores:
        store.wait()


def relay_sums(plus, minus, low, high):
    n, d = plus.shape
    return pl.pallas_call(
        relay_kernel,
        in_specs=[HBM] * 4,
        out_specs=[HBM] * 2,
        out_shape=[shape((n, d))] * 2,
        input_output_aliases={0: 0, 1: 1},
        scratch_shapes=[
            pltpu.VMEM((2, n, d // 2), F32),
            pltpu.VMEM((2,) + low.shape, F32),
            pltpu.SemaphoreType.DMA((6,)),
        ],
        compiler_params=pltpu.CompilerParams(vmem_limit_bytes=56 << 20),
        cost_estimate=pl.CostEstimate(flops=10**6, bytes_accessed=10**5, transcendentals=0),
    )(plus, minus, low, high)


def close_kernel(keep_hbm, got_hbm, right_hbm, left_hbm, out_hbm, in_ref, out_ref, sems):
    copies = Copies(sems)
    n = out_ref.shape[0]
    own = slice(2 * n, 3 * n)
    loads = [
        copies.start(src, in_ref.at[i])
        for i, src in enumerate((keep_hbm.at[own, :], got_hbm.at[own, :], right_hbm, left_hbm))
    ]
    for copy in loads:
        copy.wait()
    out_ref[...] = ((in_ref[0] + in_ref[1]) + (in_ref[2] + in_ref[3])).astype(BF16)
    copies.start(out_ref, out_hbm).wait()


def close(keep, got, right, left):
    n, d = right.shape
    return call(
        close_kernel,
        (keep, got, right, left),
        [HBM] * 4,
        shape((n, d), BF16),
        HBM,
        [((4, n, d), F32), ((n, d), BF16)],
        5,
    )


def body(acts, up_cot, up_weight, error_buf, q_init):
    n_dp = lax.axis_size("dp")
    n_tensor = lax.axis_size("tensor")
    both = ("dp", "tensor")
    groups = [[2 * i + c for i in range(n_dp * n_tensor // 2)] for c in range(2)]
    pairs = [(i, i ^ 1) for i in range(n_tensor)]
    right_ring = [(i, (i + 2) % n_tensor) for i in range(n_tensor)]
    left_ring = [(i, (i - 2) % n_tensor) for i in range(n_tensor)]
    error = error_buf[0]

    send, *held = left_send(q_init, up_cot, acts, error)
    received = lax.ppermute(send, "tensor", pairs)
    total = left_keep(held, send.shape) + received
    chunks = lax.all_to_all(total, both, 0, 0, axis_index_groups=groups)

    up_weight, _ = lax.optimization_barrier((up_weight, total))
    far_send, near_send, far_keep, near_keep = partials(up_cot, up_weight)
    chunks, far_send, near_send = lax.optimization_barrier((chunks, far_send, near_send))

    spread_left = spread(chunks, 1.0)
    mine = lax.all_to_all(spread_left, both, 0, 0, axis_index_groups=groups)
    far_send, near_send, _ = lax.optimization_barrier((far_send, near_send, spread_left))
    far_got = lax.ppermute(far_send, "tensor", pairs)
    near_got = lax.ppermute(near_send, "tensor", pairs)
    far_low, far_high, plus, minus = core_sums(far_keep, far_got, near_keep, near_got)
    low_relay = lax.ppermute(far_low, "tensor", right_ring)
    high_relay = lax.ppermute(far_high, "tensor", left_ring)
    mine, _ = lax.optimization_barrier((mine, far_low))

    other = lax.ppermute(mine, "tensor", pairs)
    terms = first(mine, up_cot, acts, error)
    factor, right = second(other, terms)

    low_relay, high_relay, right = lax.optimization_barrier((low_relay, high_relay, right))
    plus, minus = relay_sums(plus, minus, low_relay, high_relay)
    from_left = lax.ppermute(plus, "tensor", right_ring)
    from_right = lax.ppermute(minus, "tensor", left_ring)
    right_parts = lax.all_to_all(right, "dp", 0, 0)
    basis, basis4 = prep(factor, mine, other)
    right_parts, basis4 = lax.optimization_barrier((right_parts, basis4))

    spread_right = spread(right_parts, 1.0 / n_dp)
    q_chunks = lax.all_to_all(spread_right, "dp", 0, 0)
    near_keep, from_left, from_right, _ = lax.optimization_barrier((near_keep, from_left, from_right, spread_right))
    input_grad = close(near_keep, near_got, from_left, from_right)
    q_chunks, input_grad = lax.optimization_barrier((q_chunks, input_grad))
    new_error, q_factor = final(q_chunks, basis4, up_cot, acts, error)
    return (input_grad, new_error[None], basis, q_factor)


def solution(mesh):
    return jax.shard_map(
        body,
        mesh=mesh,
        in_specs=(
            P("dp", None),
            P("dp", "tensor"),
            P(None, "tensor"),
            P("dp", None, "tensor"),
            P(None, "tensor"),
        ),
        out_specs=(P(("dp", "tensor"), None), P("dp", None, "tensor"), P(), P(None, "tensor")),
        check_vma=False,
    )
```

```python
import jax
import jax.numpy as jnp
from jax import lax
from jax.experimental import pallas as pl
from jax.experimental.pallas import tpu as pltpu
from jax.sharding import PartitionSpec as P

F32 = jnp.float32
BF16 = jnp.bfloat16
HIGHEST = lax.Precision.HIGHEST
RANK = 64
LANES = 128
VMEM = pl.BlockSpec(memory_space=pltpu.VMEM)
HBM = pl.BlockSpec(memory_space=pltpu.HBM)
NN = (((1,), (0,)), ((), ()))
NT = (((1,), (1,)), ((), ()))
TN = (((0,), (0,)), ((), ()))


def shape(dims, dtype=F32):
    return jax.ShapeDtypeStruct(dims, dtype)


def call(kernel, args, specs, outs, out_specs, scratch, n_sems, limit=56 << 20):
    return pl.pallas_call(
        kernel,
        in_specs=specs,
        out_specs=out_specs,
        out_shape=outs,
        scratch_shapes=[pltpu.VMEM(dims, dtype) for dims, dtype in scratch] + [pltpu.SemaphoreType.DMA((n_sems,))],
        compiler_params=pltpu.CompilerParams(vmem_limit_bytes=limit),
        cost_estimate=pl.CostEstimate(flops=10**6, bytes_accessed=10**5, transcendentals=0),
    )(*args)


class Copies:
    def __init__(self, sems):
        self.sems = sems
        self.all = []

    def start(self, src, dst):
        copy = pltpu.make_async_copy(src, dst, self.sems.at[len(self.all)])
        copy.start()
        self.all.append(copy)
        return copy


def split3(x):
    high = x.astype(BF16)
    rest = x - high.astype(F32)
    mid = rest.astype(BF16)
    low = (rest - mid.astype(F32)).astype(BF16)
    return jnp.concatenate([high, mid, low], axis=0)


def sum3(y):
    return (y[2 * RANK : 3 * RANK] + y[RANK : 2 * RANK]) + y[:RANK]


def dot(a, b, dims=NN):
    return lax.dot_general(a, b, dims, preferred_element_type=F32)


def dot_highest(a, b):
    return lax.dot_general(a, b, NN, precision=HIGHEST, preferred_element_type=F32)


def my_core():
    return lax.rem(lax.axis_index("tensor"), 2)


def part_of(place, width, i, parts):
    step = width // parts
    return pl.ds(pl.multiple_of(place * width + i * step, step), step)


PARTS = 4


def left_part(q3t, p3, error, acts):
    y = dot(error, q3t)
    by_error = (y[:, 2 * RANK :] + y[:, RANK : 2 * RANK]) + y[:, :RANK]
    return by_error.T + sum3(dot(p3, acts))


def store_left(out_ref, i, left):
    tiles = left.shape[1] // LANES
    for j in range(tiles):
        for g in range(8):
            out_ref[8 * (i * tiles + j) + g] = left[8 * g : 8 * g + 8, LANES * j : LANES * (j + 1)]


def half_shapes(tokens, d, ff, parts):
    step = d // 2 // parts
    return [(parts, step, ff), (parts, tokens, step)]


def fetch_half(copies, place, error_hbm, acts_hbm, error_ref, acts_ref):
    width = error_hbm.shape[0] // 2
    parts = error_ref.shape[0]
    started = []
    for i in range(parts):
        at = part_of(place, width, i, parts)
        started.append(
            (copies.start(error_hbm.at[at, :], error_ref.at[i]), copies.start(acts_hbm.at[:, at], acts_ref.at[i]))
        )
    return started


def left_send_kernel(
    q_hbm,
    cot_hbm,
    acts_hbm,
    error_hbm,
    out_ref,
    q3t_ref,
    p3_ref,
    error_keep_ref,
    acts_keep_ref,
    q_ref,
    cot_ref,
    error_ref,
    acts_ref,
    sems,
):
    core = my_core()
    copies = Copies(sems)
    q_copy = copies.start(q_hbm, q_ref)
    cot_copy = copies.start(cot_hbm, cot_ref)
    now = fetch_half(copies, 1 - core, error_hbm, acts_hbm, error_ref, acts_ref)
    later = fetch_half(copies, core, error_hbm, acts_hbm, error_keep_ref, acts_keep_ref)
    q_copy.wait()
    q3 = split3(q_ref[...])
    q3t = q3.T
    q3t_ref[...] = q3t
    cot_copy.wait()
    p3 = split3(sum3(dot(q3, cot_ref[...], NT)))
    p3_ref[...] = p3
    for i, pair in enumerate(now):
        for copy in pair:
            copy.wait()
        store_left(out_ref, i, left_part(q3t, p3, error_ref[i], acts_ref[i]))
    for pair in later:
        for copy in pair:
            copy.wait()


def left_send(q, cot, acts, error):
    tokens, d = acts.shape
    ff = cot.shape[1]
    halves = half_shapes(tokens, d, ff, PARTS)
    return call(
        left_send_kernel,
        (q, cot, acts, error),
        [HBM] * 4,
        [shape((d // 32, 8, LANES)), shape((ff, 3 * RANK), BF16), shape((3 * RANK, tokens), BF16)]
        + [shape(s, BF16) for s in halves],
        [VMEM] * 5,
        [((RANK, ff), F32), ((tokens, ff), BF16)] + [(s, BF16) for s in halves],
        2 + 4 * PARTS,
        limit=44 << 20,
    )


def left_keep_kernel(q3t_ref, p3_ref, error_ref, acts_ref, out_ref):
    for i in range(error_ref.shape[0]):
        store_left(out_ref, i, left_part(q3t_ref[...], p3_ref[...], error_ref[i], acts_ref[i]))


def left_keep(held, dims):
    return pl.pallas_call(
        left_keep_kernel,
        in_specs=[VMEM] * 4,
        out_specs=VMEM,
        out_shape=shape(dims),
        compiler_params=pltpu.CompilerParams(vmem_limit_bytes=10 << 20),
        cost_estimate=pl.CostEstimate(flops=10**6, bytes_accessed=10**5, transcendentals=0),
    )(*held)


def spread_kernel(scale, kinds, in_ref, out_ref):
    n = in_ref.shape[0]
    for kind in range(kinds):
        total = in_ref[kind]
        for i in range(kind + kinds, n, kinds):
            total = total + in_ref[i]
        if scale != 1.0:
            total = total * scale
        for i in range(kind, n, kinds):
            out_ref[i] = total


def spread(x, scale, kinds=1):
    return pl.pallas_call(
        lambda i, o: spread_kernel(scale, kinds, i, o),
        in_specs=[VMEM],
        out_specs=VMEM,
        out_shape=shape(x.shape),
        compiler_params=pltpu.CompilerParams(vmem_limit_bytes=8 << 20),
        cost_estimate=pl.CostEstimate(flops=10**6, bytes_accessed=10**5, transcendentals=0),
    )(x)


def inverse_factor(gram):
    groups = RANK // 8
    a = [gram[8 * i : 8 * i + 8] for i in range(groups)]
    row = lax.broadcasted_iota(jnp.int32, (8, RANK), 0)
    col = lax.broadcasted_iota(jnp.int32, (8, RANK), 1)
    b = [jnp.where(row + 8 * i == col, 1.0, 0.0).astype(F32) for i in range(groups)]
    scale = []
    for k in range(groups):
        cols = [
            [jnp.broadcast_to(a[i][:, 8 * k + j : 8 * k + j + 1], (8, RANK)) if i >= k else None for i in range(groups)]
            for j in range(8)
        ]
        block_scale = jnp.zeros((8, RANK), F32)
        for j in range(8):
            pivot = jnp.broadcast_to(cols[j][k][j : j + 1], (8, RANK))
            inverse = 1.0 / pivot
            block_scale = jnp.where(row == j, lax.rsqrt(pivot), block_scale)
            row_a = jnp.broadcast_to(a[k][j : j + 1], (8, RANK))
            row_b = jnp.broadcast_to(b[k][j : j + 1], (8, RANK))
            entries = [jnp.broadcast_to(cols[m][k][j : j + 1], (8, RANK)) for m in range(j + 1, 8)]
            for i in range(k, groups):
                factor = cols[j][i] * inverse
                if i == k:
                    factor = jnp.where(row > j, factor, 0.0)
                a[i] = a[i] - factor * row_a
                b[i] = b[i] - factor * row_b
                for m in range(j + 1, 8):
                    cols[m][i] = cols[m][i] - factor * entries[m - j - 1]
        scale.append(block_scale)
    return jnp.concatenate([b[i] * scale[i] for i in range(groups)], axis=0)


def half_of(tiles_ref):
    n = tiles_ref.shape[0] // 8
    return jnp.concatenate(
        [jnp.concatenate([tiles_ref[8 * j + g] for j in range(n)], axis=1) for g in range(8)], axis=0
    )


def half_terms(left, error_ref, acts_ref, ready=None):
    parts, step = error_ref.shape[:2]
    left3 = split3(left)
    gram = [sum3(dot(left3, left3[RANK * i : RANK * (i + 1)], NT)) for i in range(3)]
    with_error = with_acts = None
    for i in range(parts):
        part = left3[:, i * step : (i + 1) * step]
        if ready is not None:
            for copy in ready[i]:
                copy.wait()
        e = dot(part, error_ref[i])
        a = dot(part, acts_ref[i], NT)
        with_error = e if i == 0 else with_error + e
        with_acts = a if i == 0 else with_acts + a
    return (gram[2] + gram[1]) + gram[0], sum3(with_error), sum3(with_acts)


def first_kernel(
    mine_hbm,
    cot_hbm,
    acts_hbm,
    error_hbm,
    gram_ref,
    with_error_ref,
    with_acts_ref,
    cot_ref,
    error_other_ref,
    acts_other_ref,
    mine_ref,
    error_ref,
    acts_ref,
    sems,
):
    core = my_core()
    copies = Copies(sems)
    mine_copy = copies.start(mine_hbm, mine_ref)
    now = fetch_half(copies, core, error_hbm, acts_hbm, error_ref, acts_ref)
    later = fetch_half(copies, 1 - core, error_hbm, acts_hbm, error_other_ref, acts_other_ref)
    cot_copy = copies.start(cot_hbm, cot_ref)
    mine_copy.wait()
    gram, with_error, with_acts = half_terms(half_of(mine_ref), error_ref, acts_ref, now)
    gram_ref[...] = gram
    with_error_ref[...] = with_error
    with_acts_ref[...] = with_acts
    for pair in later:
        for copy in pair:
            copy.wait()
    cot_copy.wait()


def first(mine, cot, acts, error, parts=1):
    tokens, d = acts.shape
    ff = cot.shape[1]
    halves = half_shapes(tokens, d, ff, parts)
    return call(
        first_kernel,
        (mine, cot, acts, error),
        [HBM] * 4,
        [shape((RANK, RANK)), shape((RANK, ff)), shape((RANK, tokens)), shape((tokens, ff), BF16)]
        + [shape(s, BF16) for s in halves],
        [VMEM] * 6,
        [(mine.shape, F32)] + [(s, BF16) for s in halves],
        2 + 4 * parts,
        limit=44 << 20,
    )


def second_kernel(
    other_ref, gram_ref, with_error_ref, with_acts_ref, cot_ref, error_ref, acts_ref, factor_ref, right_ref
):
    gram, with_error, with_acts = half_terms(half_of(other_ref), error_ref, acts_ref)
    factor = inverse_factor(gram + gram_ref[...])
    factor_ref[...] = factor
    with_acts = with_acts + with_acts_ref[...]
    merged_term = (with_error + with_error_ref[...]) + sum3(dot(split3(with_acts), cot_ref[...]))
    right = dot_highest(factor, merged_term)
    tiles = right.shape[1] // LANES
    for g in range(8):
        for j in range(tiles):
            v = g * tiles + j
            right_ref[v // 4, 8 * (v % 4) : 8 * (v % 4) + 8] = right[8 * g : 8 * g + 8, LANES * j : LANES * (j + 1)]
    for v in range(8 * tiles, 64):
        right_ref[v // 4, 8 * (v % 4) : 8 * (v % 4) + 8] = jnp.zeros((8, LANES), F32)


def second(other, terms):
    return pl.pallas_call(
        second_kernel,
        in_specs=[VMEM] * 7,
        out_specs=[VMEM, VMEM],
        out_shape=[shape((RANK, RANK)), shape((16, 32, LANES))],
        compiler_params=pltpu.CompilerParams(vmem_limit_bytes=12 << 20),
        cost_estimate=pl.CostEstimate(flops=10**6, bytes_accessed=10**5, transcendentals=0),
    )(other, *terms)


def prep_kernel(factor_ref, mine_ref, other_ref, basis_ref, out_ref):
    core = my_core()
    width = mine_ref.shape[0] // 8 * LANES
    for ref, place in ((mine_ref, core), (other_ref, 1 - core)):
        at = pl.ds(pl.multiple_of(place * width, width), width)
        x = dot_highest(factor_ref[...], half_of(ref))
        basis_ref[:, at] = x
        high = x.astype(BF16)
        low = (x - high.astype(F32)).astype(BF16)
        both = jnp.concatenate([high, low], axis=0).T
        out_ref[at, : 2 * RANK] = both
        out_ref[at, 2 * RANK :] = both


def prep(factor, mine, other):
    d = 2 * (mine.shape[0] // 8 * LANES)
    return pl.pallas_call(
        prep_kernel,
        in_specs=[VMEM] * 3,
        out_specs=[VMEM, VMEM],
        out_shape=[shape((RANK, d)), shape((d, 4 * RANK), BF16)],
        compiler_params=pltpu.CompilerParams(vmem_limit_bytes=12 << 20),
        cost_estimate=pl.CostEstimate(flops=10**6, bytes_accessed=10**5, transcendentals=0),
    )(factor, mine, other)


def final_kernel(
    chunks_hbm,
    basis_hbm,
    cot_hbm,
    acts_hbm,
    error_hbm,
    out_hbm,
    q_ref,
    chunks_ref,
    q4_ref,
    basis_ref,
    cot_ref,
    acts_ref,
    error_ref,
    out_ref,
    sems,
):
    parts, step = error_ref.shape[:2]
    copies = Copies(sems)
    chunks_copy = copies.start(chunks_hbm, chunks_ref)
    cot_copy = copies.start(cot_hbm, cot_ref)
    waits = []
    for i in range(parts):
        at = slice(i * step, (i + 1) * step)
        waits.append(
            (
                copies.start(acts_hbm.at[:, at], acts_ref.at[i]),
                copies.start(error_hbm.at[at, :], error_ref.at[i]),
                copies.start(basis_hbm.at[at, :], basis_ref.at[i]),
            )
        )
    chunks_copy.wait()
    tiles = q_ref.shape[1] // LANES
    for g in range(8):
        for j in range(tiles):
            v = g * tiles + j
            q_ref[8 * g : 8 * g + 8, LANES * j : LANES * (j + 1)] = chunks_ref[v // 4, 8 * (v % 4) : 8 * (v % 4) + 8]
    q = -q_ref[...]
    high = q.astype(BF16)
    low = (q - high.astype(F32)).astype(BF16)
    q4_ref[...] = jnp.concatenate([high, high, low, low], axis=0)
    cot_copy.wait()
    stores = []
    for i in range(parts):
        for copy in waits[i]:
            copy.wait()
        merged = dot(acts_ref[i], cot_ref[...], TN) + error_ref[i].astype(F32)
        out_ref[i] = (merged + dot(basis_ref[i], q4_ref[...])).astype(BF16)
        stores.append(copies.start(out_ref.at[i], out_hbm.at[i * step : (i + 1) * step, :]))
    for store in stores:
        store.wait()


def final(chunks, basis4, cot, acts, error, parts=8):
    tokens, d = acts.shape
    ff = cot.shape[1]
    step = d // parts
    return call(
        final_kernel,
        (chunks, basis4, cot, acts, error),
        [HBM] * 5,
        [shape((d, ff), BF16), shape((RANK, ff))],
        [HBM, VMEM],
        [
            (chunks.shape, F32),
            ((4 * RANK, ff), BF16),
            ((parts, step, 4 * RANK), BF16),
            ((tokens, ff), BF16),
            ((parts, tokens, step), BF16),
            ((parts, step, ff), BF16),
            ((parts, step, ff), BF16),
        ],
        2 + 4 * parts,
    )


def partial_kernel(
    cot_hbm,
    weight_hbm,
    far_send_hbm,
    near_send_hbm,
    far_keep_hbm,
    near_keep_hbm,
    cot_ref,
    weight_ref,
    out_ref,
    sems,
):
    parts, step = weight_ref.shape[:2]
    core = my_core()
    x = lax.div(lax.axis_index("tensor"), 2)
    n = cot_ref.shape[0] // 8
    copies = Copies(sems)
    waits = []
    for side, h in enumerate((1 - core, core)):
        for k, hop in enumerate((2, 1, 3, 0)):
            at = pl.multiple_of((lax.rem(x + hop, 4) * 2 + h) * n, n)
            to = (side * 4 + k) * n
            waits.append(copies.start(cot_hbm.at[pl.ds(at, n), :], cot_ref.at[to : to + n, :]))
    weight_copies = [
        copies.start(weight_hbm.at[i * step : (i + 1) * step, :], weight_ref.at[i]) for i in range(parts)
    ]
    for copy in waits:
        copy.wait()
    stores = []
    targets = ((far_send_hbm, 0, n), (near_send_hbm, n, 4 * n), (far_keep_hbm, 4 * n, 5 * n), (near_keep_hbm, 5 * n, 8 * n))
    for i in range(parts):
        weight_copies[i].wait()
        out_ref[i] = dot(cot_ref[...], weight_ref[i], NT)
        for hbm, lo, hi in targets:
            stores.append(copies.start(out_ref.at[i, lo:hi, :], hbm.at[:, i * step : (i + 1) * step]))
    for store in stores:
        store.wait()


def partials(cot, weight, parts=4):
    tokens, ff = cot.shape
    d = weight.shape[0]
    n = tokens // 8
    step = d // parts
    return call(
        partial_kernel,
        (cot, weight),
        [HBM, HBM],
        [shape((r, d)) for r in (n, 3 * n, n, 3 * n)],
        [HBM] * 4,
        [((tokens, ff), BF16), ((parts, step, ff), BF16), ((parts, tokens, step), F32)],
        8 + 5 * parts,
    )


def core_kernel(
    far_keep_hbm,
    far_got_hbm,
    near_keep_hbm,
    near_got_hbm,
    far_low_hbm,
    far_high_hbm,
    plus_hbm,
    minus_hbm,
    keep_ref,
    got_ref,
    sems,
):
    copies = Copies(sems)
    n, d = plus_hbm.shape
    wide = far_low_hbm.shape[1]
    rows = [slice(i * n, (i + 1) * n) for i in range(3)]
    loads = [(copies.start(far_keep_hbm, keep_ref.at[rows[0], :]), copies.start(far_got_hbm, got_ref.at[rows[0], :]))]
    for i in range(2):
        loads.append(
            (
                copies.start(near_keep_hbm.at[rows[i], :], keep_ref.at[rows[i + 1], :]),
                copies.start(near_got_hbm.at[rows[i], :], got_ref.at[rows[i + 1], :]),
            )
        )
    stores = []
    for pair, at, outs in zip(loads, rows, ((far_low_hbm, far_high_hbm), (plus_hbm,), (minus_hbm,))):
        for copy in pair:
            copy.wait()
        keep_ref[at, :] += got_ref[at, :]
        if len(outs) == 2:
            stores += [copies.start(keep_ref.at[at, :wide], outs[0]), copies.start(keep_ref.at[at, d - wide :], outs[1])]
        else:
            stores.append(copies.start(keep_ref.at[at, :], outs[0]))
    for store in stores:
        store.wait()


def core_sums(far_keep, far_got, near_keep, near_got):
    n, d = far_keep.shape
    return call(
        core_kernel,
        (far_keep, far_got, near_keep, near_got),
        [HBM] * 4,
        [shape((n, d // 2 + LANES))] * 2 + [shape((n, d))] * 2,
        [HBM] * 4,
        [((3 * n, d), F32)] * 2,
        10,
    )


def relay_kernel(plus_hbm, minus_hbm, low_ref, high_ref, plus_out, minus_out, half_ref, sems):
    copies = Copies(sems)
    d = plus_hbm.shape[1]
    w = d // 2
    wide = low_ref.shape[1]
    parts = (
        (plus_hbm, plus_out, low_ref, slice(0, w), slice(0, w)),
        (minus_hbm, minus_out, high_ref, slice(w, d), slice(wide - w, wide)),
    )
    loads = [copies.start(src.at[:, at], half_ref.at[i]) for i, (src, _, _, at, _) in enumerate(parts)]
    stores = []
    for i, (_, out, relay, at, far) in enumerate(parts):
        loads[i].wait()
        half_ref[i] += relay[:, far]
        stores.append(copies.start(half_ref.at[i], out.at[:, at]))
    for store in stores:
        store.wait()


def relay_sums(plus, minus, low, high):
    n, d = plus.shape
    return pl.pallas_call(
        relay_kernel,
        in_specs=[HBM] * 2 + [VMEM] * 2,
        out_specs=[HBM] * 2,
        out_shape=[shape((n, d))] * 2,
        input_output_aliases={0: 0, 1: 1},
        scratch_shapes=[
            pltpu.VMEM((2, n, d // 2), F32),
            pltpu.SemaphoreType.DMA((4,)),
        ],
        compiler_params=pltpu.CompilerParams(vmem_limit_bytes=52 << 20),
        cost_estimate=pl.CostEstimate(flops=10**6, bytes_accessed=10**5, transcendentals=0),
    )(plus, minus, low, high)


def close_kernel(keep_hbm, got_hbm, right_hbm, left_hbm, out_hbm, in_ref, out_ref, sems):
    copies = Copies(sems)
    n = out_ref.shape[0]
    own = slice(2 * n, 3 * n)
    loads = [
        copies.start(src, in_ref.at[i])
        for i, src in enumerate((keep_hbm.at[own, :], got_hbm.at[own, :], right_hbm, left_hbm))
    ]
    for copy in loads:
        copy.wait()
    out_ref[...] = ((in_ref[0] + in_ref[1]) + (in_ref[2] + in_ref[3])).astype(BF16)
    copies.start(out_ref, out_hbm).wait()


def close(keep, got, right, left):
    n, d = right.shape
    return call(
        close_kernel,
        (keep, got, right, left),
        [HBM] * 4,
        shape((n, d), BF16),
        HBM,
        [((4, n, d), F32), ((n, d), BF16)],
        5,
    )


def body(acts, up_cot, up_weight, error_buf, q_init):
    n_dp = lax.axis_size("dp")
    n_tensor = lax.axis_size("tensor")
    both = ("dp", "tensor")
    pairs = [(i, i ^ 1) for i in range(n_tensor)]
    right_ring = [(i, (i + 2) % n_tensor) for i in range(n_tensor)]
    left_ring = [(i, (i - 2) % n_tensor) for i in range(n_tensor)]
    error = error_buf[0]

    send, *held = left_send(q_init, up_cot, acts, error)
    received = lax.ppermute(send, "tensor", pairs)
    total = left_keep(held, send.shape) + received
    chunks = lax.all_to_all(total, both, 0, 0)

    up_weight, _ = lax.optimization_barrier((up_weight, total))
    far_send, near_send, far_keep, near_keep = partials(up_cot, up_weight)
    chunks, far_send, near_send = lax.optimization_barrier((chunks, far_send, near_send))

    spread_left = spread(chunks, 1.0, kinds=2)
    mine = lax.all_to_all(spread_left, both, 0, 0)
    far_send, near_send, _ = lax.optimization_barrier((far_send, near_send, spread_left))
    far_got = lax.ppermute(far_send, "tensor", pairs)
    near_got = lax.ppermute(near_send, "tensor", pairs)
    far_low, far_high, plus, minus = core_sums(far_keep, far_got, near_keep, near_got)
    low_relay = lax.ppermute(far_low, "tensor", right_ring)
    high_relay = lax.ppermute(far_high, "tensor", left_ring)
    mine, _ = lax.optimization_barrier((mine, far_low))

    other = lax.ppermute(mine, "tensor", pairs)
    terms = first(mine, up_cot, acts, error)
    factor, right = second(other, terms)

    low_relay, high_relay, right = lax.optimization_barrier((low_relay, high_relay, right))
    plus, minus = relay_sums(plus, minus, low_relay, high_relay)
    from_left = lax.ppermute(plus, "tensor", right_ring)
    from_right = lax.ppermute(minus, "tensor", left_ring)
    right_parts = lax.all_to_all(right, "dp", 0, 0)
    basis, basis4 = prep(factor, mine, other)
    right_parts, basis4 = lax.optimization_barrier((right_parts, basis4))

    spread_right = spread(right_parts, 1.0 / n_dp)
    q_chunks = lax.all_to_all(spread_right, "dp", 0, 0)
    near_keep, from_left, from_right, _ = lax.optimization_barrier((near_keep, from_left, from_right, spread_right))
    input_grad = close(near_keep, near_got, from_left, from_right)
    q_chunks, input_grad = lax.optimization_barrier((q_chunks, input_grad))
    new_error, q_factor = final(q_chunks, basis4, up_cot, acts, error)
    return (input_grad, new_error[None], basis, q_factor)


def solution(mesh):
    return jax.shard_map(
        body,
        mesh=mesh,
        in_specs=(
            P("dp", None),
            P("dp", "tensor"),
            P(None, "tensor"),
            P("dp", None, "tensor"),
            P(None, "tensor"),
        ),
        out_specs=(P(("dp", "tensor"), None), P("dp", None, "tensor"), P(), P(None, "tensor")),
        check_vma=False,
    )
```

```python
import jax
import jax.numpy as jnp
from jax import lax
from jax.experimental import pallas as pl
from jax.experimental.pallas import tpu as pltpu
from jax.sharding import PartitionSpec as P

F32 = jnp.float32
BF16 = jnp.bfloat16
HIGHEST = lax.Precision.HIGHEST
RANK = 64
LANES = 128
VMEM = pl.BlockSpec(memory_space=pltpu.VMEM)
HBM = pl.BlockSpec(memory_space=pltpu.HBM)
NN = (((1,), (0,)), ((), ()))
NT = (((1,), (1,)), ((), ()))
TN = (((0,), (0,)), ((), ()))


def shape(dims, dtype=F32):
    return jax.ShapeDtypeStruct(dims, dtype)


def call(kernel, args, specs, outs, out_specs, scratch, n_sems, limit=56 << 20):
    return pl.pallas_call(
        kernel,
        in_specs=specs,
        out_specs=out_specs,
        out_shape=outs,
        scratch_shapes=[pltpu.VMEM(dims, dtype) for dims, dtype in scratch] + [pltpu.SemaphoreType.DMA((n_sems,))],
        compiler_params=pltpu.CompilerParams(vmem_limit_bytes=limit),
        cost_estimate=pl.CostEstimate(flops=10**6, bytes_accessed=10**5, transcendentals=0),
    )(*args)


class Copies:
    def __init__(self, sems):
        self.sems = sems
        self.all = []

    def start(self, src, dst):
        copy = pltpu.make_async_copy(src, dst, self.sems.at[len(self.all)])
        copy.start()
        self.all.append(copy)
        return copy


def split3(x):
    high = x.astype(BF16)
    rest = x - high.astype(F32)
    mid = rest.astype(BF16)
    low = (rest - mid.astype(F32)).astype(BF16)
    return jnp.concatenate([high, mid, low], axis=0)


def sum3(y):
    return (y[2 * RANK : 3 * RANK] + y[RANK : 2 * RANK]) + y[:RANK]


def dot(a, b, dims=NN):
    return lax.dot_general(a, b, dims, preferred_element_type=F32)


def dot_highest(a, b):
    return lax.dot_general(a, b, NN, precision=HIGHEST, preferred_element_type=F32)


def my_core():
    return lax.rem(lax.axis_index("tensor"), 2)


def part_of(place, width, i, parts):
    step = width // parts
    return pl.ds(pl.multiple_of(place * width + i * step, step), step)


PARTS = 4


def left_part(q3t, p3, error, acts):
    y = dot(error, q3t)
    by_error = (y[:, 2 * RANK :] + y[:, RANK : 2 * RANK]) + y[:, :RANK]
    return by_error.T + sum3(dot(p3, acts))


def store_left(out_ref, i, left):
    tiles = left.shape[1] // LANES
    for j in range(tiles):
        for g in range(8):
            out_ref[8 * (i * tiles + j) + g] = left[8 * g : 8 * g + 8, LANES * j : LANES * (j + 1)]


def half_shapes(tokens, d, ff, parts):
    step = d // 2 // parts
    return [(parts, step, ff), (parts, tokens, step)]


def fetch_half(copies, place, error_hbm, acts_hbm, error_ref, acts_ref):
    width = error_hbm.shape[0] // 2
    parts = error_ref.shape[0]
    started = []
    for i in range(parts):
        at = part_of(place, width, i, parts)
        started.append(
            (copies.start(error_hbm.at[at, :], error_ref.at[i]), copies.start(acts_hbm.at[:, at], acts_ref.at[i]))
        )
    return started


def left_send_kernel(
    q_hbm,
    cot_hbm,
    acts_hbm,
    error_hbm,
    out_ref,
    q3t_ref,
    p3_ref,
    error_keep_ref,
    acts_keep_ref,
    q_ref,
    cot_ref,
    error_ref,
    acts_ref,
    sems,
):
    core = my_core()
    copies = Copies(sems)
    q_copy = copies.start(q_hbm, q_ref)
    cot_copy = copies.start(cot_hbm, cot_ref)
    now = fetch_half(copies, 1 - core, error_hbm, acts_hbm, error_ref, acts_ref)
    later = fetch_half(copies, core, error_hbm, acts_hbm, error_keep_ref, acts_keep_ref)
    q_copy.wait()
    q3 = split3(q_ref[...])
    q3t = q3.T
    q3t_ref[...] = q3t
    cot_copy.wait()
    p3 = split3(sum3(dot(q3, cot_ref[...], NT)))
    p3_ref[...] = p3
    for i, pair in enumerate(now):
        for copy in pair:
            copy.wait()
        store_left(out_ref, i, left_part(q3t, p3, error_ref[i], acts_ref[i]))
    for pair in later:
        for copy in pair:
            copy.wait()


def left_send(q, cot, acts, error):
    tokens, d = acts.shape
    ff = cot.shape[1]
    halves = half_shapes(tokens, d, ff, PARTS)
    return call(
        left_send_kernel,
        (q, cot, acts, error),
        [HBM] * 4,
        [shape((d // 32, 8, LANES)), shape((ff, 3 * RANK), BF16), shape((3 * RANK, tokens), BF16)]
        + [shape(s, BF16) for s in halves],
        [VMEM] * 5,
        [((RANK, ff), F32), ((tokens, ff), BF16)] + [(s, BF16) for s in halves],
        2 + 4 * PARTS,
        limit=44 << 20,
    )


def left_keep_kernel(q3t_ref, p3_ref, error_ref, acts_ref, out_ref):
    for i in range(error_ref.shape[0]):
        store_left(out_ref, i, left_part(q3t_ref[...], p3_ref[...], error_ref[i], acts_ref[i]))


def left_keep(held, dims):
    return pl.pallas_call(
        left_keep_kernel,
        in_specs=[VMEM] * 4,
        out_specs=VMEM,
        out_shape=shape(dims),
        compiler_params=pltpu.CompilerParams(vmem_limit_bytes=10 << 20),
        cost_estimate=pl.CostEstimate(flops=10**6, bytes_accessed=10**5, transcendentals=0),
    )(*held)


def spread_kernel(scale, kinds, in_ref, out_ref):
    n = in_ref.shape[0]
    for kind in range(kinds):
        total = in_ref[kind]
        for i in range(kind + kinds, n, kinds):
            total = total + in_ref[i]
        if scale != 1.0:
            total = total * scale
        for i in range(kind, n, kinds):
            out_ref[i] = total


def spread(x, scale, kinds=1):
    return pl.pallas_call(
        lambda i, o: spread_kernel(scale, kinds, i, o),
        in_specs=[VMEM],
        out_specs=VMEM,
        out_shape=shape(x.shape),
        compiler_params=pltpu.CompilerParams(vmem_limit_bytes=8 << 20),
        cost_estimate=pl.CostEstimate(flops=10**6, bytes_accessed=10**5, transcendentals=0),
    )(x)


def inverse_factor(gram):
    groups = RANK // 8
    a = [gram[8 * i : 8 * i + 8] for i in range(groups)]
    row = lax.broadcasted_iota(jnp.int32, (8, RANK), 0)
    col = lax.broadcasted_iota(jnp.int32, (8, RANK), 1)
    b = [jnp.where(row + 8 * i == col, 1.0, 0.0).astype(F32) for i in range(groups)]
    scale = []
    for k in range(groups):
        cols = [
            [jnp.broadcast_to(a[i][:, 8 * k + j : 8 * k + j + 1], (8, RANK)) if i >= k else None for i in range(groups)]
            for j in range(8)
        ]
        block_scale = jnp.zeros((8, RANK), F32)
        for j in range(8):
            pivot = jnp.broadcast_to(cols[j][k][j : j + 1], (8, RANK))
            inverse = 1.0 / pivot
            block_scale = jnp.where(row == j, lax.rsqrt(pivot), block_scale)
            row_a = jnp.broadcast_to(a[k][j : j + 1], (8, RANK))
            row_b = jnp.broadcast_to(b[k][j : j + 1], (8, RANK))
            entries = [jnp.broadcast_to(cols[m][k][j : j + 1], (8, RANK)) for m in range(j + 1, 8)]
            for i in range(k, groups):
                factor = cols[j][i] * inverse
                if i == k:
                    factor = jnp.where(row > j, factor, 0.0)
                a[i] = a[i] - factor * row_a
                b[i] = b[i] - factor * row_b
                for m in range(j + 1, 8):
                    cols[m][i] = cols[m][i] - factor * entries[m - j - 1]
        scale.append(block_scale)
    return jnp.concatenate([b[i] * scale[i] for i in range(groups)], axis=0)


def half_of(tiles_ref):
    n = tiles_ref.shape[0] // 8
    return jnp.concatenate(
        [jnp.concatenate([tiles_ref[8 * j + g] for j in range(n)], axis=1) for g in range(8)], axis=0
    )


def half_terms(left, error_ref, acts_ref, ready=None):
    parts, step = error_ref.shape[:2]
    left3 = split3(left)
    gram = [sum3(dot(left3, left3[RANK * i : RANK * (i + 1)], NT)) for i in range(3)]
    with_error = with_acts = None
    for i in range(parts):
        part = left3[:, i * step : (i + 1) * step]
        if ready is not None:
            for copy in ready[i]:
                copy.wait()
        e = dot(part, error_ref[i])
        a = dot(part, acts_ref[i], NT)
        with_error = e if i == 0 else with_error + e
        with_acts = a if i == 0 else with_acts + a
    return (gram[2] + gram[1]) + gram[0], sum3(with_error), sum3(with_acts)


def first_kernel(
    mine_hbm,
    cot_hbm,
    acts_hbm,
    error_hbm,
    gram_ref,
    with_error_ref,
    with_acts_ref,
    cot_ref,
    error_other_ref,
    acts_other_ref,
    mine_ref,
    error_ref,
    acts_ref,
    sems,
):
    core = my_core()
    copies = Copies(sems)
    mine_copy = copies.start(mine_hbm, mine_ref)
    now = fetch_half(copies, core, error_hbm, acts_hbm, error_ref, acts_ref)
    later = fetch_half(copies, 1 - core, error_hbm, acts_hbm, error_other_ref, acts_other_ref)
    cot_copy = copies.start(cot_hbm, cot_ref)
    mine_copy.wait()
    gram, with_error, with_acts = half_terms(half_of(mine_ref), error_ref, acts_ref, now)
    gram_ref[...] = gram
    with_error_ref[...] = with_error
    with_acts_ref[...] = with_acts
    for pair in later:
        for copy in pair:
            copy.wait()
    cot_copy.wait()


def first(mine, cot, acts, error, parts=1):
    tokens, d = acts.shape
    ff = cot.shape[1]
    halves = half_shapes(tokens, d, ff, parts)
    return call(
        first_kernel,
        (mine, cot, acts, error),
        [HBM] * 4,
        [shape((RANK, RANK)), shape((RANK, ff)), shape((RANK, tokens)), shape((tokens, ff), BF16)]
        + [shape(s, BF16) for s in halves],
        [VMEM] * 6,
        [(mine.shape, F32)] + [(s, BF16) for s in halves],
        2 + 4 * parts,
        limit=44 << 20,
    )


def second_kernel(
    other_ref, gram_ref, with_error_ref, with_acts_ref, cot_ref, error_ref, acts_ref, factor_ref, right_ref
):
    gram, with_error, with_acts = half_terms(half_of(other_ref), error_ref, acts_ref)
    factor = inverse_factor(gram + gram_ref[...])
    factor_ref[...] = factor
    with_acts = with_acts + with_acts_ref[...]
    merged_term = (with_error + with_error_ref[...]) + sum3(dot(split3(with_acts), cot_ref[...]))
    right = dot_highest(factor, merged_term)
    tiles = right.shape[1] // LANES
    for g in range(8):
        for j in range(tiles):
            v = g * tiles + j
            right_ref[v // 4, 8 * (v % 4) : 8 * (v % 4) + 8] = right[8 * g : 8 * g + 8, LANES * j : LANES * (j + 1)]
    for v in range(8 * tiles, 64):
        right_ref[v // 4, 8 * (v % 4) : 8 * (v % 4) + 8] = jnp.zeros((8, LANES), F32)


def second(other, terms):
    return pl.pallas_call(
        second_kernel,
        in_specs=[VMEM] * 7,
        out_specs=[VMEM, VMEM],
        out_shape=[shape((RANK, RANK)), shape((16, 32, LANES))],
        compiler_params=pltpu.CompilerParams(vmem_limit_bytes=12 << 20),
        cost_estimate=pl.CostEstimate(flops=10**6, bytes_accessed=10**5, transcendentals=0),
    )(other, *terms)


def prep_kernel(factor_ref, mine_ref, other_ref, basis_ref, out_ref):
    core = my_core()
    width = mine_ref.shape[0] // 8 * LANES
    for ref, place in ((mine_ref, core), (other_ref, 1 - core)):
        at = pl.ds(pl.multiple_of(place * width, width), width)
        x = dot_highest(factor_ref[...], half_of(ref))
        basis_ref[:, at] = x
        high = x.astype(BF16)
        low = (x - high.astype(F32)).astype(BF16)
        both = jnp.concatenate([high, low], axis=0).T
        out_ref[at, : 2 * RANK] = both
        out_ref[at, 2 * RANK :] = both


def prep(factor, mine, other):
    d = 2 * (mine.shape[0] // 8 * LANES)
    return pl.pallas_call(
        prep_kernel,
        in_specs=[VMEM] * 3,
        out_specs=[VMEM, VMEM],
        out_shape=[shape((RANK, d)), shape((d, 4 * RANK), BF16)],
        compiler_params=pltpu.CompilerParams(vmem_limit_bytes=12 << 20),
        cost_estimate=pl.CostEstimate(flops=10**6, bytes_accessed=10**5, transcendentals=0),
    )(factor, mine, other)


def final_kernel(
    chunks_hbm,
    basis_hbm,
    cot_hbm,
    acts_hbm,
    error_hbm,
    out_hbm,
    q_ref,
    chunks_ref,
    q4_ref,
    basis_ref,
    cot_ref,
    acts_ref,
    error_ref,
    out_ref,
    sems,
):
    parts, step = error_ref.shape[:2]
    copies = Copies(sems)
    chunks_copy = copies.start(chunks_hbm, chunks_ref)
    cot_copy = copies.start(cot_hbm, cot_ref)
    waits = []
    for i in range(parts):
        at = slice(i * step, (i + 1) * step)
        waits.append(
            (
                copies.start(acts_hbm.at[:, at], acts_ref.at[i]),
                copies.start(error_hbm.at[at, :], error_ref.at[i]),
                copies.start(basis_hbm.at[at, :], basis_ref.at[i]),
            )
        )
    chunks_copy.wait()
    cot_copy.wait()
    for copy in waits[0]:
        copy.wait()
    tiles = q_ref.shape[1] // LANES
    for g in range(8):
        for j in range(tiles):
            v = g * tiles + j
            q_ref[8 * g : 8 * g + 8, LANES * j : LANES * (j + 1)] = chunks_ref[v // 4, 8 * (v % 4) : 8 * (v % 4) + 8]
    q = -q_ref[...]
    high = q.astype(BF16)
    low = (q - high.astype(F32)).astype(BF16)
    q4 = jnp.concatenate([high, high, low, low], axis=0)
    q4_ref[...] = q4
    stores = []
    for i in range(parts):
        if i:
            for copy in waits[i]:
                copy.wait()
        merged = dot(acts_ref[i], cot_ref[...], TN) + error_ref[i].astype(F32)
        out_ref[i] = (merged + dot(basis_ref[i], q4_ref[...] if i else q4)).astype(BF16)
        stores.append(copies.start(out_ref.at[i], out_hbm.at[i * step : (i + 1) * step, :]))
    for store in stores:
        store.wait()


def final(chunks, basis4, cot, acts, error, parts=8):
    tokens, d = acts.shape
    ff = cot.shape[1]
    step = d // parts
    return call(
        final_kernel,
        (chunks, basis4, cot, acts, error),
        [HBM] * 5,
        [shape((d, ff), BF16), shape((RANK, ff))],
        [HBM, VMEM],
        [
            (chunks.shape, F32),
            ((4 * RANK, ff), BF16),
            ((parts, step, 4 * RANK), BF16),
            ((tokens, ff), BF16),
            ((parts, tokens, step), BF16),
            ((parts, step, ff), BF16),
            ((parts, step, ff), BF16),
        ],
        2 + 4 * parts,
    )


def partial_kernel(
    cot_hbm,
    weight_hbm,
    far_send_hbm,
    near_send_hbm,
    far_keep_hbm,
    near_keep_hbm,
    cot_ref,
    weight_ref,
    out_ref,
    sems,
):
    parts, step = weight_ref.shape[:2]
    core = my_core()
    x = lax.div(lax.axis_index("tensor"), 2)
    n = cot_ref.shape[0] // 8
    copies = Copies(sems)
    waits = []
    for side, h in enumerate((1 - core, core)):
        for k, hop in enumerate((2, 1, 3, 0)):
            at = pl.multiple_of((lax.rem(x + hop, 4) * 2 + h) * n, n)
            to = (side * 4 + k) * n
            waits.append(copies.start(cot_hbm.at[pl.ds(at, n), :], cot_ref.at[to : to + n, :]))
    weight_copies = [
        copies.start(weight_hbm.at[i * step : (i + 1) * step, :], weight_ref.at[i]) for i in range(parts)
    ]
    for copy in waits:
        copy.wait()
    stores = []
    targets = ((far_send_hbm, 0, n), (near_send_hbm, n, 4 * n), (far_keep_hbm, 4 * n, 5 * n), (near_keep_hbm, 5 * n, 8 * n))
    for i in range(parts):
        weight_copies[i].wait()
        out_ref[i] = dot(cot_ref[...], weight_ref[i], NT)
        for hbm, lo, hi in targets:
            stores.append(copies.start(out_ref.at[i, lo:hi, :], hbm.at[:, i * step : (i + 1) * step]))
    for store in stores:
        store.wait()


def partials(cot, weight, parts=4):
    tokens, ff = cot.shape
    d = weight.shape[0]
    n = tokens // 8
    step = d // parts
    return call(
        partial_kernel,
        (cot, weight),
        [HBM, HBM],
        [shape((r, d)) for r in (n, 3 * n, n, 3 * n)],
        [HBM] * 4,
        [((tokens, ff), BF16), ((parts, step, ff), BF16), ((parts, tokens, step), F32)],
        8 + 5 * parts,
    )


def far_kernel(keep_hbm, got_hbm, low_hbm, high_hbm, keep_ref, got_ref, sems):
    copies = Copies(sems)
    d = keep_ref.shape[1]
    wide = low_hbm.shape[1]
    halves = (slice(0, d // 2), slice(d // 2, d))
    loads = [
        (copies.start(keep_hbm.at[:, at], keep_ref.at[:, at]), copies.start(got_hbm.at[:, at], got_ref.at[:, at]))
        for at in halves
    ]
    for at, pair in zip(halves, loads):
        for copy in pair:
            copy.wait()
        keep_ref[:, at] += got_ref[:, at]
    stores = [copies.start(keep_ref.at[:, :wide], low_hbm), copies.start(keep_ref.at[:, d - wide :], high_hbm)]
    for store in stores:
        store.wait()


def far_sums(keep, got):
    n, d = keep.shape
    return call(
        far_kernel,
        (keep, got),
        [HBM] * 2,
        [shape((n, d // 2 + LANES))] * 2,
        [HBM] * 2,
        [((n, d), F32)] * 2,
        6,
    )


def near_kernel(keep_hbm, got_hbm, plus_hbm, minus_hbm, keep_ref, got_ref, sems):
    copies = Copies(sems)
    n = plus_hbm.shape[0]
    rows = (slice(0, n), slice(n, 2 * n))
    loads = [
        (copies.start(keep_hbm.at[at, :], keep_ref.at[at, :]), copies.start(got_hbm.at[at, :], got_ref.at[at, :]))
        for at in rows
    ]
    stores = []
    for at, pair, out in zip(rows, loads, (plus_hbm, minus_hbm)):
        for copy in pair:
            copy.wait()
        keep_ref[at, :] += got_ref[at, :]
        stores.append(copies.start(keep_ref.at[at, :], out))
    for store in stores:
        store.wait()


def near_sums(keep, got, n):
    d = keep.shape[1]
    return call(
        near_kernel,
        (keep, got),
        [HBM] * 2,
        [shape((n, d))] * 2,
        [HBM] * 2,
        [((2 * n, d), F32)] * 2,
        6,
    )


def relay_kernel(plus_hbm, minus_hbm, low_ref, high_ref, plus_out, minus_out, half_ref, sems):
    copies = Copies(sems)
    d = plus_hbm.shape[1]
    w = d // 2
    wide = low_ref.shape[1]
    parts = (
        (plus_hbm, plus_out, low_ref, slice(0, w), slice(0, w)),
        (minus_hbm, minus_out, high_ref, slice(w, d), slice(wide - w, wide)),
    )
    loads = [copies.start(src.at[:, at], half_ref.at[i]) for i, (src, _, _, at, _) in enumerate(parts)]
    stores = []
    for i, (_, out, relay, at, far) in enumerate(parts):
        loads[i].wait()
        half_ref[i] += relay[:, far]
        stores.append(copies.start(half_ref.at[i], out.at[:, at]))
    for store in stores:
        store.wait()


def relay_sums(plus, minus, low, high):
    n, d = plus.shape
    return pl.pallas_call(
        relay_kernel,
        in_specs=[HBM] * 2 + [VMEM] * 2,
        out_specs=[HBM] * 2,
        out_shape=[shape((n, d))] * 2,
        input_output_aliases={0: 0, 1: 1},
        scratch_shapes=[
            pltpu.VMEM((2, n, d // 2), F32),
            pltpu.SemaphoreType.DMA((4,)),
        ],
        compiler_params=pltpu.CompilerParams(vmem_limit_bytes=52 << 20),
        cost_estimate=pl.CostEstimate(flops=10**6, bytes_accessed=10**5, transcendentals=0),
    )(plus, minus, low, high)


def close_kernel(keep_hbm, got_hbm, right_hbm, left_hbm, out_hbm, in_ref, out_ref, sems):
    copies = Copies(sems)
    n = out_ref.shape[0]
    own = slice(2 * n, 3 * n)
    loads = [
        copies.start(src, in_ref.at[i])
        for i, src in enumerate((keep_hbm.at[own, :], got_hbm.at[own, :], right_hbm, left_hbm))
    ]
    for copy in loads:
        copy.wait()
    out_ref[...] = ((in_ref[0] + in_ref[1]) + (in_ref[2] + in_ref[3])).astype(BF16)
    copies.start(out_ref, out_hbm).wait()


def close(keep, got, right, left):
    n, d = right.shape
    return call(
        close_kernel,
        (keep, got, right, left),
        [HBM] * 4,
        shape((n, d), BF16),
        HBM,
        [((4, n, d), F32), ((n, d), BF16)],
        5,
    )


def body(acts, up_cot, up_weight, error_buf, q_init):
    n_dp = lax.axis_size("dp")
    n_tensor = lax.axis_size("tensor")
    both = ("dp", "tensor")
    pairs = [(i, i ^ 1) for i in range(n_tensor)]
    right_ring = [(i, (i + 2) % n_tensor) for i in range(n_tensor)]
    left_ring = [(i, (i - 2) % n_tensor) for i in range(n_tensor)]
    error = error_buf[0]

    send, *held = left_send(q_init, up_cot, acts, error)
    received = lax.ppermute(send, "tensor", pairs)
    total = left_keep(held, send.shape) + received
    chunks = lax.all_to_all(total, both, 0, 0)

    up_weight, _ = lax.optimization_barrier((up_weight, total))
    far_send, near_send, far_keep, near_keep = partials(up_cot, up_weight)
    chunks, far_send, near_send = lax.optimization_barrier((chunks, far_send, near_send))

    spread_left = spread(chunks, 1.0, kinds=2)
    mine = lax.all_to_all(spread_left, both, 0, 0)
    far_send, near_send, _ = lax.optimization_barrier((far_send, near_send, spread_left))
    far_got = lax.ppermute(far_send, "tensor", pairs)
    near_got = lax.ppermute(near_send, "tensor", pairs)
    far_low, far_high = far_sums(far_keep, far_got)
    low_relay = lax.ppermute(far_low, "tensor", right_ring)
    high_relay = lax.ppermute(far_high, "tensor", left_ring)
    plus, minus = near_sums(near_keep, near_got, far_keep.shape[0])
    mine, _, plus = lax.optimization_barrier((mine, far_low, plus))

    other = lax.ppermute(mine, "tensor", pairs)
    terms = first(mine, up_cot, acts, error)
    factor, right = second(other, terms)

    low_relay, high_relay, right = lax.optimization_barrier((low_relay, high_relay, right))
    plus, minus = relay_sums(plus, minus, low_relay, high_relay)
    from_left = lax.ppermute(plus, "tensor", right_ring)
    from_right = lax.ppermute(minus, "tensor", left_ring)
    right_parts = lax.all_to_all(right, "dp", 0, 0)
    basis, basis4 = prep(factor, mine, other)
    right_parts, basis4 = lax.optimization_barrier((right_parts, basis4))

    spread_right = spread(right_parts, 1.0 / n_dp)
    q_chunks = lax.all_to_all(spread_right, "dp", 0, 0)
    near_keep, from_left, from_right, _ = lax.optimization_barrier((near_keep, from_left, from_right, spread_right))
    input_grad = close(near_keep, near_got, from_left, from_right)
    q_chunks, input_grad = lax.optimization_barrier((q_chunks, input_grad))
    new_error, q_factor = final(q_chunks, basis4, up_cot, acts, error)
    return (input_grad, new_error[None], basis, q_factor)


def solution(mesh):
    return jax.shard_map(
        body,
        mesh=mesh,
        in_specs=(
            P("dp", None),
            P("dp", "tensor"),
            P(None, "tensor"),
            P("dp", None, "tensor"),
            P(None, "tensor"),
        ),
        out_specs=(P(("dp", "tensor"), None), P("dp", None, "tensor"), P(), P(None, "tensor")),
        check_vma=False,
    )
```

```python
import jax
import jax.numpy as jnp
from jax import lax
from jax.experimental import pallas as pl
from jax.experimental.pallas import tpu as pltpu
from jax.sharding import PartitionSpec as P

F32 = jnp.float32
BF16 = jnp.bfloat16
HIGHEST = lax.Precision.HIGHEST
RANK = 64
LANES = 128
VMEM = pl.BlockSpec(memory_space=pltpu.VMEM)
HBM = pl.BlockSpec(memory_space=pltpu.HBM)
NN = (((1,), (0,)), ((), ()))
NT = (((1,), (1,)), ((), ()))
TN = (((0,), (0,)), ((), ()))


def shape(dims, dtype=F32):
    return jax.ShapeDtypeStruct(dims, dtype)


def call(kernel, args, specs, outs, out_specs, scratch, n_sems, limit=56 << 20):
    return pl.pallas_call(
        kernel,
        in_specs=specs,
        out_specs=out_specs,
        out_shape=outs,
        scratch_shapes=[pltpu.VMEM(dims, dtype) for dims, dtype in scratch] + [pltpu.SemaphoreType.DMA((n_sems,))],
        compiler_params=pltpu.CompilerParams(vmem_limit_bytes=limit),
        cost_estimate=pl.CostEstimate(flops=10**6, bytes_accessed=10**5, transcendentals=0),
    )(*args)


class Copies:
    def __init__(self, sems):
        self.sems = sems
        self.all = []

    def start(self, src, dst):
        copy = pltpu.make_async_copy(src, dst, self.sems.at[len(self.all)])
        copy.start()
        self.all.append(copy)
        return copy


def split3(x):
    high = x.astype(BF16)
    rest = x - high.astype(F32)
    mid = rest.astype(BF16)
    low = (rest - mid.astype(F32)).astype(BF16)
    return jnp.concatenate([high, mid, low], axis=0)


def sum3(y):
    return (y[2 * RANK : 3 * RANK] + y[RANK : 2 * RANK]) + y[:RANK]


def dot(a, b, dims=NN):
    return lax.dot_general(a, b, dims, preferred_element_type=F32)


def dot_highest(a, b):
    return lax.dot_general(a, b, NN, precision=HIGHEST, preferred_element_type=F32)


def my_core():
    return lax.rem(lax.axis_index("tensor"), 2)


def part_of(place, width, i, parts):
    step = width // parts
    return pl.ds(pl.multiple_of(place * width + i * step, step), step)


PARTS = 4


def left_part(q3t, p3, error, acts):
    y = dot(error, q3t)
    by_error = (y[:, 2 * RANK :] + y[:, RANK : 2 * RANK]) + y[:, :RANK]
    return by_error.T + sum3(dot(p3, acts))


def store_left(out_ref, i, left):
    tiles = left.shape[1] // LANES
    for j in range(tiles):
        for g in range(8):
            out_ref[8 * (i * tiles + j) + g] = left[8 * g : 8 * g + 8, LANES * j : LANES * (j + 1)]


def half_shapes(tokens, d, ff, parts):
    step = d // 2 // parts
    return [(parts, step, ff), (parts, tokens, step)]


def fetch_half(copies, place, error_hbm, acts_hbm, error_ref, acts_ref):
    width = error_hbm.shape[0] // 2
    parts = error_ref.shape[0]
    started = []
    for i in range(parts):
        at = part_of(place, width, i, parts)
        started.append(
            (copies.start(error_hbm.at[at, :], error_ref.at[i]), copies.start(acts_hbm.at[:, at], acts_ref.at[i]))
        )
    return started


def left_send_kernel(
    q_hbm,
    cot_hbm,
    acts_hbm,
    error_hbm,
    out_ref,
    q3t_ref,
    p3_ref,
    error_keep_ref,
    acts_keep_ref,
    q_ref,
    cot_ref,
    error_ref,
    acts_ref,
    sems,
):
    core = my_core()
    copies = Copies(sems)
    q_copy = copies.start(q_hbm, q_ref)
    cot_copy = copies.start(cot_hbm, cot_ref)
    now = fetch_half(copies, 1 - core, error_hbm, acts_hbm, error_ref, acts_ref)
    later = fetch_half(copies, core, error_hbm, acts_hbm, error_keep_ref, acts_keep_ref)
    q_copy.wait()
    q3 = split3(q_ref[...])
    q3t = q3.T
    q3t_ref[...] = q3t
    cot_copy.wait()
    p3 = split3(sum3(dot(q3, cot_ref[...], NT)))
    p3_ref[...] = p3
    for i, pair in enumerate(now):
        for copy in pair:
            copy.wait()
        store_left(out_ref, i, left_part(q3t, p3, error_ref[i], acts_ref[i]))
    for pair in later:
        for copy in pair:
            copy.wait()


def left_send(q, cot, acts, error):
    tokens, d = acts.shape
    ff = cot.shape[1]
    halves = half_shapes(tokens, d, ff, PARTS)
    return call(
        left_send_kernel,
        (q, cot, acts, error),
        [HBM] * 4,
        [shape((d // 32, 8, LANES)), shape((ff, 3 * RANK), BF16), shape((3 * RANK, tokens), BF16)]
        + [shape(s, BF16) for s in halves],
        [VMEM] * 5,
        [((RANK, ff), F32), ((tokens, ff), BF16)] + [(s, BF16) for s in halves],
        2 + 4 * PARTS,
        limit=44 << 20,
    )


def left_keep_kernel(q3t_ref, p3_ref, error_ref, acts_ref, out_ref):
    for i in range(error_ref.shape[0]):
        store_left(out_ref, i, left_part(q3t_ref[...], p3_ref[...], error_ref[i], acts_ref[i]))


def left_keep(held, dims):
    return pl.pallas_call(
        left_keep_kernel,
        in_specs=[VMEM] * 4,
        out_specs=VMEM,
        out_shape=shape(dims),
        compiler_params=pltpu.CompilerParams(vmem_limit_bytes=10 << 20),
        cost_estimate=pl.CostEstimate(flops=10**6, bytes_accessed=10**5, transcendentals=0),
    )(*held)


def spread_kernel(scale, kinds, in_ref, out_ref):
    n = in_ref.shape[0]
    for kind in range(kinds):
        total = in_ref[kind]
        for i in range(kind + kinds, n, kinds):
            total = total + in_ref[i]
        if scale != 1.0:
            total = total * scale
        for i in range(kind, n, kinds):
            out_ref[i] = total


def spread(x, scale, kinds=1):
    return pl.pallas_call(
        lambda i, o: spread_kernel(scale, kinds, i, o),
        in_specs=[VMEM],
        out_specs=VMEM,
        out_shape=shape(x.shape),
        compiler_params=pltpu.CompilerParams(vmem_limit_bytes=8 << 20),
        cost_estimate=pl.CostEstimate(flops=10**6, bytes_accessed=10**5, transcendentals=0),
    )(x)


def inverse_factor(gram):
    groups = RANK // 8
    a = [gram[8 * i : 8 * i + 8] for i in range(groups)]
    row = lax.broadcasted_iota(jnp.int32, (8, RANK), 0)
    col = lax.broadcasted_iota(jnp.int32, (8, RANK), 1)
    b = [jnp.where(row + 8 * i == col, 1.0, 0.0).astype(F32) for i in range(groups)]
    scale = []
    for k in range(groups):
        cols = [
            [jnp.broadcast_to(a[i][:, 8 * k + j : 8 * k + j + 1], (8, RANK)) if i >= k else None for i in range(groups)]
            for j in range(8)
        ]
        block_scale = jnp.zeros((8, RANK), F32)
        for j in range(8):
            pivot = jnp.broadcast_to(cols[j][k][j : j + 1], (8, RANK))
            inverse = 1.0 / pivot
            block_scale = jnp.where(row == j, lax.rsqrt(pivot), block_scale)
            row_a = jnp.broadcast_to(a[k][j : j + 1], (8, RANK))
            row_b = jnp.broadcast_to(b[k][j : j + 1], (8, RANK))
            entries = [jnp.broadcast_to(cols[m][k][j : j + 1], (8, RANK)) for m in range(j + 1, 8)]
            for i in range(k, groups):
                factor = cols[j][i] * inverse
                if i == k:
                    factor = jnp.where(row > j, factor, 0.0)
                a[i] = a[i] - factor * row_a
                b[i] = b[i] - factor * row_b
                for m in range(j + 1, 8):
                    cols[m][i] = cols[m][i] - factor * entries[m - j - 1]
        scale.append(block_scale)
    return jnp.concatenate([b[i] * scale[i] for i in range(groups)], axis=0)


def half_of(tiles_ref):
    n = tiles_ref.shape[0] // 8
    return jnp.concatenate(
        [jnp.concatenate([tiles_ref[8 * j + g] for j in range(n)], axis=1) for g in range(8)], axis=0
    )


def half_terms(left, error_ref, acts_ref, ready=None):
    parts, step = error_ref.shape[:2]
    left3 = split3(left)
    gram = [sum3(dot(left3, left3[RANK * i : RANK * (i + 1)], NT)) for i in range(3)]
    with_error = with_acts = None
    for i in range(parts):
        part = left3[:, i * step : (i + 1) * step]
        if ready is not None:
            for copy in ready[i]:
                copy.wait()
        e = dot(part, error_ref[i])
        a = dot(part, acts_ref[i], NT)
        with_error = e if i == 0 else with_error + e
        with_acts = a if i == 0 else with_acts + a
    return (gram[2] + gram[1]) + gram[0], sum3(with_error), sum3(with_acts)


def first_kernel(
    mine_hbm,
    cot_hbm,
    acts_hbm,
    error_hbm,
    gram_ref,
    with_error_ref,
    with_acts_ref,
    cot_ref,
    error_other_ref,
    acts_other_ref,
    mine_ref,
    error_ref,
    acts_ref,
    sems,
):
    core = my_core()
    copies = Copies(sems)
    mine_copy = copies.start(mine_hbm, mine_ref)
    now = fetch_half(copies, core, error_hbm, acts_hbm, error_ref, acts_ref)
    later = fetch_half(copies, 1 - core, error_hbm, acts_hbm, error_other_ref, acts_other_ref)
    cot_copy = copies.start(cot_hbm, cot_ref)
    mine_copy.wait()
    gram, with_error, with_acts = half_terms(half_of(mine_ref), error_ref, acts_ref, now)
    gram_ref[...] = gram
    with_error_ref[...] = with_error
    with_acts_ref[...] = with_acts
    for pair in later:
        for copy in pair:
            copy.wait()
    cot_copy.wait()


def first(mine, cot, acts, error, parts=1):
    tokens, d = acts.shape
    ff = cot.shape[1]
    halves = half_shapes(tokens, d, ff, parts)
    return call(
        first_kernel,
        (mine, cot, acts, error),
        [HBM] * 4,
        [shape((RANK, RANK)), shape((RANK, ff)), shape((RANK, tokens)), shape((tokens, ff), BF16)]
        + [shape(s, BF16) for s in halves],
        [VMEM] * 6,
        [(mine.shape, F32)] + [(s, BF16) for s in halves],
        2 + 4 * parts,
        limit=44 << 20,
    )


def second_kernel(
    other_ref, gram_ref, with_error_ref, with_acts_ref, cot_ref, error_ref, acts_ref, factor_ref, right_ref
):
    gram, with_error, with_acts = half_terms(half_of(other_ref), error_ref, acts_ref)
    factor = inverse_factor(gram + gram_ref[...])
    factor_ref[...] = factor
    with_acts = with_acts + with_acts_ref[...]
    merged_term = (with_error + with_error_ref[...]) + sum3(dot(split3(with_acts), cot_ref[...]))
    right = dot_highest(factor, merged_term)
    tiles = right.shape[1] // LANES
    for g in range(8):
        for j in range(tiles):
            v = g * tiles + j
            right_ref[v // 4, 8 * (v % 4) : 8 * (v % 4) + 8] = right[8 * g : 8 * g + 8, LANES * j : LANES * (j + 1)]
    for v in range(8 * tiles, 64):
        right_ref[v // 4, 8 * (v % 4) : 8 * (v % 4) + 8] = jnp.zeros((8, LANES), F32)


def second(other, terms):
    return pl.pallas_call(
        second_kernel,
        in_specs=[VMEM] * 7,
        out_specs=[VMEM, VMEM],
        out_shape=[shape((RANK, RANK)), shape((16, 32, LANES))],
        compiler_params=pltpu.CompilerParams(vmem_limit_bytes=12 << 20),
        cost_estimate=pl.CostEstimate(flops=10**6, bytes_accessed=10**5, transcendentals=0),
    )(other, *terms)


def prep_kernel(factor_ref, mine_ref, other_ref, basis_ref, out_ref):
    core = my_core()
    width = mine_ref.shape[0] // 8 * LANES
    for ref, place in ((mine_ref, core), (other_ref, 1 - core)):
        at = pl.ds(pl.multiple_of(place * width, width), width)
        x = dot_highest(factor_ref[...], half_of(ref))
        basis_ref[:, at] = x
        high = x.astype(BF16)
        low = (x - high.astype(F32)).astype(BF16)
        both = jnp.concatenate([high, low], axis=0).T
        out_ref[at, : 2 * RANK] = both
        out_ref[at, 2 * RANK :] = both


def prep(factor, mine, other):
    d = 2 * (mine.shape[0] // 8 * LANES)
    return pl.pallas_call(
        prep_kernel,
        in_specs=[VMEM] * 3,
        out_specs=[VMEM, VMEM],
        out_shape=[shape((RANK, d)), shape((d, 4 * RANK), BF16)],
        compiler_params=pltpu.CompilerParams(vmem_limit_bytes=12 << 20),
        cost_estimate=pl.CostEstimate(flops=10**6, bytes_accessed=10**5, transcendentals=0),
    )(factor, mine, other)


def final_kernel(
    chunks_hbm,
    basis_hbm,
    cot_hbm,
    acts_hbm,
    error_hbm,
    keep_hbm,
    got_hbm,
    left_hbm,
    right_hbm,
    out_hbm,
    q_ref,
    input_grad_hbm,
    chunks_ref,
    q4_ref,
    basis_ref,
    cot_ref,
    acts_ref,
    error_ref,
    out_ref,
    sums_ref,
    input_grad_ref,
    sems,
):
    parts, step = error_ref.shape[:2]
    copies = Copies(sems)
    chunks_copy = copies.start(chunks_hbm, chunks_ref)
    cot_copy = copies.start(cot_hbm, cot_ref)
    waits = []
    for i in range(parts):
        at = slice(i * step, (i + 1) * step)
        waits.append(
            (
                copies.start(acts_hbm.at[:, at], acts_ref.at[i]),
                copies.start(error_hbm.at[at, :], error_ref.at[i]),
                copies.start(basis_hbm.at[at, :], basis_ref.at[i]),
            )
        )
    n = input_grad_ref.shape[0]
    own = slice(2 * n, 3 * n)
    sums = [
        copies.start(src, sums_ref.at[i])
        for i, src in enumerate((keep_hbm.at[own, :], got_hbm.at[own, :], left_hbm, right_hbm))
    ]
    chunks_copy.wait()
    cot_copy.wait()
    for copy in waits[0]:
        copy.wait()
    tiles = q_ref.shape[1] // LANES
    for g in range(8):
        for j in range(tiles):
            v = g * tiles + j
            q_ref[8 * g : 8 * g + 8, LANES * j : LANES * (j + 1)] = chunks_ref[v // 4, 8 * (v % 4) : 8 * (v % 4) + 8]
    q = -q_ref[...]
    high = q.astype(BF16)
    low = (q - high.astype(F32)).astype(BF16)
    q4 = jnp.concatenate([high, high, low, low], axis=0)
    q4_ref[...] = q4
    stores = []
    for i in range(parts):
        if i:
            for copy in waits[i]:
                copy.wait()
        merged = dot(acts_ref[i], cot_ref[...], TN) + error_ref[i].astype(F32)
        out_ref[i] = (merged + dot(basis_ref[i], q4_ref[...] if i else q4)).astype(BF16)
        stores.append(copies.start(out_ref.at[i], out_hbm.at[i * step : (i + 1) * step, :]))
        if i == parts - 2:
            for copy in sums:
                copy.wait()
            total = (sums_ref[0] + sums_ref[1]) + (sums_ref[2] + sums_ref[3])
            input_grad_ref[...] = total.astype(BF16)
            stores.append(copies.start(input_grad_ref, input_grad_hbm))
    for store in stores:
        store.wait()


def final(chunks, basis4, cot, acts, error, keep, got, from_left, from_right, parts=8):
    tokens, d = acts.shape
    ff = cot.shape[1]
    step = d // parts
    return call(
        final_kernel,
        (chunks, basis4, cot, acts, error, keep, got, from_left, from_right),
        [HBM] * 9,
        [shape((d, ff), BF16), shape((RANK, ff)), shape(from_left.shape, BF16)],
        [HBM, VMEM, HBM],
        [
            (chunks.shape, F32),
            ((4 * RANK, ff), BF16),
            ((parts, step, 4 * RANK), BF16),
            ((tokens, ff), BF16),
            ((parts, tokens, step), BF16),
            ((parts, step, ff), BF16),
            ((parts, step, ff), BF16),
            ((4,) + from_left.shape, F32),
            (from_left.shape, BF16),
        ],
        7 + 4 * parts,
        limit=52 << 20,
    )


def partial_kernel(
    cot_hbm,
    weight_hbm,
    far_send_hbm,
    near_send_hbm,
    far_keep_hbm,
    near_keep_hbm,
    cot_ref,
    weight_ref,
    out_ref,
    sems,
):
    parts, step = weight_ref.shape[:2]
    core = my_core()
    x = lax.div(lax.axis_index("tensor"), 2)
    n = cot_ref.shape[0] // 8
    copies = Copies(sems)
    waits = []
    for side, h in enumerate((1 - core, core)):
        for k, hop in enumerate((2, 1, 3, 0)):
            at = pl.multiple_of((lax.rem(x + hop, 4) * 2 + h) * n, n)
            to = (side * 4 + k) * n
            waits.append(copies.start(cot_hbm.at[pl.ds(at, n), :], cot_ref.at[to : to + n, :]))
    weight_copies = [
        copies.start(weight_hbm.at[i * step : (i + 1) * step, :], weight_ref.at[i]) for i in range(parts)
    ]
    for copy in waits:
        copy.wait()
    stores = []
    targets = ((far_send_hbm, 0, n), (near_send_hbm, n, 4 * n), (far_keep_hbm, 4 * n, 5 * n), (near_keep_hbm, 5 * n, 8 * n))
    for i in range(parts):
        weight_copies[i].wait()
        out_ref[i] = dot(cot_ref[...], weight_ref[i], NT)
        for hbm, lo, hi in targets:
            stores.append(copies.start(out_ref.at[i, lo:hi, :], hbm.at[:, i * step : (i + 1) * step]))
    for store in stores:
        store.wait()


def partials(cot, weight, parts=4):
    tokens, ff = cot.shape
    d = weight.shape[0]
    n = tokens // 8
    step = d // parts
    return call(
        partial_kernel,
        (cot, weight),
        [HBM, HBM],
        [shape((r, d)) for r in (n, 3 * n, n, 3 * n)],
        [HBM] * 4,
        [((tokens, ff), BF16), ((parts, step, ff), BF16), ((parts, tokens, step), F32)],
        8 + 5 * parts,
    )


def far_kernel(keep_hbm, got_hbm, low_hbm, high_hbm, keep_ref, got_ref, sems):
    copies = Copies(sems)
    d = keep_ref.shape[1]
    wide = low_hbm.shape[1]
    halves = (slice(0, d // 2), slice(d // 2, d))
    loads = [
        (copies.start(keep_hbm.at[:, at], keep_ref.at[:, at]), copies.start(got_hbm.at[:, at], got_ref.at[:, at]))
        for at in halves
    ]
    for at, pair in zip(halves, loads):
        for copy in pair:
            copy.wait()
        keep_ref[:, at] += got_ref[:, at]
    stores = [copies.start(keep_ref.at[:, :wide], low_hbm), copies.start(keep_ref.at[:, d - wide :], high_hbm)]
    for store in stores:
        store.wait()


def far_sums(keep, got):
    n, d = keep.shape
    return call(
        far_kernel,
        (keep, got),
        [HBM] * 2,
        [shape((n, d // 2 + LANES))] * 2,
        [HBM] * 2,
        [((n, d), F32)] * 2,
        6,
    )


def near_kernel(keep_hbm, got_hbm, plus_hbm, minus_hbm, keep_ref, got_ref, sems):
    copies = Copies(sems)
    n = plus_hbm.shape[0]
    rows = (slice(0, n), slice(n, 2 * n))
    loads = [
        (copies.start(keep_hbm.at[at, :], keep_ref.at[at, :]), copies.start(got_hbm.at[at, :], got_ref.at[at, :]))
        for at in rows
    ]
    stores = []
    for at, pair, out in zip(rows, loads, (plus_hbm, minus_hbm)):
        for copy in pair:
            copy.wait()
        keep_ref[at, :] += got_ref[at, :]
        stores.append(copies.start(keep_ref.at[at, :], out))
    for store in stores:
        store.wait()


def near_sums(keep, got, n):
    d = keep.shape[1]
    return call(
        near_kernel,
        (keep, got),
        [HBM] * 2,
        [shape((n, d))] * 2,
        [HBM] * 2,
        [((2 * n, d), F32)] * 2,
        6,
    )


def relay_kernel(plus_hbm, minus_hbm, low_ref, high_ref, plus_out, minus_out, half_ref, sems):
    copies = Copies(sems)
    d = plus_hbm.shape[1]
    w = d // 2
    wide = low_ref.shape[1]
    parts = (
        (plus_hbm, plus_out, low_ref, slice(0, w), slice(0, w)),
        (minus_hbm, minus_out, high_ref, slice(w, d), slice(wide - w, wide)),
    )
    loads = [copies.start(src.at[:, at], half_ref.at[i]) for i, (src, _, _, at, _) in enumerate(parts)]
    stores = []
    for i, (_, out, relay, at, far) in enumerate(parts):
        loads[i].wait()
        half_ref[i] += relay[:, far]
        stores.append(copies.start(half_ref.at[i], out.at[:, at]))
    for store in stores:
        store.wait()


def relay_sums(plus, minus, low, high):
    n, d = plus.shape
    return pl.pallas_call(
        relay_kernel,
        in_specs=[HBM] * 2 + [VMEM] * 2,
        out_specs=[HBM] * 2,
        out_shape=[shape((n, d))] * 2,
        input_output_aliases={0: 0, 1: 1},
        scratch_shapes=[
            pltpu.VMEM((2, n, d // 2), F32),
            pltpu.SemaphoreType.DMA((4,)),
        ],
        compiler_params=pltpu.CompilerParams(vmem_limit_bytes=52 << 20),
        cost_estimate=pl.CostEstimate(flops=10**6, bytes_accessed=10**5, transcendentals=0),
    )(plus, minus, low, high)


def body(acts, up_cot, up_weight, error_buf, q_init):
    n_dp = lax.axis_size("dp")
    n_tensor = lax.axis_size("tensor")
    both = ("dp", "tensor")
    pairs = [(i, i ^ 1) for i in range(n_tensor)]
    right_ring = [(i, (i + 2) % n_tensor) for i in range(n_tensor)]
    left_ring = [(i, (i - 2) % n_tensor) for i in range(n_tensor)]
    error = error_buf[0]

    send, *held = left_send(q_init, up_cot, acts, error)
    received = lax.ppermute(send, "tensor", pairs)
    total = left_keep(held, send.shape) + received
    chunks = lax.all_to_all(total, both, 0, 0)

    up_weight, _ = lax.optimization_barrier((up_weight, total))
    far_send, near_send, far_keep, near_keep = partials(up_cot, up_weight)
    chunks, far_send, near_send = lax.optimization_barrier((chunks, far_send, near_send))

    spread_left = spread(chunks, 1.0, kinds=2)
    mine = lax.all_to_all(spread_left, both, 0, 0)
    far_send, near_send, _ = lax.optimization_barrier((far_send, near_send, spread_left))
    far_got = lax.ppermute(far_send, "tensor", pairs)
    near_got = lax.ppermute(near_send, "tensor", pairs)
    far_low, far_high = far_sums(far_keep, far_got)
    low_relay = lax.ppermute(far_low, "tensor", right_ring)
    high_relay = lax.ppermute(far_high, "tensor", left_ring)
    plus, minus = near_sums(near_keep, near_got, far_keep.shape[0])
    mine, _, plus = lax.optimization_barrier((mine, far_low, plus))

    other = lax.ppermute(mine, "tensor", pairs)
    terms = first(mine, up_cot, acts, error)
    factor, right = second(other, terms)

    low_relay, high_relay, right = lax.optimization_barrier((low_relay, high_relay, right))
    plus, minus = relay_sums(plus, minus, low_relay, high_relay)
    from_left = lax.ppermute(plus, "tensor", right_ring)
    from_right = lax.ppermute(minus, "tensor", left_ring)
    right_parts = lax.all_to_all(right, "dp", 0, 0)
    basis, basis4 = prep(factor, mine, other)
    right_parts, basis4 = lax.optimization_barrier((right_parts, basis4))

    q_chunks = lax.all_to_all(spread(right_parts, 1.0 / n_dp), "dp", 0, 0)
    new_error, q_factor, input_grad = final(
        q_chunks, basis4, up_cot, acts, error, near_keep, near_got, from_left, from_right
    )
    return (input_grad, new_error[None], basis, q_factor)


def solution(mesh):
    return jax.shard_map(
        body,
        mesh=mesh,
        in_specs=(
            P("dp", None),
            P("dp", "tensor"),
            P(None, "tensor"),
            P("dp", None, "tensor"),
            P(None, "tensor"),
        ),
        out_specs=(P(("dp", "tensor"), None), P("dp", None, "tensor"), P(), P(None, "tensor")),
        check_vma=False,
    )
```

```python
import jax
import jax.numpy as jnp
from jax import lax
from jax.experimental import pallas as pl
from jax.experimental.pallas import tpu as pltpu
from jax.sharding import PartitionSpec as P

F32 = jnp.float32
BF16 = jnp.bfloat16
HIGHEST = lax.Precision.HIGHEST
RANK = 64
LANES = 128
VMEM = pl.BlockSpec(memory_space=pltpu.VMEM)
HBM = pl.BlockSpec(memory_space=pltpu.HBM)
NN = (((1,), (0,)), ((), ()))
NT = (((1,), (1,)), ((), ()))
TN = (((0,), (0,)), ((), ()))


def shape(dims, dtype=F32):
    return jax.ShapeDtypeStruct(dims, dtype)


def call(kernel, args, specs, outs, out_specs, scratch, n_sems, limit=56 << 20):
    return pl.pallas_call(
        kernel,
        in_specs=specs,
        out_specs=out_specs,
        out_shape=outs,
        scratch_shapes=[pltpu.VMEM(dims, dtype) for dims, dtype in scratch] + [pltpu.SemaphoreType.DMA((n_sems,))],
        compiler_params=pltpu.CompilerParams(vmem_limit_bytes=limit),
        cost_estimate=pl.CostEstimate(flops=10**6, bytes_accessed=10**5, transcendentals=0),
    )(*args)


class Copies:
    def __init__(self, sems):
        self.sems = sems
        self.all = []

    def start(self, src, dst):
        copy = pltpu.make_async_copy(src, dst, self.sems.at[len(self.all)])
        copy.start()
        self.all.append(copy)
        return copy


def split3(x):
    high = x.astype(BF16)
    rest = x - high.astype(F32)
    mid = rest.astype(BF16)
    low = (rest - mid.astype(F32)).astype(BF16)
    return jnp.concatenate([high, mid, low], axis=0)


def sum3(y):
    return (y[2 * RANK : 3 * RANK] + y[RANK : 2 * RANK]) + y[:RANK]


def dot(a, b, dims=NN):
    return lax.dot_general(a, b, dims, preferred_element_type=F32)


def dot_highest(a, b):
    return lax.dot_general(a, b, NN, precision=HIGHEST, preferred_element_type=F32)


def my_core():
    return lax.rem(lax.axis_index("tensor"), 2)


def part_of(place, width, i, parts):
    step = width // parts
    return pl.ds(pl.multiple_of(place * width + i * step, step), step)


PARTS = 4


def left_part(q3t, p3, error, acts):
    y = dot(error, q3t)
    by_error = (y[:, 2 * RANK :] + y[:, RANK : 2 * RANK]) + y[:, :RANK]
    return by_error.T + sum3(dot(p3, acts))


def store_left(out_ref, i, left):
    tiles = left.shape[1] // LANES
    for j in range(tiles):
        for g in range(8):
            out_ref[8 * (i * tiles + j) + g] = left[8 * g : 8 * g + 8, LANES * j : LANES * (j + 1)]


def half_shapes(tokens, d, ff, parts):
    step = d // 2 // parts
    return [(parts, step, ff), (parts, tokens, step)]


def fetch_half(copies, place, error_hbm, acts_hbm, error_ref, acts_ref):
    width = error_hbm.shape[0] // 2
    parts = error_ref.shape[0]
    started = []
    for i in range(parts):
        at = part_of(place, width, i, parts)
        started.append(
            (copies.start(error_hbm.at[at, :], error_ref.at[i]), copies.start(acts_hbm.at[:, at], acts_ref.at[i]))
        )
    return started


def left_send_kernel(
    q_hbm,
    cot_hbm,
    acts_hbm,
    error_hbm,
    out_ref,
    q3t_ref,
    p3_ref,
    error_keep_ref,
    acts_keep_ref,
    q_ref,
    cot_ref,
    error_ref,
    acts_ref,
    sems,
):
    core = my_core()
    copies = Copies(sems)
    q_copy = copies.start(q_hbm, q_ref)
    cot_copy = copies.start(cot_hbm, cot_ref)
    now = fetch_half(copies, 1 - core, error_hbm, acts_hbm, error_ref, acts_ref)
    later = fetch_half(copies, core, error_hbm, acts_hbm, error_keep_ref, acts_keep_ref)
    q_copy.wait()
    q3 = split3(q_ref[...])
    q3t = q3.T
    q3t_ref[...] = q3t
    cot_copy.wait()
    p3 = split3(sum3(dot(q3, cot_ref[...], NT)))
    p3_ref[...] = p3
    for i, pair in enumerate(now):
        for copy in pair:
            copy.wait()
        store_left(out_ref, i, left_part(q3t, p3, error_ref[i], acts_ref[i]))
    for pair in later:
        for copy in pair:
            copy.wait()


def left_send(q, cot, acts, error):
    tokens, d = acts.shape
    ff = cot.shape[1]
    halves = half_shapes(tokens, d, ff, PARTS)
    return call(
        left_send_kernel,
        (q, cot, acts, error),
        [HBM] * 4,
        [shape((d // 32, 8, LANES)), shape((ff, 3 * RANK), BF16), shape((3 * RANK, tokens), BF16)]
        + [shape(s, BF16) for s in halves],
        [VMEM] * 5,
        [((RANK, ff), F32), ((tokens, ff), BF16)] + [(s, BF16) for s in halves],
        2 + 4 * PARTS,
        limit=44 << 20,
    )


def left_keep_kernel(q3t_ref, p3_ref, error_ref, acts_ref, out_ref):
    for i in range(error_ref.shape[0]):
        store_left(out_ref, i, left_part(q3t_ref[...], p3_ref[...], error_ref[i], acts_ref[i]))


def left_keep(held, dims):
    return pl.pallas_call(
        left_keep_kernel,
        in_specs=[VMEM] * 4,
        out_specs=VMEM,
        out_shape=shape(dims),
        compiler_params=pltpu.CompilerParams(vmem_limit_bytes=10 << 20),
        cost_estimate=pl.CostEstimate(flops=10**6, bytes_accessed=10**5, transcendentals=0),
    )(*held)


def spread_kernel(scale, kinds, in_ref, out_ref):
    n = in_ref.shape[0]
    for kind in range(kinds):
        total = in_ref[kind]
        for i in range(kind + kinds, n, kinds):
            total = total + in_ref[i]
        if scale != 1.0:
            total = total * scale
        for i in range(kind, n, kinds):
            out_ref[i] = total


def spread(x, scale, kinds=1):
    return pl.pallas_call(
        lambda i, o: spread_kernel(scale, kinds, i, o),
        in_specs=[VMEM],
        out_specs=VMEM,
        out_shape=shape(x.shape),
        compiler_params=pltpu.CompilerParams(vmem_limit_bytes=8 << 20),
        cost_estimate=pl.CostEstimate(flops=10**6, bytes_accessed=10**5, transcendentals=0),
    )(x)


def inverse_factor(gram):
    groups = RANK // 8
    a = [gram[8 * i : 8 * i + 8] for i in range(groups)]
    row = lax.broadcasted_iota(jnp.int32, (8, RANK), 0)
    col = lax.broadcasted_iota(jnp.int32, (8, RANK), 1)
    b = [jnp.where(row + 8 * i == col, 1.0, 0.0).astype(F32) for i in range(groups)]
    scale = []
    for k in range(groups):
        cols = [
            [jnp.broadcast_to(a[i][:, 8 * k + j : 8 * k + j + 1], (8, RANK)) if i >= k else None for i in range(groups)]
            for j in range(8)
        ]
        block_scale = jnp.zeros((8, RANK), F32)
        for j in range(8):
            pivot = jnp.broadcast_to(cols[j][k][j : j + 1], (8, RANK))
            inverse = 1.0 / pivot
            block_scale = jnp.where(row == j, lax.rsqrt(pivot), block_scale)
            row_a = jnp.broadcast_to(a[k][j : j + 1], (8, RANK))
            row_b = jnp.broadcast_to(b[k][j : j + 1], (8, RANK))
            entries = [jnp.broadcast_to(cols[m][k][j : j + 1], (8, RANK)) for m in range(j + 1, 8)]
            for i in range(k, groups):
                factor = cols[j][i] * inverse
                if i == k:
                    factor = jnp.where(row > j, factor, 0.0)
                a[i] = a[i] - factor * row_a
                b[i] = b[i] - factor * row_b
                for m in range(j + 1, 8):
                    cols[m][i] = cols[m][i] - factor * entries[m - j - 1]
        scale.append(block_scale)
    return jnp.concatenate([b[i] * scale[i] for i in range(groups)], axis=0)


def half_of(tiles_ref):
    n = tiles_ref.shape[0] // 8
    return jnp.concatenate(
        [jnp.concatenate([tiles_ref[8 * j + g] for j in range(n)], axis=1) for g in range(8)], axis=0
    )


def half_terms(left, error_ref, acts_ref, ready=None):
    parts, step = error_ref.shape[:2]
    left3 = split3(left)
    gram = [sum3(dot(left3, left3[RANK * i : RANK * (i + 1)], NT)) for i in range(3)]
    with_error = with_acts = None
    for i in range(parts):
        part = left3[:, i * step : (i + 1) * step]
        if ready is not None:
            for copy in ready[i]:
                copy.wait()
        e = dot(part, error_ref[i])
        a = dot(part, acts_ref[i], NT)
        with_error = e if i == 0 else with_error + e
        with_acts = a if i == 0 else with_acts + a
    return (gram[2] + gram[1]) + gram[0], sum3(with_error), sum3(with_acts)


def first_kernel(
    mine_hbm,
    cot_hbm,
    acts_hbm,
    error_hbm,
    gram_ref,
    with_error_ref,
    with_acts_ref,
    cot_ref,
    error_other_ref,
    acts_other_ref,
    mine_ref,
    error_ref,
    acts_ref,
    sems,
):
    core = my_core()
    copies = Copies(sems)
    mine_copy = copies.start(mine_hbm, mine_ref)
    now = fetch_half(copies, core, error_hbm, acts_hbm, error_ref, acts_ref)
    later = fetch_half(copies, 1 - core, error_hbm, acts_hbm, error_other_ref, acts_other_ref)
    cot_copy = copies.start(cot_hbm, cot_ref)
    mine_copy.wait()
    gram, with_error, with_acts = half_terms(half_of(mine_ref), error_ref, acts_ref, now)
    gram_ref[...] = gram
    with_error_ref[...] = with_error
    with_acts_ref[...] = with_acts
    for pair in later:
        for copy in pair:
            copy.wait()
    cot_copy.wait()


def first(mine, cot, acts, error, parts=1):
    tokens, d = acts.shape
    ff = cot.shape[1]
    halves = half_shapes(tokens, d, ff, parts)
    return call(
        first_kernel,
        (mine, cot, acts, error),
        [HBM] * 4,
        [shape((RANK, RANK)), shape((RANK, ff)), shape((RANK, tokens)), shape((tokens, ff), BF16)]
        + [shape(s, BF16) for s in halves],
        [VMEM] * 6,
        [(mine.shape, F32)] + [(s, BF16) for s in halves],
        2 + 4 * parts,
        limit=44 << 20,
    )


def second_kernel(
    other_ref,
    gram_ref,
    with_error_ref,
    with_acts_ref,
    cot_ref,
    error_ref,
    acts_ref,
    low_hbm,
    high_hbm,
    plus_hbm,
    minus_hbm,
    factor_ref,
    right_ref,
    plus_out,
    minus_out,
    half_ref,
    relay_ref,
    sems,
):
    copies = Copies(sems)
    w = half_ref.shape[2]
    wide = low_hbm.shape[1]
    relays = (
        (plus_hbm, plus_out, low_hbm, slice(0, w), slice(0, w)),
        (minus_hbm, minus_out, high_hbm, slice(w, 2 * w), slice(wide - w, wide)),
    )
    loads = [
        (copies.start(src.at[:, at], half_ref.at[i]), copies.start(relay, relay_ref.at[i]))
        for i, (src, _, relay, at, _) in enumerate(relays)
    ]

    gram, with_error, with_acts = half_terms(half_of(other_ref), error_ref, acts_ref)
    factor = inverse_factor(gram + gram_ref[...])
    factor_ref[...] = factor

    stores = []
    for i, (_, out, _, at, far) in enumerate(relays):
        for copy in loads[i]:
            copy.wait()
        half_ref[i] += relay_ref[i, :, far]
        stores.append(copies.start(half_ref.at[i], out.at[:, at]))

    with_acts = with_acts + with_acts_ref[...]
    merged_term = (with_error + with_error_ref[...]) + sum3(dot(split3(with_acts), cot_ref[...]))
    right = dot_highest(factor, merged_term)
    tiles = right.shape[1] // LANES
    for g in range(8):
        for j in range(tiles):
            v = g * tiles + j
            right_ref[v // 4, 8 * (v % 4) : 8 * (v % 4) + 8] = right[8 * g : 8 * g + 8, LANES * j : LANES * (j + 1)]
    for v in range(8 * tiles, 64):
        right_ref[v // 4, 8 * (v % 4) : 8 * (v % 4) + 8] = jnp.zeros((8, LANES), F32)
    for store in stores:
        store.wait()


def second(other, terms, low, high, plus, minus):
    n, d = plus.shape
    return pl.pallas_call(
        second_kernel,
        in_specs=[VMEM] * 7 + [HBM] * 4,
        out_specs=[VMEM, VMEM, HBM, HBM],
        out_shape=[shape((RANK, RANK)), shape((16, 32, LANES)), shape((n, d)), shape((n, d))],
        input_output_aliases={9: 2, 10: 3},
        scratch_shapes=[
            pltpu.VMEM((2, n, d // 2), F32),
            pltpu.VMEM((2,) + low.shape, F32),
            pltpu.SemaphoreType.DMA((6,)),
        ],
        compiler_params=pltpu.CompilerParams(vmem_limit_bytes=12 << 20),
        cost_estimate=pl.CostEstimate(flops=10**6, bytes_accessed=10**5, transcendentals=0),
    )(other, *terms, low, high, plus, minus)


def prep_kernel(factor_ref, mine_ref, other_ref, basis_ref, out_ref):
    core = my_core()
    width = mine_ref.shape[0] // 8 * LANES
    for ref, place in ((mine_ref, core), (other_ref, 1 - core)):
        at = pl.ds(pl.multiple_of(place * width, width), width)
        x = dot_highest(factor_ref[...], half_of(ref))
        basis_ref[:, at] = x
        high = x.astype(BF16)
        low = (x - high.astype(F32)).astype(BF16)
        both = jnp.concatenate([high, low], axis=0).T
        out_ref[at, : 2 * RANK] = both
        out_ref[at, 2 * RANK :] = both


def prep(factor, mine, other):
    d = 2 * (mine.shape[0] // 8 * LANES)
    return pl.pallas_call(
        prep_kernel,
        in_specs=[VMEM] * 3,
        out_specs=[VMEM, VMEM],
        out_shape=[shape((RANK, d)), shape((d, 4 * RANK), BF16)],
        compiler_params=pltpu.CompilerParams(vmem_limit_bytes=12 << 20),
        cost_estimate=pl.CostEstimate(flops=10**6, bytes_accessed=10**5, transcendentals=0),
    )(factor, mine, other)


def final_kernel(
    chunks_hbm,
    basis_hbm,
    cot_hbm,
    acts_hbm,
    error_hbm,
    keep_hbm,
    got_hbm,
    left_hbm,
    right_hbm,
    out_hbm,
    q_ref,
    input_grad_hbm,
    chunks_ref,
    q4_ref,
    basis_ref,
    cot_ref,
    acts_ref,
    error_ref,
    out_ref,
    sums_ref,
    input_grad_ref,
    sems,
):
    parts, step = error_ref.shape[:2]
    copies = Copies(sems)
    chunks_copy = copies.start(chunks_hbm, chunks_ref)
    cot_copy = copies.start(cot_hbm, cot_ref)
    waits = []
    for i in range(parts):
        at = slice(i * step, (i + 1) * step)
        waits.append(
            (
                copies.start(acts_hbm.at[:, at], acts_ref.at[i]),
                copies.start(error_hbm.at[at, :], error_ref.at[i]),
                copies.start(basis_hbm.at[at, :], basis_ref.at[i]),
            )
        )
    n = input_grad_ref.shape[0]
    own = slice(2 * n, 3 * n)
    sums = [
        copies.start(src, sums_ref.at[i])
        for i, src in enumerate((keep_hbm.at[own, :], got_hbm.at[own, :], left_hbm, right_hbm))
    ]
    chunks_copy.wait()
    cot_copy.wait()
    for copy in waits[0]:
        copy.wait()
    tiles = q_ref.shape[1] // LANES
    for g in range(8):
        for j in range(tiles):
            v = g * tiles + j
            q_ref[8 * g : 8 * g + 8, LANES * j : LANES * (j + 1)] = chunks_ref[v // 4, 8 * (v % 4) : 8 * (v % 4) + 8]
    q = -q_ref[...]
    high = q.astype(BF16)
    low = (q - high.astype(F32)).astype(BF16)
    q4 = jnp.concatenate([high, high, low, low], axis=0)
    q4_ref[...] = q4
    stores = []
    for i in range(parts):
        if i:
            for copy in waits[i]:
                copy.wait()
        merged = dot(acts_ref[i], cot_ref[...], TN) + error_ref[i].astype(F32)
        out_ref[i] = (merged + dot(basis_ref[i], q4_ref[...] if i else q4)).astype(BF16)
        stores.append(copies.start(out_ref.at[i], out_hbm.at[i * step : (i + 1) * step, :]))
        if i == parts - 2:
            for copy in sums:
                copy.wait()
            total = (sums_ref[0] + sums_ref[1]) + (sums_ref[2] + sums_ref[3])
            input_grad_ref[...] = total.astype(BF16)
            stores.append(copies.start(input_grad_ref, input_grad_hbm))
    for store in stores:
        store.wait()


def final(chunks, basis4, cot, acts, error, keep, got, from_left, from_right, parts=8):
    tokens, d = acts.shape
    ff = cot.shape[1]
    step = d // parts
    return call(
        final_kernel,
        (chunks, basis4, cot, acts, error, keep, got, from_left, from_right),
        [HBM] * 9,
        [shape((d, ff), BF16), shape((RANK, ff)), shape(from_left.shape, BF16)],
        [HBM, VMEM, HBM],
        [
            (chunks.shape, F32),
            ((4 * RANK, ff), BF16),
            ((parts, step, 4 * RANK), BF16),
            ((tokens, ff), BF16),
            ((parts, tokens, step), BF16),
            ((parts, step, ff), BF16),
            ((parts, step, ff), BF16),
            ((4,) + from_left.shape, F32),
            (from_left.shape, BF16),
        ],
        7 + 4 * parts,
        limit=52 << 20,
    )


def partial_kernel(
    cot_hbm,
    weight_hbm,
    far_send_hbm,
    near_send_hbm,
    far_keep_hbm,
    near_keep_hbm,
    cot_ref,
    weight_ref,
    out_ref,
    sems,
):
    parts, step = weight_ref.shape[:2]
    core = my_core()
    x = lax.div(lax.axis_index("tensor"), 2)
    n = cot_ref.shape[0] // 8
    copies = Copies(sems)
    waits = []
    for side, h in enumerate((1 - core, core)):
        for k, hop in enumerate((2, 1, 3, 0)):
            at = pl.multiple_of((lax.rem(x + hop, 4) * 2 + h) * n, n)
            to = (side * 4 + k) * n
            waits.append(copies.start(cot_hbm.at[pl.ds(at, n), :], cot_ref.at[to : to + n, :]))
    weight_copies = [
        copies.start(weight_hbm.at[i * step : (i + 1) * step, :], weight_ref.at[i]) for i in range(parts)
    ]
    for copy in waits:
        copy.wait()
    stores = []
    targets = ((far_send_hbm, 0, n), (near_send_hbm, n, 4 * n), (far_keep_hbm, 4 * n, 5 * n), (near_keep_hbm, 5 * n, 8 * n))
    for i in range(parts):
        weight_copies[i].wait()
        out_ref[i] = dot(cot_ref[...], weight_ref[i], NT)
        for hbm, lo, hi in targets:
            stores.append(copies.start(out_ref.at[i, lo:hi, :], hbm.at[:, i * step : (i + 1) * step]))
    for store in stores:
        store.wait()


def partials(cot, weight, parts=4):
    tokens, ff = cot.shape
    d = weight.shape[0]
    n = tokens // 8
    step = d // parts
    return call(
        partial_kernel,
        (cot, weight),
        [HBM, HBM],
        [shape((r, d)) for r in (n, 3 * n, n, 3 * n)],
        [HBM] * 4,
        [((tokens, ff), BF16), ((parts, step, ff), BF16), ((parts, tokens, step), F32)],
        8 + 5 * parts,
    )


def far_kernel(keep_hbm, got_hbm, low_hbm, high_hbm, keep_ref, got_ref, sems):
    copies = Copies(sems)
    d = keep_ref.shape[1]
    wide = low_hbm.shape[1]
    halves = (slice(0, d // 2), slice(d // 2, d))
    loads = [
        (copies.start(keep_hbm.at[:, at], keep_ref.at[:, at]), copies.start(got_hbm.at[:, at], got_ref.at[:, at]))
        for at in halves
    ]
    for at, pair in zip(halves, loads):
        for copy in pair:
            copy.wait()
        keep_ref[:, at] += got_ref[:, at]
    stores = [copies.start(keep_ref.at[:, :wide], low_hbm), copies.start(keep_ref.at[:, d - wide :], high_hbm)]
    for store in stores:
        store.wait()


def far_sums(keep, got):
    n, d = keep.shape
    return call(
        far_kernel,
        (keep, got),
        [HBM] * 2,
        [shape((n, d // 2 + LANES))] * 2,
        [HBM] * 2,
        [((n, d), F32)] * 2,
        6,
    )


def near_kernel(keep_hbm, got_hbm, plus_hbm, minus_hbm, keep_ref, got_ref, sems):
    copies = Copies(sems)
    n = plus_hbm.shape[0]
    rows = (slice(0, n), slice(n, 2 * n))
    loads = [
        (copies.start(keep_hbm.at[at, :], keep_ref.at[at, :]), copies.start(got_hbm.at[at, :], got_ref.at[at, :]))
        for at in rows
    ]
    stores = []
    for at, pair, out in zip(rows, loads, (plus_hbm, minus_hbm)):
        for copy in pair:
            copy.wait()
        keep_ref[at, :] += got_ref[at, :]
        stores.append(copies.start(keep_ref.at[at, :], out))
    for store in stores:
        store.wait()


def near_sums(keep, got, n):
    d = keep.shape[1]
    return call(
        near_kernel,
        (keep, got),
        [HBM] * 2,
        [shape((n, d))] * 2,
        [HBM] * 2,
        [((2 * n, d), F32)] * 2,
        6,
    )


def body(acts, up_cot, up_weight, error_buf, q_init):
    n_dp = lax.axis_size("dp")
    n_tensor = lax.axis_size("tensor")
    both = ("dp", "tensor")
    pairs = [(i, i ^ 1) for i in range(n_tensor)]
    right_ring = [(i, (i + 2) % n_tensor) for i in range(n_tensor)]
    left_ring = [(i, (i - 2) % n_tensor) for i in range(n_tensor)]
    error = error_buf[0]

    send, *held = left_send(q_init, up_cot, acts, error)
    received = lax.ppermute(send, "tensor", pairs)
    total = left_keep(held, send.shape) + received
    chunks = lax.all_to_all(total, both, 0, 0)

    up_weight, _ = lax.optimization_barrier((up_weight, total))
    far_send, near_send, far_keep, near_keep = partials(up_cot, up_weight)
    chunks, far_send, near_send = lax.optimization_barrier((chunks, far_send, near_send))

    spread_left = spread(chunks, 1.0, kinds=2)
    mine = lax.all_to_all(spread_left, both, 0, 0)
    far_send, near_send, _ = lax.optimization_barrier((far_send, near_send, spread_left))
    far_got = lax.ppermute(far_send, "tensor", pairs)
    near_got = lax.ppermute(near_send, "tensor", pairs)
    far_low, far_high = far_sums(far_keep, far_got)
    low_relay = lax.ppermute(far_low, "tensor", right_ring)
    high_relay = lax.ppermute(far_high, "tensor", left_ring)
    plus, minus = near_sums(near_keep, near_got, far_keep.shape[0])
    mine, _, plus = lax.optimization_barrier((mine, far_low, plus))

    other = lax.ppermute(mine, "tensor", pairs)
    terms = first(mine, up_cot, acts, error)
    factor, right, plus, minus = second(other, terms, low_relay, high_relay, plus, minus)
    from_left = lax.ppermute(plus, "tensor", right_ring)
    from_right = lax.ppermute(minus, "tensor", left_ring)
    right_parts = lax.all_to_all(right, "dp", 0, 0)
    basis, basis4 = prep(factor, mine, other)
    right_parts, basis4 = lax.optimization_barrier((right_parts, basis4))

    q_chunks = lax.all_to_all(spread(right_parts, 1.0 / n_dp), "dp", 0, 0)
    new_error, q_factor, input_grad = final(
        q_chunks, basis4, up_cot, acts, error, near_keep, near_got, from_left, from_right
    )
    return (input_grad, new_error[None], basis, q_factor)


def solution(mesh):
    return jax.shard_map(
        body,
        mesh=mesh,
        in_specs=(
            P("dp", None),
            P("dp", "tensor"),
            P(None, "tensor"),
            P("dp", None, "tensor"),
            P(None, "tensor"),
        ),
        out_specs=(P(("dp", "tensor"), None), P("dp", None, "tensor"), P(), P(None, "tensor")),
        check_vma=False,
    )
```

```python
import jax
import jax.numpy as jnp
from jax import lax
from jax.experimental import pallas as pl
from jax.experimental.pallas import tpu as pltpu
from jax.sharding import PartitionSpec as P

F32 = jnp.float32
BF16 = jnp.bfloat16
HIGHEST = lax.Precision.HIGHEST
RANK = 64
LANES = 128
VMEM = pl.BlockSpec(memory_space=pltpu.VMEM)
HBM = pl.BlockSpec(memory_space=pltpu.HBM)
NN = (((1,), (0,)), ((), ()))
NT = (((1,), (1,)), ((), ()))
TN = (((0,), (0,)), ((), ()))


def shape(dims, dtype=F32):
    return jax.ShapeDtypeStruct(dims, dtype)


def call(kernel, args, specs, outs, out_specs, scratch, n_sems, limit=56 << 20):
    return pl.pallas_call(
        kernel,
        in_specs=specs,
        out_specs=out_specs,
        out_shape=outs,
        scratch_shapes=[pltpu.VMEM(dims, dtype) for dims, dtype in scratch] + [pltpu.SemaphoreType.DMA((n_sems,))],
        compiler_params=pltpu.CompilerParams(vmem_limit_bytes=limit),
        cost_estimate=pl.CostEstimate(flops=10**6, bytes_accessed=10**5, transcendentals=0),
    )(*args)


class Copies:
    def __init__(self, sems):
        self.sems = sems
        self.all = []

    def start(self, src, dst):
        copy = pltpu.make_async_copy(src, dst, self.sems.at[len(self.all)])
        copy.start()
        self.all.append(copy)
        return copy


def split3(x):
    high = x.astype(BF16)
    rest = x - high.astype(F32)
    mid = rest.astype(BF16)
    low = (rest - mid.astype(F32)).astype(BF16)
    return jnp.concatenate([high, mid, low], axis=0)


def sum3(y):
    return (y[2 * RANK : 3 * RANK] + y[RANK : 2 * RANK]) + y[:RANK]


def dot(a, b, dims=NN):
    return lax.dot_general(a, b, dims, preferred_element_type=F32)


def dot_highest(a, b):
    return lax.dot_general(a, b, NN, precision=HIGHEST, preferred_element_type=F32)


def my_core():
    return lax.rem(lax.axis_index("tensor"), 2)


def part_of(place, width, i, parts):
    step = width // parts
    return pl.ds(pl.multiple_of(place * width + i * step, step), step)


PARTS = 2


def left_part(q3t, p3, error, acts):
    y = dot(error, q3t)
    by_error = (y[:, 2 * RANK :] + y[:, RANK : 2 * RANK]) + y[:, :RANK]
    return by_error.T + sum3(dot(p3, acts))


def store_left(out_ref, i, left):
    tiles = left.shape[1] // LANES
    for j in range(tiles):
        for g in range(8):
            out_ref[8 * (i * tiles + j) + g] = left[8 * g : 8 * g + 8, LANES * j : LANES * (j + 1)]


def half_shapes(tokens, d, ff, parts):
    step = d // 2 // parts
    return [(parts, step, ff), (parts, tokens, step)]


def fetch_half(copies, place, error_hbm, acts_hbm, error_ref, acts_ref):
    width = error_hbm.shape[0] // 2
    parts = error_ref.shape[0]
    started = []
    for i in range(parts):
        at = part_of(place, width, i, parts)
        started.append(
            (copies.start(error_hbm.at[at, :], error_ref.at[i]), copies.start(acts_hbm.at[:, at], acts_ref.at[i]))
        )
    return started


def left_send_kernel(
    q_hbm,
    cot_hbm,
    acts_hbm,
    error_hbm,
    out_ref,
    q3t_ref,
    p3_ref,
    error_keep_ref,
    acts_keep_ref,
    q_ref,
    cot_ref,
    error_ref,
    acts_ref,
    sems,
):
    core = my_core()
    copies = Copies(sems)
    q_copy = copies.start(q_hbm, q_ref)
    cot_copy = copies.start(cot_hbm, cot_ref)
    now = fetch_half(copies, 1 - core, error_hbm, acts_hbm, error_ref, acts_ref)
    later = fetch_half(copies, core, error_hbm, acts_hbm, error_keep_ref, acts_keep_ref)
    q_copy.wait()
    q3 = split3(q_ref[...])
    q3t = q3.T
    q3t_ref[...] = q3t
    cot_copy.wait()
    p3 = split3(sum3(dot(q3, cot_ref[...], NT)))
    p3_ref[...] = p3
    for i, pair in enumerate(now):
        for copy in pair:
            copy.wait()
        store_left(out_ref, i, left_part(q3t, p3, error_ref[i], acts_ref[i]))
    for pair in later:
        for copy in pair:
            copy.wait()


def left_send(q, cot, acts, error):
    tokens, d = acts.shape
    ff = cot.shape[1]
    halves = half_shapes(tokens, d, ff, PARTS)
    return call(
        left_send_kernel,
        (q, cot, acts, error),
        [HBM] * 4,
        [shape((d // 32, 8, LANES)), shape((ff, 3 * RANK), BF16), shape((3 * RANK, tokens), BF16)]
        + [shape(s, BF16) for s in halves],
        [VMEM] * 5,
        [((RANK, ff), F32), ((tokens, ff), BF16)] + [(s, BF16) for s in halves],
        2 + 4 * PARTS,
        limit=44 << 20,
    )


def left_keep_kernel(q3t_ref, p3_ref, error_ref, acts_ref, out_ref):
    for i in range(error_ref.shape[0]):
        store_left(out_ref, i, left_part(q3t_ref[...], p3_ref[...], error_ref[i], acts_ref[i]))


def left_keep(held, dims):
    return pl.pallas_call(
        left_keep_kernel,
        in_specs=[VMEM] * 4,
        out_specs=VMEM,
        out_shape=shape(dims),
        compiler_params=pltpu.CompilerParams(vmem_limit_bytes=10 << 20),
        cost_estimate=pl.CostEstimate(flops=10**6, bytes_accessed=10**5, transcendentals=0),
    )(*held)


def spread_kernel(scale, kinds, in_ref, out_ref):
    n = in_ref.shape[0]
    for kind in range(kinds):
        total = in_ref[kind]
        for i in range(kind + kinds, n, kinds):
            total = total + in_ref[i]
        if scale != 1.0:
            total = total * scale
        for i in range(kind, n, kinds):
            out_ref[i] = total


def spread(x, scale, kinds=1):
    return pl.pallas_call(
        lambda i, o: spread_kernel(scale, kinds, i, o),
        in_specs=[VMEM],
        out_specs=VMEM,
        out_shape=shape(x.shape),
        compiler_params=pltpu.CompilerParams(vmem_limit_bytes=8 << 20),
        cost_estimate=pl.CostEstimate(flops=10**6, bytes_accessed=10**5, transcendentals=0),
    )(x)


def inverse_factor(gram):
    groups = RANK // 8
    a = [gram[8 * i : 8 * i + 8] for i in range(groups)]
    row = lax.broadcasted_iota(jnp.int32, (8, RANK), 0)
    col = lax.broadcasted_iota(jnp.int32, (8, RANK), 1)
    b = [jnp.where(row + 8 * i == col, 1.0, 0.0).astype(F32) for i in range(groups)]
    scale = []
    for k in range(groups):
        cols = [
            [jnp.broadcast_to(a[i][:, 8 * k + j : 8 * k + j + 1], (8, RANK)) if i >= k else None for i in range(groups)]
            for j in range(8)
        ]
        block_scale = jnp.zeros((8, RANK), F32)
        for j in range(8):
            pivot = jnp.broadcast_to(cols[j][k][j : j + 1], (8, RANK))
            inverse = 1.0 / pivot
            block_scale = jnp.where(row == j, lax.rsqrt(pivot), block_scale)
            row_a = jnp.broadcast_to(a[k][j : j + 1], (8, RANK))
            row_b = jnp.broadcast_to(b[k][j : j + 1], (8, RANK))
            entries = [jnp.broadcast_to(cols[m][k][j : j + 1], (8, RANK)) for m in range(j + 1, 8)]
            for i in range(k, groups):
                factor = cols[j][i] * inverse
                if i == k:
                    factor = jnp.where(row > j, factor, 0.0)
                a[i] = a[i] - factor * row_a
                b[i] = b[i] - factor * row_b
                for m in range(j + 1, 8):
                    cols[m][i] = cols[m][i] - factor * entries[m - j - 1]
        scale.append(block_scale)
    return jnp.concatenate([b[i] * scale[i] for i in range(groups)], axis=0)


def half_of(tiles_ref):
    n = tiles_ref.shape[0] // 8
    return jnp.concatenate(
        [jnp.concatenate([tiles_ref[8 * j + g] for j in range(n)], axis=1) for g in range(8)], axis=0
    )


def half_terms(left, error_ref, acts_ref, ready=None):
    parts, step = error_ref.shape[:2]
    left3 = split3(left)
    gram = [sum3(dot(left3, left3[RANK * i : RANK * (i + 1)], NT)) for i in range(3)]
    with_error = with_acts = None
    for i in range(parts):
        part = left3[:, i * step : (i + 1) * step]
        if ready is not None:
            for copy in ready[i]:
                copy.wait()
        e = dot(part, error_ref[i])
        a = dot(part, acts_ref[i], NT)
        with_error = e if i == 0 else with_error + e
        with_acts = a if i == 0 else with_acts + a
    return (gram[2] + gram[1]) + gram[0], sum3(with_error), sum3(with_acts)


def first_kernel(
    mine_hbm,
    cot_hbm,
    acts_hbm,
    error_hbm,
    gram_ref,
    with_error_ref,
    with_acts_ref,
    cot_ref,
    error_other_ref,
    acts_other_ref,
    mine_ref,
    error_ref,
    acts_ref,
    sems,
):
    core = my_core()
    copies = Copies(sems)
    mine_copy = copies.start(mine_hbm, mine_ref)
    now = fetch_half(copies, core, error_hbm, acts_hbm, error_ref, acts_ref)
    later = fetch_half(copies, 1 - core, error_hbm, acts_hbm, error_other_ref, acts_other_ref)
    cot_copy = copies.start(cot_hbm, cot_ref)
    mine_copy.wait()
    gram, with_error, with_acts = half_terms(half_of(mine_ref), error_ref, acts_ref, now)
    gram_ref[...] = gram
    with_error_ref[...] = with_error
    with_acts_ref[...] = with_acts
    for pair in later:
        for copy in pair:
            copy.wait()
    cot_copy.wait()


def first(mine, cot, acts, error, parts=1):
    tokens, d = acts.shape
    ff = cot.shape[1]
    halves = half_shapes(tokens, d, ff, parts)
    return call(
        first_kernel,
        (mine, cot, acts, error),
        [HBM] * 4,
        [shape((RANK, RANK)), shape((RANK, ff)), shape((RANK, tokens)), shape((tokens, ff), BF16)]
        + [shape(s, BF16) for s in halves],
        [VMEM] * 6,
        [(mine.shape, F32)] + [(s, BF16) for s in halves],
        2 + 4 * parts,
        limit=44 << 20,
    )


def second_kernel(
    other_ref, gram_ref, with_error_ref, with_acts_ref, cot_ref, error_ref, acts_ref, factor_ref, right_ref
):
    gram, with_error, with_acts = half_terms(half_of(other_ref), error_ref, acts_ref)
    factor = inverse_factor(gram + gram_ref[...])
    factor_ref[...] = factor
    with_acts = with_acts + with_acts_ref[...]
    merged_term = (with_error + with_error_ref[...]) + sum3(dot(split3(with_acts), cot_ref[...]))
    right = dot_highest(factor, merged_term)
    tiles = right.shape[1] // LANES
    for g in range(8):
        for j in range(tiles):
            v = g * tiles + j
            right_ref[v // 4, 8 * (v % 4) : 8 * (v % 4) + 8] = right[8 * g : 8 * g + 8, LANES * j : LANES * (j + 1)]
    for v in range(8 * tiles, 64):
        right_ref[v // 4, 8 * (v % 4) : 8 * (v % 4) + 8] = jnp.zeros((8, LANES), F32)


def second(other, terms):
    return pl.pallas_call(
        second_kernel,
        in_specs=[VMEM] * 7,
        out_specs=[VMEM, VMEM],
        out_shape=[shape((RANK, RANK)), shape((16, 32, LANES))],
        compiler_params=pltpu.CompilerParams(vmem_limit_bytes=12 << 20),
        cost_estimate=pl.CostEstimate(flops=10**6, bytes_accessed=10**5, transcendentals=0),
    )(other, *terms)


def prep_kernel(factor_ref, mine_ref, other_ref, basis_ref, out_ref):
    core = my_core()
    width = mine_ref.shape[0] // 8 * LANES
    for ref, place in ((mine_ref, core), (other_ref, 1 - core)):
        at = pl.ds(pl.multiple_of(place * width, width), width)
        x = dot_highest(factor_ref[...], half_of(ref))
        basis_ref[:, at] = x
        high = x.astype(BF16)
        low = (x - high.astype(F32)).astype(BF16)
        both = jnp.concatenate([high, low], axis=0).T
        out_ref[at, : 2 * RANK] = both
        out_ref[at, 2 * RANK :] = both


def prep(factor, mine, other):
    d = 2 * (mine.shape[0] // 8 * LANES)
    return pl.pallas_call(
        prep_kernel,
        in_specs=[VMEM] * 3,
        out_specs=[VMEM, VMEM],
        out_shape=[shape((RANK, d)), shape((d, 4 * RANK), BF16)],
        compiler_params=pltpu.CompilerParams(vmem_limit_bytes=12 << 20),
        cost_estimate=pl.CostEstimate(flops=10**6, bytes_accessed=10**5, transcendentals=0),
    )(factor, mine, other)


def final_kernel(
    chunks_hbm,
    basis_hbm,
    cot_hbm,
    acts_hbm,
    error_hbm,
    keep_hbm,
    got_hbm,
    left_hbm,
    right_hbm,
    out_hbm,
    q_ref,
    input_grad_hbm,
    chunks_ref,
    q4_ref,
    basis_ref,
    cot_ref,
    acts_ref,
    error_ref,
    out_ref,
    sums_ref,
    input_grad_ref,
    sems,
):
    parts, step = error_ref.shape[:2]
    copies = Copies(sems)
    chunks_copy = copies.start(chunks_hbm, chunks_ref)
    cot_copy = copies.start(cot_hbm, cot_ref)
    waits = []
    for i in range(parts):
        at = slice(i * step, (i + 1) * step)
        waits.append(
            (
                copies.start(acts_hbm.at[:, at], acts_ref.at[i]),
                copies.start(error_hbm.at[at, :], error_ref.at[i]),
                copies.start(basis_hbm.at[at, :], basis_ref.at[i]),
            )
        )
    n = input_grad_ref.shape[0]
    own = slice(3 * n, 4 * n)
    sums = [
        copies.start(src, sums_ref.at[i])
        for i, src in enumerate((keep_hbm.at[own, :], got_hbm.at[own, :], left_hbm, right_hbm))
    ]
    chunks_copy.wait()
    cot_copy.wait()
    for copy in waits[0]:
        copy.wait()
    tiles = q_ref.shape[1] // LANES
    for g in range(8):
        for j in range(tiles):
            v = g * tiles + j
            q_ref[8 * g : 8 * g + 8, LANES * j : LANES * (j + 1)] = chunks_ref[v // 4, 8 * (v % 4) : 8 * (v % 4) + 8]
    q = -q_ref[...]
    high = q.astype(BF16)
    low = (q - high.astype(F32)).astype(BF16)
    q4 = jnp.concatenate([high, high, low, low], axis=0)
    q4_ref[...] = q4
    stores = []
    for i in range(parts):
        if i:
            for copy in waits[i]:
                copy.wait()
        merged = dot(acts_ref[i], cot_ref[...], TN) + error_ref[i].astype(F32)
        out_ref[i] = (merged + dot(basis_ref[i], q4_ref[...] if i else q4)).astype(BF16)
        stores.append(copies.start(out_ref.at[i], out_hbm.at[i * step : (i + 1) * step, :]))
        if i == parts - 2:
            for copy in sums:
                copy.wait()
            total = (sums_ref[0] + sums_ref[1]) + (sums_ref[2] + sums_ref[3])
            input_grad_ref[...] = total.astype(BF16)
            stores.append(copies.start(input_grad_ref, input_grad_hbm))
    for store in stores:
        store.wait()


def final(chunks, basis4, cot, acts, error, keep, got, from_left, from_right, parts=8):
    tokens, d = acts.shape
    ff = cot.shape[1]
    step = d // parts
    return call(
        final_kernel,
        (chunks, basis4, cot, acts, error, keep, got, from_left, from_right),
        [HBM] * 9,
        [shape((d, ff), BF16), shape((RANK, ff)), shape(from_left.shape, BF16)],
        [HBM, VMEM, HBM],
        [
            (chunks.shape, F32),
            ((4 * RANK, ff), BF16),
            ((parts, step, 4 * RANK), BF16),
            ((tokens, ff), BF16),
            ((parts, tokens, step), BF16),
            ((parts, step, ff), BF16),
            ((parts, step, ff), BF16),
            ((4,) + from_left.shape, F32),
            (from_left.shape, BF16),
        ],
        7 + 4 * parts,
        limit=52 << 20,
    )


def partial_kernel(
    cot_hbm,
    weight_hbm,
    send_hbm,
    keep_hbm,
    cot_ref,
    weight_ref,
    out_ref,
    sems,
):
    parts, step = weight_ref.shape[:2]
    core = my_core()
    x = lax.div(lax.axis_index("tensor"), 2)
    n = cot_ref.shape[0] // 8
    copies = Copies(sems)
    waits = []
    for side, h in enumerate((1 - core, core)):
        for k, hop in enumerate((2, 1, 3, 0)):
            at = pl.multiple_of((lax.rem(x + hop, 4) * 2 + h) * n, n)
            to = (side * 4 + k) * n
            waits.append(copies.start(cot_hbm.at[pl.ds(at, n), :], cot_ref.at[to : to + n, :]))
    weight_copies = [
        copies.start(weight_hbm.at[i * step : (i + 1) * step, :], weight_ref.at[i]) for i in range(parts)
    ]
    for copy in waits:
        copy.wait()
    stores = []
    targets = ((send_hbm, 0, 4 * n), (keep_hbm, 4 * n, 8 * n))
    for i in range(parts):
        weight_copies[i].wait()
        out_ref[i] = dot(cot_ref[...], weight_ref[i], NT)
        for hbm, lo, hi in targets:
            stores.append(copies.start(out_ref.at[i, lo:hi, :], hbm.at[:, i * step : (i + 1) * step]))
    for store in stores:
        store.wait()


def partials(cot, weight, parts=4):
    tokens, ff = cot.shape
    d = weight.shape[0]
    n = tokens // 8
    step = d // parts
    return call(
        partial_kernel,
        (cot, weight),
        [HBM, HBM],
        [shape((4 * n, d))] * 2,
        [HBM] * 2,
        [((tokens, ff), BF16), ((parts, step, ff), BF16), ((parts, tokens, step), F32)],
        8 + 3 * parts,
    )


def far_kernel(keep_hbm, got_hbm, low_hbm, high_hbm, keep_ref, got_ref, sems):
    copies = Copies(sems)
    n, d = keep_ref.shape
    wide = low_hbm.shape[1]
    halves = (slice(0, d // 2), slice(d // 2, d))
    loads = [
        (copies.start(keep_hbm.at[:n, at], keep_ref.at[:, at]), copies.start(got_hbm.at[:n, at], got_ref.at[:, at]))
        for at in halves
    ]
    for at, pair in zip(halves, loads):
        for copy in pair:
            copy.wait()
        keep_ref[:, at] += got_ref[:, at]
    stores = [copies.start(keep_ref.at[:, :wide], low_hbm), copies.start(keep_ref.at[:, d - wide :], high_hbm)]
    for store in stores:
        store.wait()


def far_sums(keep, got):
    n, d = keep.shape[0] // 4, keep.shape[1]
    return call(
        far_kernel,
        (keep, got),
        [HBM] * 2,
        [shape((n, d // 2 + LANES))] * 2,
        [HBM] * 2,
        [((n, d), F32)] * 2,
        6,
    )


def near_kernel(keep_hbm, got_hbm, plus_hbm, minus_hbm, keep_ref, got_ref, sems):
    copies = Copies(sems)
    n = plus_hbm.shape[0]
    rows = (slice(0, n), slice(n, 2 * n))
    loads = [
        (copies.start(keep_hbm.at[src, :], keep_ref.at[at, :]), copies.start(got_hbm.at[src, :], got_ref.at[at, :]))
        for at, src in zip(rows, (slice(n, 2 * n), slice(2 * n, 3 * n)))
    ]
    stores = []
    for at, pair, out in zip(rows, loads, (plus_hbm, minus_hbm)):
        for copy in pair:
            copy.wait()
        keep_ref[at, :] += got_ref[at, :]
        stores.append(copies.start(keep_ref.at[at, :], out))
    for store in stores:
        store.wait()


def near_sums(keep, got):
    n, d = keep.shape[0] // 4, keep.shape[1]
    return call(
        near_kernel,
        (keep, got),
        [HBM] * 2,
        [shape((n, d))] * 2,
        [HBM] * 2,
        [((2 * n, d), F32)] * 2,
        6,
    )


def relay_kernel(plus_hbm, minus_hbm, low_ref, high_ref, plus_out, minus_out, half_ref, sems):
    copies = Copies(sems)
    d = plus_hbm.shape[1]
    w = d // 2
    wide = low_ref.shape[1]
    parts = (
        (plus_hbm, plus_out, low_ref, slice(0, w), slice(0, w)),
        (minus_hbm, minus_out, high_ref, slice(w, d), slice(wide - w, wide)),
    )
    loads = [copies.start(src.at[:, at], half_ref.at[i]) for i, (src, _, _, at, _) in enumerate(parts)]
    stores = []
    for i, (_, out, relay, at, far) in enumerate(parts):
        loads[i].wait()
        half_ref[i] += relay[:, far]
        stores.append(copies.start(half_ref.at[i], out.at[:, at]))
    for store in stores:
        store.wait()


def relay_sums(plus, minus, low, high):
    n, d = plus.shape
    return pl.pallas_call(
        relay_kernel,
        in_specs=[HBM] * 2 + [VMEM] * 2,
        out_specs=[HBM] * 2,
        out_shape=[shape((n, d))] * 2,
        input_output_aliases={0: 0, 1: 1},
        scratch_shapes=[
            pltpu.VMEM((2, n, d // 2), F32),
            pltpu.SemaphoreType.DMA((4,)),
        ],
        compiler_params=pltpu.CompilerParams(vmem_limit_bytes=52 << 20),
        cost_estimate=pl.CostEstimate(flops=10**6, bytes_accessed=10**5, transcendentals=0),
    )(plus, minus, low, high)


def body(acts, up_cot, up_weight, error_buf, q_init):
    n_dp = lax.axis_size("dp")
    n_tensor = lax.axis_size("tensor")
    both = ("dp", "tensor")
    pairs = [(i, i ^ 1) for i in range(n_tensor)]
    right_ring = [(i, (i + 2) % n_tensor) for i in range(n_tensor)]
    left_ring = [(i, (i - 2) % n_tensor) for i in range(n_tensor)]
    error = error_buf[0]

    send, *held = left_send(q_init, up_cot, acts, error)
    received = lax.ppermute(send, "tensor", pairs)
    total = left_keep(held, send.shape) + received
    chunks = lax.all_to_all(total, both, 0, 0)

    up_weight, _ = lax.optimization_barrier((up_weight, total))
    grad_send, grad_keep = partials(up_cot, up_weight)
    chunks, grad_send = lax.optimization_barrier((chunks, grad_send))

    spread_left = spread(chunks, 1.0, kinds=2)
    mine = lax.all_to_all(spread_left, both, 0, 0)
    grad_send, _ = lax.optimization_barrier((grad_send, spread_left))
    grad_got = lax.ppermute(grad_send, "tensor", pairs)
    far_low, far_high = far_sums(grad_keep, grad_got)
    low_relay = lax.ppermute(far_low, "tensor", right_ring)
    high_relay = lax.ppermute(far_high, "tensor", left_ring)
    plus, minus = near_sums(grad_keep, grad_got)
    mine, _, plus = lax.optimization_barrier((mine, far_low, plus))

    other = lax.ppermute(mine, "tensor", pairs)
    terms = first(mine, up_cot, acts, error)
    factor, right = second(other, terms)

    low_relay, high_relay, right = lax.optimization_barrier((low_relay, high_relay, right))
    plus, minus = relay_sums(plus, minus, low_relay, high_relay)
    from_left = lax.ppermute(plus, "tensor", right_ring)
    from_right = lax.ppermute(minus, "tensor", left_ring)
    right_parts = lax.all_to_all(right, "dp", 0, 0)
    basis, basis4 = prep(factor, mine, other)
    right_parts, basis4 = lax.optimization_barrier((right_parts, basis4))

    q_chunks = lax.all_to_all(spread(right_parts, 1.0 / n_dp), "dp", 0, 0)
    new_error, q_factor, input_grad = final(
        q_chunks, basis4, up_cot, acts, error, grad_keep, grad_got, from_left, from_right
    )
    return (input_grad, new_error[None], basis, q_factor)


def solution(mesh):
    return jax.shard_map(
        body,
        mesh=mesh,
        in_specs=(
            P("dp", None),
            P("dp", "tensor"),
            P(None, "tensor"),
            P("dp", None, "tensor"),
            P(None, "tensor"),
        ),
        out_specs=(P(("dp", "tensor"), None), P("dp", None, "tensor"), P(), P(None, "tensor")),
        check_vma=False,
    )
```
